32 devices in a mesh: ta: 2 (over x), gx: 16 (over z, y, core).
Axes of the slice: x: 2, y: 2, z: 4, core: 2. Of those that a mesh axis runs over, the one named last changes fastest.
Arguments:
- gauge_links: float32 [3, 2, 3, 3, 32, 9216], P(None, None, None, None, ('ta', 'gx')), parts along dimension 4, may hold values from -1 to 1, as said below
Outputs:
- fixed_links: float32 [3, 2, 3, 3, 32, 9216], P(None, None, None, None, ('ta', 'gx')), parts along dimension 4
- drift_values: float32 [2], P('ta'), parts along dimension 0
The draws below stay inside these ranges and needn't reach their ends.
There are 2 independent parts, one for each index of `ta`. The reference program is written for one: setup_inputs(seed, part) draws one part's arguments, and reference() takes and returns one part's arrays. A program takes and returns all parts, laid end to end along the dimension named above; each array names one. Nothing has to cross between parts.
Inputs may be any that keep to these rules, and one draw needn't show every extreme that they name: `gauge_links`: for every direction and site the complex matrix is unitary.
All inputs are finite; a program needn't handle non-finite values.
Results may differ from the reference program's by a relative error of at most 0.0003.
Values sent between devices are 32-bit elements; how exact they have to be, the bound alone decides.
No kernel may reach another device: no remote copies, remote signals or barrier semaphores. Data moves between devices by JAX's collectives and lax.ppermute only.
A program may use at most 128 MiB of HBM per device.

```python
import math
import jax
import jax.numpy as jnp

SIDE = 96
ITERS = 1
NX = 16


def matrix_mul_drawn(left, right):
    return jnp.sum(left[:, :, None] * right[None, :, :], axis=1)


def complex_mul_drawn(left, right):
    real_part = matrix_mul_drawn(left[0], right[0]) - matrix_mul_drawn(left[1], right[1])
    imag_part = matrix_mul_drawn(left[0], right[1]) + matrix_mul_drawn(left[1], right[0])
    return (real_part, imag_part)


def scalar_mul_drawn(left, right):
    return (left[0] * right[0] - left[1] * right[1], left[0] * right[1] + left[1] * right[0])


def inverse_three_drawn(real_part, imag_part):

    def entry(i, j):
        return (real_part[i % 3, j % 3], imag_part[i % 3, j % 3])
    cofactor = []
    for i in range(3):
        row_list = []
        for j in range(3):
            first = scalar_mul_drawn(entry(i + 1, j + 1), entry(i + 2, j + 2))
            second = scalar_mul_drawn(entry(i + 1, j + 2), entry(i + 2, j + 1))
            row_list.append((first[0] - second[0], first[1] - second[1]))
        cofactor.append(row_list)
    det_real = 0.0
    det_imag = 0.0
    for j in range(3):
        term = scalar_mul_drawn(entry(0, j), cofactor[0][j])
        det_real = det_real + term[0]
        det_imag = det_imag + term[1]
    denom = det_real * det_real + det_imag * det_imag
    recip = (det_real / denom, -det_imag / denom)
    rows_real = []
    rows_imag = []
    for i in range(3):
        line_real = []
        line_imag = []
        for j in range(3):
            value = scalar_mul_drawn(cofactor[j][i], recip)
            line_real.append(value[0])
            line_imag.append(value[1])
        rows_real.append(jnp.stack(line_real))
        rows_imag.append(jnp.stack(line_imag))
    return (jnp.stack(rows_real), jnp.stack(rows_imag))


def make_unitary(fields):
    empty_part = jnp.zeros_like(fields[0])
    rows_real = [[empty_part, fields[2], fields[4]], [-fields[2], empty_part, fields[6]], [-fields[4], -fields[6], empty_part]]
    rows_imag = [[fields[0], fields[3], fields[5]], [fields[3], fields[1], fields[7]], [fields[5], fields[7], -(fields[0] + fields[1])]]
    gen_real = jnp.stack([jnp.stack(r) for r in rows_real])
    gen_imag = jnp.stack([jnp.stack(r) for r in rows_imag])
    eye_full = jnp.eye(3, dtype=jnp.float32).reshape((3, 3) + (1,) * (gen_real.ndim - 2))
    lower = inverse_three_drawn(eye_full - 0.5 * gen_real, -0.5 * gen_imag)
    upper = (eye_full + 0.5 * gen_real, 0.5 * gen_imag)
    return jnp.stack(complex_mul_drawn(upper, lower))


def draw_gauge_links(key, part):
    coord_x = jnp.arange(NX, dtype=jnp.float32) / (NX - 1)
    coord_s = jnp.arange(SIDE, dtype=jnp.float32) / (SIDE - 1)
    shape = (3, 8, NX, SIDE, SIDE)
    noise = jax.random.normal(key, shape, jnp.float32)
    scale = 0.15 * jnp.power(10.0, 0.5 * coord_x[:, None, None] + 0.5 * coord_s[None, :, None])
    fields = noise * scale
    built = jnp.stack([make_unitary(fields[d]) for d in range(3)])
    return built.reshape(3, 2, 3, 3, NX, SIDE * SIDE).astype(jnp.float32)


def setup_inputs(seed: int = 0, part: int = 0) -> dict:
    splits = jax.random.split(jax.random.key(seed), 2)
    part_splits = jax.random.split(jax.random.fold_in(splits[1], part), 2)
    return {
        "gauge_links": draw_gauge_links(jax.random.fold_in(jax.random.fold_in(splits[1], part), 71), part),
    }


step_size = 0.08
peak_square = 12.0


def matrix_mul(left, right):
    return jnp.sum(left[:, :, None] * right[None, :, :], axis=1)


def complex_mul(left, right):
    real_part = matrix_mul(left[0], right[0]) - matrix_mul(left[1], right[1])
    imag_part = matrix_mul(left[0], right[1]) + matrix_mul(left[1], right[0])
    return real_part, imag_part


def dagger(matrix):
    return jnp.swapaxes(matrix[0], 0, 1), -jnp.swapaxes(matrix[1], 0, 1)


def scalar_mul(left, right):
    return left[0] * right[0] - left[1] * right[1], left[0] * right[1] + left[1] * right[0]


def inverse_three(real_part, imag_part):
    def entry(i, j):
        return real_part[i % 3, j % 3], imag_part[i % 3, j % 3]

    cofactor = []
    for i in range(3):
        row_list = []
        for j in range(3):
            first = scalar_mul(entry(i + 1, j + 1), entry(i + 2, j + 2))
            second = scalar_mul(entry(i + 1, j + 2), entry(i + 2, j + 1))
            row_list.append((first[0] - second[0], first[1] - second[1]))
        cofactor.append(row_list)
    det_real = 0.0
    det_imag = 0.0
    for j in range(3):
        term = scalar_mul(entry(0, j), cofactor[0][j])
        det_real = det_real + term[0]
        det_imag = det_imag + term[1]
    denom = det_real * det_real + det_imag * det_imag
    recip = (det_real / denom, -det_imag / denom)
    rows_real = []
    rows_imag = []
    for i in range(3):
        line_real = []
        line_imag = []
        for j in range(3):
            value = scalar_mul(cofactor[j][i], recip)
            line_real.append(value[0])
            line_imag.append(value[1])
        rows_real.append(jnp.stack(line_real))
        rows_imag.append(jnp.stack(line_imag))
    return jnp.stack(rows_real), jnp.stack(rows_imag)


def identity_like(array):
    return jnp.eye(3, dtype=jnp.float32).reshape((3, 3) + (1,) * (array.ndim - 2))


def cayley(matrix):
    eye_full = identity_like(matrix[0])
    lower_real, lower_imag = inverse_three(eye_full - 0.5 * matrix[0], -0.5 * matrix[1])
    upper = (eye_full + 0.5 * matrix[0], 0.5 * matrix[1])
    return complex_mul(upper, (lower_real, lower_imag))


def rebuild(fields):
    empty_part = jnp.zeros_like(fields[0])
    rows_real = [[empty_part, fields[2], fields[4]], [-fields[2], empty_part, fields[6]], [-fields[4], -fields[6], empty_part]]
    rows_imag = [[fields[0], fields[3], fields[5]], [fields[3], fields[1], fields[7]], [fields[5], fields[7], -(fields[0] + fields[1])]]
    return jnp.stack([jnp.stack(r) for r in rows_real]), jnp.stack([jnp.stack(r) for r in rows_imag])


def traceless(div_real, div_imag):
    anti_real = 0.5 * (div_real - jnp.swapaxes(div_real, 0, 1))
    anti_imag = 0.5 * (div_imag + jnp.swapaxes(div_imag, 0, 1))
    trace_part = (anti_imag[0, 0] + anti_imag[1, 1] + anti_imag[2, 2]) / 3.0
    anti_imag = anti_imag - identity_like(anti_imag) * trace_part
    fields = jnp.stack([anti_imag[0, 0], anti_imag[1, 1], anti_real[0, 1], anti_imag[0, 1], anti_real[0, 2], anti_imag[0, 2], anti_real[1, 2], anti_imag[1, 2]])
    return anti_real, anti_imag, fields


def sine_square(index, length):
    value = jnp.sin(index.astype(jnp.float32) * (math.pi / length))
    return 4.0 * value * value


def reference(gauge_links):
    count_x = gauge_links.shape[4]
    cells = SIDE * SIDE
    merged = jnp.arange(cells, dtype=jnp.int32)
    square_x = sine_square(jnp.arange(count_x, dtype=jnp.int32), count_x)
    square_yz = sine_square(merged // SIDE, SIDE) + sine_square(merged % SIDE, SIDE)
    total = square_x[:, None] + square_yz[None, :]
    safe = jnp.where(total > 0, total, 1.0)
    kernel = jnp.where(total > 0, peak_square / safe, 0.0).reshape(count_x, SIDE, SIDE)
    state = gauge_links
    values = []
    for turn in range(ITERS):
        cube = state.reshape(3, 2, 3, 3, count_x, SIDE, SIDE)
        diverge = jnp.roll(cube[0], 1, axis=3) - cube[0]
        diverge = diverge + jnp.roll(cube[1], 1, axis=4) - cube[1]
        diverge = diverge + jnp.roll(cube[2], 1, axis=5) - cube[2]
        anti_real, anti_imag, fields = traceless(diverge[0], diverge[1])
        values.append(jnp.sum(anti_real * anti_real + anti_imag * anti_imag) / (9.0 * count_x * cells))
        spectrum = jnp.fft.fftn(fields, axes=(1, 2, 3)) * kernel
        filtered = jnp.real(jnp.fft.ifftn(spectrum, axes=(1, 2, 3))).astype(jnp.float32)
        rotation = cayley(rebuild(step_size * filtered))
        updated = []
        for d in range(3):
            ahead = (jnp.roll(rotation[0], -1, axis=2 + d), jnp.roll(rotation[1], -1, axis=2 + d))
            moved = complex_mul(complex_mul(rotation, (cube[d, 0], cube[d, 1])), dagger(ahead))
            updated.append(jnp.stack(moved))
        state = jnp.stack(updated).reshape(3, 2, 3, 3, count_x, cells)
    return state, jnp.stack(values)
```

```python
import functools
import math

import jax
import jax.numpy as jnp
import numpy as np
from jax import lax
from jax.experimental import pallas as pl
from jax.experimental.pallas import tpu as pltpu
from jax.sharding import PartitionSpec as P

SIDE = 96
LANES = 128

step_size = 0.08
peak_square = 12.0
gain = 0.5 * step_size * peak_square

params = functools.partial(pltpu.CompilerParams, vmem_limit_bytes=48 * 1024 * 1024)


class Plan:
    def __init__(self, count_x, side):
        self.count_x, self.side = count_x, side
        self.cells = side * side
        self.rows = self.cells // LANES
        self.period = side * LANES // math.gcd(side, LANES)
        self.wide = self.period // LANES
        self.folds = self.period // side
        self.groups = self.cells // self.period
        self.pairs = count_x // 2
        self.share = side // self.pairs
        self.full = self.share // 8 * 8
        self.rest = self.share - self.full
        self.tiles = 4 * side // LANES
        self.block = self.tiles * self.share
        self.sent = -(-3 * self.block // 8) * 8
        self.returned = -(-2 * self.block // 8) * 8 + 8


def fourier(length):
    site = np.arange(length)
    basis = np.zeros((length, length))
    for k in range(length):
        angle = 2.0 * math.pi * (k * site % length) / length
        if k == 0 or 2 * k == length:
            basis[k] = np.cos(angle) / math.sqrt(length)
        elif 2 * k < length:
            basis[k] = np.cos(angle) * math.sqrt(2.0 / length)
        else:
            basis[k] = np.sin(angle) * math.sqrt(2.0 / length)
    return basis


def eigen(length):
    return 4.0 * np.sin(math.pi * np.arange(length) / length) ** 2


def split_table(table):
    high = table.astype(jnp.bfloat16)
    low = (table - high.astype(np.float64)).astype(jnp.bfloat16)
    return np.stack([high, low])


def tables(plan):
    side, folds, groups = plan.side, plan.folds, plan.groups
    basis = fourier(side)
    last = np.zeros((folds, side, folds, LANES))
    for j in range(folds):
        last[j, :, j, :side] = basis.T
    last = last.reshape(folds * side, folds * LANES)
    order = [plan.share * j + i for j in range(plan.pairs) for i in range(plan.full)]
    order += [plan.share * j + plan.full + i for j in range(plan.pairs) for i in range(plan.rest)]
    columns = [folds * g + j for j in range(folds) for g in range(groups)]
    second = basis[order][:, columns]
    value = eigen(side)
    inverse_side = np.zeros((side, LANES))
    inverse_side[:, :side] = 1.0 / (2.0 + value[order][:, None] + value[None, :])
    lane = np.arange(plan.tiles * LANES).reshape(plan.tiles, 1, LANES)
    owner = np.zeros((plan.pairs, plan.block, LANES))
    for j in range(plan.pairs):
        parts = []
        for start, size in ((0, plan.full), (plan.full, plan.rest)):
            mode = plan.share * j + start + np.arange(size).reshape(1, size, 1)
            parts.append((value[mode] + value[lane % side]).reshape(plan.tiles * size, LANES))
        owner[j] = np.concatenate(parts)
    weights = np.zeros((2, plan.block, LANES))
    for quad, values in enumerate(((1.5, 0.5, 2.0, 2.0), (2.0, 2.0, 2.0, 2.0))):
        of_lane = np.array(values)[lane // side]
        parts = [
            np.broadcast_to(of_lane, (plan.tiles, size, LANES)).reshape(plan.tiles * size, LANES)
            for size in (plan.full, plan.rest)
        ]
        weights[quad] = np.concatenate(parts)
    return {
        "last": split_table(last),
        "last_back": split_table(last.T),
        "second": split_table(second),
        "second_back": split_table(second.T),
        "inverse_side": inverse_side.astype(np.float32),
        "owner": owner.astype(np.float32),
        "weights": weights.astype(np.float32),
    }


def halve(value):
    high = value.astype(jnp.bfloat16)
    low = (value - high.astype(jnp.float32)).astype(jnp.bfloat16)
    return high, low


def product(left, right):
    dot = functools.partial(jnp.dot, preferred_element_type=jnp.float32)
    return dot(left[0], right[0]) + (dot(left[0], right[1]) + dot(left[1], right[0]))


def lane_of(shape):
    return lax.broadcasted_iota(jnp.int32, shape, 1)


def moved(ref, field, start, size, distance):
    down, over = distance // LANES, distance % LANES
    here = ref[field, pl.ds(start + down, size), :]
    after = ref[field, pl.ds(start + down + 1, size), :]
    mixed = jnp.where(lane_of(here.shape) >= over, here, after)
    return pltpu.roll(mixed, LANES - over, 1)


def last_index(rows, side):
    row = lax.broadcasted_iota(jnp.int32, (rows, LANES), 0)
    return (row * LANES + lane_of((rows, LANES))) % side


def wrap(ref, field, rows):
    ref[field, pl.ds(0, 8), :] = ref[field, pl.ds(rows, 8), :]
    ref[field, pl.ds(8 + rows, 8), :] = ref[field, pl.ds(8, 8), :]


def projected(links, d):
    def entry(part, i, j):
        return links[((d * 2 + part) * 3 + i) * 3 + j]

    im00, im11, im22 = entry(1, 0, 0), entry(1, 1, 1), entry(1, 2, 2)
    fields = [(im00 + im11 - 2.0 * im22) * (1.0 / 3.0), im00 - im11]
    for i, j in ((0, 1), (0, 2), (1, 2)):
        fields.append(0.5 * (entry(0, i, j) - entry(0, j, i)))
        fields.append(0.5 * (entry(1, i, j) + entry(1, j, i)))
    return fields


def divergence_kernel(plan, steps, index_ref, links_ref, keep_ref, send_ref, first, second, third):
    rows, side = plan.rows, plan.side
    size = rows // steps
    step = pl.program_id(0)
    start = pl.multiple_of(step * size, 8)
    for d, target, lead in ((0, first, 0), (1, second, 8), (2, third, 8)):
        for f, value in enumerate(projected(links_ref, d)):
            target[f, pl.ds(start + lead, size), :] = value

    @pl.when(step == steps - 1)
    def _():
        odd = index_ref[0] % 2
        at_start = last_index(rows, side) == 0
        diverge, direct = [], []
        for f in range(8):
            wrap(second, f, rows)
            wrap(third, f, rows)
            behind = moved(second, f, 8, rows, -side)
            beside = jnp.where(
                at_start, moved(third, f, 8, rows, side - 1), moved(third, f, 8, rows, -1)
            )
            here = first[f]
            total = (behind - second[f, pl.ds(8, rows), :]) + (
                beside - third[f, pl.ds(8, rows), :]
            )
            diverge.append(total - here)
            direct.append(here)
        for f in range(4):
            for part, values in enumerate((diverge, direct)):
                place = pl.ds((part * 4 + f) * rows, rows)
                keep_ref[place, :] = jnp.where(odd == 0, values[f], values[4 + f])
                send_ref[place, :] = jnp.where(odd == 0, values[4 + f], values[f])


def forward_kernel(
    plan, index_ref, keep_ref, got_ref, last_ref, second_ref, inverse_ref, sent_ref, odd_ref, dense
):
    rows, groups, folds, side = plan.rows, plan.groups, plan.folds, plan.side
    odd = index_ref[0] % 2
    quad = 4 * rows
    for f in range(4):
        own_d, own_a = keep_ref[pl.ds(f * rows, rows), :], keep_ref[pl.ds(quad + f * rows, rows), :]
        got_d, got_a = got_ref[pl.ds(f * rows, rows), :], got_ref[pl.ds(quad + f * rows, rows), :]
        even_d, odd_d = jnp.where(odd == 0, own_d, got_d), jnp.where(odd == 0, got_d, own_d)
        even_a, odd_a = jnp.where(odd == 0, own_a, got_a), jnp.where(odd == 0, got_a, own_a)
        for q, value in enumerate((even_d, odd_d + even_a, odd_a)):
            dense[pl.ds((q * 4 + f) * rows, rows), :] = value
    count = 12 * groups
    wide = jnp.concatenate(
        [dense[pl.ds(s, count, stride=plan.wide), :] for s in range(plan.wide)], axis=1
    )
    waves = product(halve(wide), (last_ref[0], last_ref[1]))
    columns = []
    for pf in range(12):
        part = waves[pf * groups : (pf + 1) * groups]
        columns.append(
            jnp.concatenate([part[:, j * LANES : (j + 1) * LANES] for j in range(folds)], axis=0)
        )
    modes = product((second_ref[0], second_ref[1]), halve(jnp.concatenate(columns, axis=1)))
    inverse = inverse_ref[...]
    full, rest, pairs, tiles = plan.full, plan.rest, plan.pairs, plan.tiles
    lane = lane_of((side, LANES))
    for q in range(3):
        fields = [modes[:, (q * 4 + f) * LANES : (q * 4 + f + 1) * LANES] for f in range(4)]
        if q == 1:
            for f in range(4):
                odd_ref[:, f * LANES : (f + 1) * LANES] = fields[f] * (gain * inverse)
        for t, value in enumerate(pack(fields, lane, side)):
            at = q * tiles + t
            for j in range(pairs):
                if full:
                    sent_ref[j, pl.ds(at * full, full), :] = value[j * full : (j + 1) * full]
                if rest:
                    begin = pairs * full + j * rest
                    sent_ref[j, pl.ds(3 * tiles * full + at * rest, rest), :] = value[
                        begin : begin + rest
                    ]
    spare = plan.sent - 3 * plan.block
    if spare:
        sent_ref[:, pl.ds(3 * plan.block, spare), :] = jnp.zeros((pairs, spare, LANES), jnp.float32)


def pack(fields, lane, side):
    rolled = [
        value if f * side % LANES == 0 else pltpu.roll(value, f * side % LANES, 1)
        for f, value in enumerate(fields)
    ]
    packed = []
    for t in range(4 * side // LANES):
        value = None
        for f in range(4):
            if f * side < (t + 1) * LANES and (f + 1) * side > t * LANES:
                value = rolled[f] if value is None else jnp.where(lane >= f * side - t * LANES, rolled[f], value)
        packed.append(value)
    return packed


def unpack(packed, lane, side):
    fields = []
    for f in range(4):
        begin = f * side // LANES
        end = ((f + 1) * side - 1) // LANES
        offset = f * side % LANES
        value = packed[begin]
        if end != begin:
            value = jnp.where(lane >= offset, packed[begin], packed[end])
        if offset:
            value = pltpu.roll(value, LANES - offset, 1)
        fields.append(jnp.where(lane < side, value, 0.0))
    return fields


def filter_kernel(plan, index_ref, got_ref, owner_ref, weight_ref, back_ref):
    pairs, tiles, count_x = plan.pairs, plan.tiles, plan.count_x
    half = pairs // 2
    drift = 0.0
    for part, (size, first, second) in enumerate(
        ((plan.full, 0, 0), (plan.rest, 3 * tiles * plan.full, 2 * tiles * plan.full))
    ):
        if not size:
            continue
        length = tiles * size
        own = pl.ds(0 if part == 0 else tiles * plan.full, length)
        value = owner_ref[0, own, :]
        weight = weight_ref[0, own, :]

        def plane(p, q):
            return got_ref[p, pl.ds(first + q * length, length), :]

        inverse = 1.0 / (2.0 + value)
        odds = [plane(p, 1) for p in range(pairs)]
        evens = [plane(p, 0) + plane((p - 1) % pairs, 2) for p in range(pairs)]
        square = jnp.zeros_like(value)
        for p in range(pairs):
            square = square + (odds[p] * odds[p] + evens[p] * evens[p])
        drift = drift + jnp.sum(square * weight)
        rhs = [evens[p] + (odds[p] + odds[(p - 1) % pairs]) * inverse for p in range(pairs)]
        plus = [rhs[d] + rhs[pairs - d] for d in range(1, half)]
        minus = [rhs[d] - rhs[pairs - d] for d in range(1, half)]
        cosines, sines = [], []
        for k in range(half + 1):
            total = rhs[0] + rhs[half] if k % 2 == 0 else rhs[0] - rhs[half]
            for d in range(1, half):
                total = total + plus[d - 1] * math.cos(2 * math.pi * (k * d % pairs) / pairs)
            root = 4.0 * math.sin(math.pi * k / count_x) ** 2
            below = (value + root) * (value + (4.0 - root))
            scale = gain / pairs * (1.0 if k in (0, half) else 2.0)
            if k == 0:
                factor = jnp.where(value > 0, scale * (2.0 + value) / jnp.where(value > 0, below, 1.0), 0.0)
                whole = odds[0]
                for p in range(1, pairs):
                    whole = whole + odds[p]
                mean = jnp.where(value > 0, 0.0, whole * (-0.25 * gain / pairs))
                cosines.append(total * factor + mean)
            else:
                factor = scale * (2.0 + value) / below
                cosines.append(total * factor)
                if k < half:
                    wave = jnp.zeros_like(value)
                    for d in range(1, half):
                        wave = wave + minus[d - 1] * math.sin(2 * math.pi * (k * d % pairs) / pairs)
                    sines.append(wave * factor)
        results = [None] * pairs
        for d in range(half + 1):
            even = cosines[0]
            for k in range(1, half + 1):
                even = even + cosines[k] * math.cos(2 * math.pi * (k * d % pairs) / pairs)
            if d in (0, half):
                results[d] = even
            else:
                wave = jnp.zeros_like(value)
                for k in range(1, half):
                    wave = wave + sines[k - 1] * math.sin(2 * math.pi * (k * d % pairs) / pairs)
                results[d] = even + wave
                results[pairs - d] = even - wave
        for p in range(pairs):
            back_ref[p, pl.ds(second, length), :] = results[p]
            back_ref[p, pl.ds(second + length, length), :] = results[(p + 1) % pairs]
    spare = plan.returned - 2 * plan.block
    for p in range(pairs):
        back_ref[p, pl.ds(2 * plan.block, spare), :] = jnp.full((spare, LANES), drift, jnp.float32)


def backward_kernel(
    plan, index_ref, got_ref, odd_ref, last_ref, second_ref, inverse_ref, keep_ref, send_ref, packed, dense
):
    rows, groups, folds, side = plan.rows, plan.groups, plan.folds, plan.side
    full, rest, pairs, tiles = plan.full, plan.rest, plan.pairs, plan.tiles
    odd = index_ref[0] % 2
    for q in range(2):
        for t in range(tiles):
            at = q * tiles + t
            for j in range(pairs):
                if full:
                    packed[at, pl.ds(j * full, full), :] = got_ref[j, pl.ds(at * full, full), :]
                if rest:
                    packed[at, pl.ds(pairs * full + j * rest, rest), :] = got_ref[
                        j, pl.ds(2 * tiles * full + at * rest, rest), :
                    ]
    lane = lane_of((side, LANES))
    inverse = inverse_ref[...]
    even, after = [
        unpack([packed[q * tiles + t] for t in range(tiles)], lane, side) for q in range(2)
    ]
    between = [
        odd_ref[:, f * LANES : (f + 1) * LANES] + (even[f] + after[f]) * inverse for f in range(4)
    ]
    waves = product(
        (second_ref[0], second_ref[1]), halve(jnp.concatenate(even + between + after, axis=1))
    )
    blocks = []
    for pf in range(12):
        part = waves[:, pf * LANES : (pf + 1) * LANES]
        blocks.append(
            jnp.concatenate([part[j * groups : (j + 1) * groups] for j in range(folds)], axis=1)
        )
    wide = product(halve(jnp.concatenate(blocks, axis=0)), (last_ref[0], last_ref[1]))
    count = 12 * groups
    for s in range(plan.wide):
        dense[pl.ds(s, count, stride=plan.wide), :] = wide[:, s * LANES : (s + 1) * LANES]
    quad = 4 * rows
    low, middle, high = [dense[pl.ds(q * quad, quad), :] for q in range(3)]
    keep_ref[pl.ds(0, quad), :] = jnp.where(odd == 0, low, middle)
    keep_ref[pl.ds(quad, quad), :] = jnp.where(odd == 0, middle, high)
    send_ref[pl.ds(0, quad), :] = jnp.where(odd == 0, middle, low)
    send_ref[pl.ds(quad, quad), :] = jnp.where(odd == 0, high, middle)
    drift = got_ref[0, pl.ds(2 * plan.block, 8), :]
    for j in range(1, pairs):
        drift = drift + got_ref[j, pl.ds(2 * plan.block, 8), :]
    keep_ref[pl.ds(2 * quad, 8), :] = drift
    send_ref[pl.ds(2 * quad, 8), :] = drift


def times(left, right):
    return (left[0] * right[0] - left[1] * right[1], left[0] * right[1] + left[1] * right[0])


def times_conj(left, right):
    return (left[0] * right[0] + left[1] * right[1], left[1] * right[0] - left[0] * right[1])


def rotation(fields):
    both, apart = fields[0], fields[1]
    a, b, e = 0.5 * (both + apart), 0.5 * (both - apart), -both
    u, v, w = (fields[2], fields[3]), (fields[4], fields[5]), (fields[6], fields[7])
    square = [x[0] * x[0] + x[1] * x[1] for x in (u, v, w)]
    a00, a11, a22 = square[2] - b * e, square[1] - a * e, square[0] - a * b
    vw, uw, vu = times_conj(v, w), times(u, w), times_conj(v, u)
    a01 = (e * u[1] - vw[0], -(e * u[0]) - vw[1])
    a02 = (uw[0] + b * v[1], uw[1] - b * v[0])
    a12 = (a * w[1] - vu[0], -(a * w[0]) - vu[1])
    turn = a * a00 + times_conj(u, a01)[1] + times_conj(v, a02)[1]
    real = 1.0 + (a00 + a11 + a22)
    scale = 2.0 / (real * real + turn * turn)
    factor = (real * scale, turn * scale)
    entries = [[None] * 3 for _ in range(3)]
    for i, (up, imag) in enumerate(((a00, a), (a11, b), (a22, e))):
        value = times((1.0 + up, imag), factor)
        entries[i][i] = (value[0] - 1.0, value[1])
    for (i, j), up, off in (((0, 1), a01, u), ((0, 2), a02, v), ((1, 2), a12, w)):
        entries[i][j] = times((up[0] + off[0], up[1] + off[1]), factor)
        entries[j][i] = times((up[0] - off[0], off[1] - up[1]), factor)
    return [entries[i][j][part] for part in range(2) for i in range(3) for j in range(3)]


def update_kernel(
    plan, steps, index_ref, keep_ref, got_ref, links_ref, fixed_ref, drift_ref, here, along_x, along_y, along_z
):
    rows, side = plan.rows, plan.side
    quad = 4 * rows
    size = rows // steps
    step = pl.program_id(0)

    @pl.when(step == 0)
    def _():
        odd = index_ref[0] % 2

        def turn(i, _):
            begin = pl.multiple_of(i * 8, 8)
            for q, target, lead in ((0, here, 8), (1, along_x, 0)):
                fields = [None] * 8
                for f in range(4):
                    place = pl.ds(pl.multiple_of(q * quad + f * rows + begin, 8), 8)
                    own, other = keep_ref[place, :], got_ref[place, :]
                    fields[f] = jnp.where(odd == 0, own, other)
                    fields[4 + f] = jnp.where(odd == 0, other, own)
                for n, value in enumerate(rotation(fields)):
                    target[n, pl.ds(begin + lead, 8), :] = value
            return 0

        lax.fori_loop(0, rows // 8, turn, 0)
        at_end = last_index(rows, side) == side - 1
        for n in range(18):
            wrap(here, n, rows)
            along_y[n] = moved(here, n, 8, rows, side)
            along_z[n] = jnp.where(
                at_end, moved(here, n, 8, rows, 1 - side), moved(here, n, 8, rows, 1)
            )
        total = keep_ref[pl.ds(2 * quad, 8), :] + got_ref[pl.ds(2 * quad, 8), :]
        drift_ref[0] = total[0, 0] * (1.0 / (9.0 * plan.count_x * plan.cells))

    def update(i, _):
        begin = pl.multiple_of(i * 8, 8)
        place = pl.multiple_of(step * size + i * 8, 8)

        def matrix(ref, lead):
            value = [ref[n, pl.ds(place + lead, 8), :] for n in range(18)]
            return [[(value[3 * r + c], value[9 + 3 * r + c]) for c in range(3)] for r in range(3)]

        for d, ahead_ref in enumerate((along_x, along_y, along_z)):
            own = matrix(here, 8)
            links = [
                [
                    tuple(links_ref[((d * 2 + part) * 3 + r) * 3 + c, pl.ds(begin, 8), :] for part in range(2))
                    for c in range(3)
                ]
                for r in range(3)
            ]
            ahead = matrix(ahead_ref, 0)
            for r in range(3):
                line = [
                    add(times(own[r][0], links[0][c]), times(own[r][1], links[1][c]), times(own[r][2], links[2][c]))
                    for c in range(3)
                ]
                for c in range(3):
                    value = add(*[times_conj(line[k], ahead[c][k]) for k in range(3)])
                    for part in range(2):
                        fixed_ref[((d * 2 + part) * 3 + r) * 3 + c, pl.ds(begin, 8), :] = value[part]
        return 0

    lax.fori_loop(0, size // 8, update, 0)


def add(first, second, third):
    return (first[0] + second[0] + third[0], first[1] + second[1] + third[1])


def whole_spec():
    return pl.BlockSpec(memory_space=pltpu.VMEM)


def scalar_spec():
    return pl.BlockSpec(memory_space=pltpu.SMEM)


def shape_of(*shape):
    return jax.ShapeDtypeStruct(shape, jnp.float32)


def local(gauge_links):
    count_x = lax.axis_size("gx")
    plan = Plan(count_x, SIDE)
    rows, pairs = plan.rows, plan.pairs
    table = tables(plan)
    index = lax.axis_index("gx").astype(jnp.int32).reshape(1)
    links = gauge_links.reshape(54, rows, LANES)
    steps = 3
    block = pl.BlockSpec((54, rows // steps, LANES), lambda i: (0, i, 0))
    quads = 8 * rows
    swap = [(i, i ^ 1) for i in range(count_x)]
    same_core = [[c + 2 * p for p in range(pairs)] for c in range(2)]

    keep, send = pl.pallas_call(
        functools.partial(divergence_kernel, plan, steps),
        grid=(steps,),
        out_shape=(shape_of(quads, LANES), shape_of(quads, LANES)),
        in_specs=[scalar_spec(), block],
        out_specs=(whole_spec(), whole_spec()),
        scratch_shapes=[
            pltpu.VMEM((8, rows, LANES), jnp.float32),
            pltpu.VMEM((8, rows + 16, LANES), jnp.float32),
            pltpu.VMEM((8, rows + 16, LANES), jnp.float32),
        ],
        compiler_params=params(),
        name="divergence",
    )(index, links)
    got = lax.ppermute(send, "gx", swap)
    sent, odd_part = pl.pallas_call(
        functools.partial(forward_kernel, plan),
        out_shape=(shape_of(pairs, plan.sent, LANES), shape_of(SIDE, 4 * LANES)),
        in_specs=[scalar_spec()] + [whole_spec()] * 5,
        out_specs=(whole_spec(), whole_spec()),
        scratch_shapes=[pltpu.VMEM((12 * rows, LANES), jnp.float32)],
        compiler_params=params(),
        name="forward",
    )(index, keep, got, table["last"], table["second"], table["inverse_side"])
    arrived = lax.all_to_all(
        sent, "gx", split_axis=0, concat_axis=0, tiled=True, axis_index_groups=same_core
    )
    back = pl.pallas_call(
        functools.partial(filter_kernel, plan),
        grid_spec=pltpu.PrefetchScalarGridSpec(
            num_scalar_prefetch=1,
            grid=(1,),
            in_specs=[
                pl.BlockSpec((pairs, plan.sent, LANES), lambda i, at: (0, 0, 0)),
                pl.BlockSpec((1, plan.block, LANES), lambda i, at: (at[0] // 2, 0, 0)),
                pl.BlockSpec((1, plan.block, LANES), lambda i, at: (at[0] % 2, 0, 0)),
            ],
            out_specs=pl.BlockSpec((pairs, plan.returned, LANES), lambda i, at: (0, 0, 0)),
        ),
        out_shape=shape_of(pairs, plan.returned, LANES),
        compiler_params=params(),
        name="filter",
    )(index, arrived, table["owner"], table["weights"])
    returned = lax.all_to_all(
        back, "gx", split_axis=0, concat_axis=0, tiled=True, axis_index_groups=same_core
    )
    keep, send = pl.pallas_call(
        functools.partial(backward_kernel, plan),
        out_shape=(shape_of(quads + 8, LANES), shape_of(quads + 8, LANES)),
        in_specs=[scalar_spec()] + [whole_spec()] * 5,
        out_specs=(whole_spec(), whole_spec()),
        scratch_shapes=[
            pltpu.VMEM((2 * plan.tiles, SIDE, LANES), jnp.float32),
            pltpu.VMEM((12 * rows, LANES), jnp.float32),
        ],
        compiler_params=params(),
        name="backward",
    )(index, returned, odd_part, table["last_back"], table["second_back"], table["inverse_side"])
    got = lax.ppermute(send, "gx", swap)
    fixed, drift = pl.pallas_call(
        functools.partial(update_kernel, plan, steps),
        grid=(steps,),
        out_shape=(shape_of(54, rows, LANES), shape_of(1)),
        in_specs=[scalar_spec(), whole_spec(), whole_spec(), block],
        out_specs=(block, scalar_spec()),
        scratch_shapes=[
            pltpu.VMEM((18, rows + 16, LANES), jnp.float32),
            pltpu.VMEM((18, rows, LANES), jnp.float32),
            pltpu.VMEM((18, rows, LANES), jnp.float32),
            pltpu.VMEM((18, rows, LANES), jnp.float32),
        ],
        compiler_params=params(),
        name="update",
    )(index, keep, got, links)
    return fixed.reshape(gauge_links.shape), drift


def solution(mesh):
    in_specs = (P(None, None, None, None, ("ta", "gx"), None),)
    out_specs = (P(None, None, None, None, ("ta", "gx"), None), P("ta"))
    return jax.shard_map(local, mesh=mesh, in_specs=in_specs, out_specs=out_specs, check_vma=False)
```

```python
import functools
import math

import jax
import jax.numpy as jnp
import numpy as np
from jax import lax
from jax.experimental import pallas as pl
from jax.experimental.pallas import tpu as pltpu
from jax.sharding import PartitionSpec as P

SIDE = 96
LANES = 128

step_size = 0.08
peak_square = 12.0
gain = 0.5 * step_size * peak_square

params = functools.partial(pltpu.CompilerParams, vmem_limit_bytes=48 * 1024 * 1024)
drift_weights = (1.5, 0.5, 2.0, 2.0, 2.0, 2.0, 2.0, 2.0)


class Plan:
    def __init__(self, count_x, side):
        self.count_x, self.side = count_x, side
        self.cells = side * side
        self.rows = self.cells // LANES
        self.period = side * LANES // math.gcd(side, LANES)
        self.wide = self.period // LANES
        self.folds = self.period // side
        self.groups = self.cells // self.period
        self.pairs = count_x // 2
        self.share = side // self.pairs
        self.full = self.share // 8 * 8
        self.rest = self.share - self.full
        self.tiles = 4 * side // LANES
        self.block = self.tiles * self.share
        self.sent = -(-2 * self.block // 8) * 8
        self.place = [(p + self.pairs // 2) % self.pairs for p in range(self.pairs)]
        self.returned = -(-(2 * self.block + 8) // 8) * 8


def fourier(length):
    site = np.arange(length)
    basis = np.zeros((length, length))
    for k in range(length):
        angle = 2.0 * math.pi * (k * site % length) / length
        if k == 0 or 2 * k == length:
            basis[k] = np.cos(angle) / math.sqrt(length)
        elif 2 * k < length:
            basis[k] = np.cos(angle) * math.sqrt(2.0 / length)
        else:
            basis[k] = np.sin(angle) * math.sqrt(2.0 / length)
    return basis


def eigen(length):
    return 4.0 * np.sin(math.pi * np.arange(length) / length) ** 2


def split_table(table):
    high = table.astype(jnp.bfloat16)
    low = (table - high.astype(np.float64)).astype(jnp.bfloat16)
    return np.stack([high, low])


def tables(plan):
    side, folds, groups = plan.side, plan.folds, plan.groups
    basis = fourier(side)
    last = np.zeros((folds, side, folds, LANES))
    for j in range(folds):
        last[j, :, j, :side] = basis.T
    last = last.reshape(folds * side, folds * LANES)
    order = [plan.share * j + i for j in range(plan.pairs) for i in range(plan.full)]
    order += [plan.share * j + plan.full + i for j in range(plan.pairs) for i in range(plan.rest)]
    columns = [folds * g + j for j in range(folds) for g in range(groups)]
    second = basis[order][:, columns]
    value = eigen(side)
    inverse_side = np.zeros((side, LANES))
    inverse_side[:, :side] = 1.0 / (2.0 + value[order][:, None] + value[None, :])
    lane = np.arange(plan.tiles * LANES).reshape(plan.tiles, 1, LANES)
    owner = np.zeros((plan.pairs, plan.block, LANES))
    for j in range(plan.pairs):
        parts = []
        for start, size in ((0, plan.full), (plan.full, plan.rest)):
            mode = plan.share * j + start + np.arange(size).reshape(1, size, 1)
            parts.append((value[mode] + value[lane % side]).reshape(plan.tiles * size, LANES))
        owner[j] = np.concatenate(parts)
    return {
        "last": split_table(last),
        "last_back": split_table(last.T),
        "second": split_table(second),
        "second_back": split_table(second.T),
        "inverse_side": inverse_side.astype(np.float32),
        "owner": owner.astype(np.float32),
    }


def halve(value):
    high = value.astype(jnp.bfloat16)
    low = (value - high.astype(jnp.float32)).astype(jnp.bfloat16)
    return high, low


def product(left, right):
    dot = functools.partial(jnp.dot, preferred_element_type=jnp.float32)
    return dot(left[0], right[0]) + (dot(left[0], right[1]) + dot(left[1], right[0]))


def lane_of(shape):
    return lax.broadcasted_iota(jnp.int32, shape, 1)


def moved(ref, field, start, size, distance):
    down, over = distance // LANES, distance % LANES
    here = ref[field, pl.ds(start + down, size), :]
    after = ref[field, pl.ds(start + down + 1, size), :]
    mixed = jnp.where(lane_of(here.shape) >= over, here, after)
    return pltpu.roll(mixed, LANES - over, 1)


def last_index(rows, side):
    row = lax.broadcasted_iota(jnp.int32, (rows, LANES), 0)
    return (row * LANES + lane_of((rows, LANES))) % side


def wrap(ref, field, rows):
    ref[field, pl.ds(0, 8), :] = ref[field, pl.ds(rows, 8), :]
    ref[field, pl.ds(8 + rows, 8), :] = ref[field, pl.ds(8, 8), :]


def projected(links, d):
    def entry(part, i, j):
        return links[((d * 2 + part) * 3 + i) * 3 + j]

    im00, im11, im22 = entry(1, 0, 0), entry(1, 1, 1), entry(1, 2, 2)
    fields = [(im00 + im11 - 2.0 * im22) * (1.0 / 3.0), im00 - im11]
    for i, j in ((0, 1), (0, 2), (1, 2)):
        fields.append(0.5 * (entry(0, i, j) - entry(0, j, i)))
        fields.append(0.5 * (entry(1, i, j) + entry(1, j, i)))
    return fields


def divergence_kernel(
    plan, index_ref, links_ref, keep_ref, send_ref, ahead_ref, base_ref, second, third
):
    rows, side = plan.rows, plan.side
    odd = index_ref[0] % 2
    at_start = last_index(rows, side) == 0
    middle = pl.ds(8, rows)
    for f, value in enumerate(projected(links_ref, 1)):
        second[f, middle, :] = value
        wrap(second, f, rows)
    diverge = [moved(second, f, 8, rows, -side) - second[f, middle, :] for f in range(8)]
    for f, value in enumerate(projected(links_ref, 2)):
        third[f, middle, :] = value
        wrap(third, f, rows)
    for f in range(8):
        beside = jnp.where(
            at_start, moved(third, f, 8, rows, side - 1), moved(third, f, 8, rows, -1)
        )
        diverge[f] = diverge[f] + (beside - third[f, middle, :])
        second[f, middle, :] = diverge[f]
    direct = projected(links_ref, 0)
    index = index_ref[0]
    for f in range(8):
        place = pl.ds(f * rows, rows)
        total = second[f, middle, :] - direct[f]
        ahead_ref[place, :] = jnp.where(index == plan.count_x - 1, direct[f], total)
        base_ref[place, :] = jnp.where(index == 0, total, direct[f])
    for f in range(4):
        for part in range(2):
            place = pl.ds((part * 4 + f) * rows, rows)
            low, high = direct[f], direct[4 + f]
            if part == 0:
                low, high = second[f, middle, :] - low, second[4 + f, middle, :] - high
            keep_ref[place, :] = jnp.where(odd == 0, low, high)
            send_ref[place, :] = jnp.where(odd == 0, high, low)


def forward_kernel(
    plan, index_ref, keep_ref, got_ref, last_ref, second_ref, inverse_ref, sent_ref, odd_ref, drift_ref, dense
):
    rows, groups, folds, side = plan.rows, plan.groups, plan.folds, plan.side
    odd = index_ref[0] % 2
    quad = 4 * rows
    square = jnp.zeros((rows, LANES), jnp.float32)
    for f in range(4):
        own_d, own_a = keep_ref[pl.ds(f * rows, rows), :], keep_ref[pl.ds(quad + f * rows, rows), :]
        got_d, got_a = got_ref[pl.ds(f * rows, rows), :], got_ref[pl.ds(quad + f * rows, rows), :]
        even_d, odd_d = jnp.where(odd == 0, own_d, got_d), jnp.where(odd == 0, got_d, own_d)
        even_a, odd_a = jnp.where(odd == 0, own_a, got_a), jnp.where(odd == 0, got_a, own_a)
        whole = odd_d + even_a
        for q, value in enumerate((even_d, whole, odd_a)):
            dense[pl.ds((q * 4 + f) * rows, rows), :] = value
        square = square + whole * whole * jnp.where(odd == 0, drift_weights[f], drift_weights[4 + f])
    drift_ref[...] = sum_tiles(square)
    count = 12 * groups
    wide = jnp.concatenate(
        [dense[pl.ds(s, count, stride=plan.wide), :] for s in range(plan.wide)], axis=1
    )
    waves = product(halve(wide), (last_ref[0], last_ref[1]))
    columns = []
    for pf in range(12):
        part = waves[pf * groups : (pf + 1) * groups]
        columns.append(
            jnp.concatenate([part[:, j * LANES : (j + 1) * LANES] for j in range(folds)], axis=0)
        )
    modes = product((second_ref[0], second_ref[1]), halve(jnp.concatenate(columns, axis=1)))
    inverse = inverse_ref[...]
    full, rest, pairs, tiles = plan.full, plan.rest, plan.pairs, plan.tiles
    lane = lane_of((side, LANES))
    zero = (lane == 0) & (lax.broadcasted_iota(jnp.int32, (side, LANES), 0) == 0)
    even, between, after = [
        [modes[:, (q * 4 + f) * LANES : (q * 4 + f + 1) * LANES] for f in range(4)] for q in range(3)
    ]
    shared = [value * inverse for value in between]
    for f in range(4):
        odd_ref[:, f * LANES : (f + 1) * LANES] = gain * shared[f]
    below = [even[f] + shared[f] for f in range(4)]
    above = [jnp.where(zero, between[f], after[f] + shared[f]) for f in range(4)]
    for q, fields in enumerate((below, above)):
        for t, value in enumerate(pack(fields, lane, side)):
            at = q * tiles + t
            for j in range(pairs):
                if full:
                    sent_ref[plan.place[j], pl.ds(at * full, full), :] = value[j * full : (j + 1) * full]
                if rest:
                    begin = pairs * full + j * rest
                    sent_ref[plan.place[j], pl.ds(2 * tiles * full + at * rest, rest), :] = value[
                        begin : begin + rest
                    ]
    spare = plan.sent - 2 * plan.block
    if spare:
        sent_ref[:, pl.ds(2 * plan.block, spare), :] = jnp.zeros((pairs, spare, LANES), jnp.float32)


def sum_tiles(value):
    total = value[:8]
    for i in range(1, value.shape[0] // 8):
        total = total + value[i * 8 : (i + 1) * 8]
    return total


def pack(fields, lane, side):
    rolled = [
        value if f * side % LANES == 0 else pltpu.roll(value, f * side % LANES, 1)
        for f, value in enumerate(fields)
    ]
    packed = []
    for t in range(4 * side // LANES):
        value = None
        for f in range(4):
            if f * side < (t + 1) * LANES and (f + 1) * side > t * LANES:
                value = rolled[f] if value is None else jnp.where(lane >= f * side - t * LANES, rolled[f], value)
        packed.append(value)
    return packed


def unpack(packed, lane, side):
    fields = []
    for f in range(4):
        begin = f * side // LANES
        end = ((f + 1) * side - 1) // LANES
        offset = f * side % LANES
        value = packed[begin]
        if end != begin:
            value = jnp.where(lane >= offset, packed[begin], packed[end])
        if offset:
            value = pltpu.roll(value, LANES - offset, 1)
        fields.append(jnp.where(lane < side, value, 0.0))
    return fields


def drift_kernel(plan, index_ref, odd_ref, beside_ref, base_ref, drift_ref):
    rows, count_x = plan.rows, plan.count_x
    index = index_ref[0]
    square = jnp.zeros((rows, LANES), jnp.float32)
    for f in range(8):
        place = pl.ds(f * rows, rows)
        value = beside_ref[place, :] + base_ref[place, :]
        square = square + value * value * drift_weights[f]
    complete = (index == 0) | ((index % 2 == 1) & (index < count_x - 1))
    drift_ref[...] = odd_ref[...] + jnp.where(complete, sum_tiles(square), 0.0)


def filter_kernel(plan, index_ref, got_ref, owner_ref, drift_ref, back_ref):
    pairs, tiles, count_x = plan.pairs, plan.tiles, plan.count_x
    half = pairs // 2
    drift = drift_ref[...]
    for part, (size, first) in enumerate(((plan.full, 0), (plan.rest, 2 * tiles * plan.full))):
        if not size:
            continue
        length = tiles * size
        value = owner_ref[0, pl.ds(0 if part == 0 else tiles * plan.full, length), :]
        low, high = pl.ds(first, length), pl.ds(first + length, length)
        inside = value > 0
        below = [got_ref[plan.place[p], low, :] for p in range(pairs)]
        above = [got_ref[plan.place[p], high, :] for p in range(pairs)]
        rhs = [
            below[p] + jnp.where(inside, above[(p - 1) % pairs], -below[(p - 1) % pairs])
            for p in range(pairs)
        ]
        plus = [rhs[d] + rhs[pairs - d] for d in range(1, half)]
        minus = [rhs[d] - rhs[pairs - d] for d in range(1, half)]
        cosines, sines = [], []
        for k in range(half + 1):
            total = rhs[0] + rhs[half] if k % 2 == 0 else rhs[0] - rhs[half]
            for d in range(1, half):
                total = total + plus[d - 1] * math.cos(2 * math.pi * (k * d % pairs) / pairs)
            root = 4.0 * math.sin(math.pi * k / count_x) ** 2
            split = (value + root) * (value + (4.0 - root))
            scale = gain / pairs * (1.0 if k in (0, half) else 2.0)
            if k == 0:
                factor = jnp.where(inside, scale * (2.0 + value) / jnp.where(inside, split, 1.0), 0.0)
                whole = above[0]
                for p in range(1, pairs):
                    whole = whole + above[p]
                mean = jnp.where(inside, 0.0, whole * (-0.25 * gain / pairs))
                cosines.append(total * factor + mean)
            else:
                factor = scale * (2.0 + value) / split
                cosines.append(total * factor)
                if k < half:
                    wave = jnp.zeros_like(value)
                    for d in range(1, half):
                        wave = wave + minus[d - 1] * math.sin(2 * math.pi * (k * d % pairs) / pairs)
                    sines.append(wave * factor)
        results = [None] * pairs
        for d in range(half + 1):
            even = cosines[0]
            for k in range(1, half + 1):
                even = even + cosines[k] * math.cos(2 * math.pi * (k * d % pairs) / pairs)
            if d in (0, half):
                results[d] = even
            else:
                wave = jnp.zeros_like(value)
                for k in range(1, half):
                    wave = wave + sines[k - 1] * math.sin(2 * math.pi * (k * d % pairs) / pairs)
                results[d] = even + wave
                results[pairs - d] = even - wave
        for p in range(pairs):
            back_ref[plan.place[p], low, :] = results[p]
            back_ref[plan.place[p], high, :] = results[(p + 1) % pairs]
    for p in range(pairs):
        back_ref[p, pl.ds(2 * plan.block, 8), :] = drift


def backward_kernel(
    plan, index_ref, got_ref, odd_ref, last_ref, second_ref, inverse_ref, keep_ref, send_ref, packed, dense
):
    rows, groups, folds, side = plan.rows, plan.groups, plan.folds, plan.side
    full, rest, pairs, tiles = plan.full, plan.rest, plan.pairs, plan.tiles
    odd = index_ref[0] % 2
    for q in range(2):
        for t in range(tiles):
            at = q * tiles + t
            for j in range(pairs):
                if full:
                    packed[at, pl.ds(j * full, full), :] = got_ref[plan.place[j], pl.ds(at * full, full), :]
                if rest:
                    packed[at, pl.ds(pairs * full + j * rest, rest), :] = got_ref[
                        plan.place[j], pl.ds(2 * tiles * full + at * rest, rest), :
                    ]
    lane = lane_of((side, LANES))
    inverse = inverse_ref[...]
    even, after = [
        unpack([packed[q * tiles + t] for t in range(tiles)], lane, side) for q in range(2)
    ]
    between = [
        odd_ref[:, f * LANES : (f + 1) * LANES] + (even[f] + after[f]) * inverse for f in range(4)
    ]
    waves = product(
        (second_ref[0], second_ref[1]), halve(jnp.concatenate(even + between + after, axis=1))
    )
    blocks = []
    for pf in range(12):
        part = waves[:, pf * LANES : (pf + 1) * LANES]
        blocks.append(
            jnp.concatenate([part[j * groups : (j + 1) * groups] for j in range(folds)], axis=1)
        )
    wide = product(halve(jnp.concatenate(blocks, axis=0)), (last_ref[0], last_ref[1]))
    count = 12 * groups
    for s in range(plan.wide):
        dense[pl.ds(s, count, stride=plan.wide), :] = wide[:, s * LANES : (s + 1) * LANES]
    quad = 4 * rows
    low, middle, high = [dense[pl.ds(q * quad, quad), :] for q in range(3)]
    keep_ref[pl.ds(0, quad), :] = jnp.where(odd == 0, low, middle)
    keep_ref[pl.ds(quad, quad), :] = jnp.where(odd == 0, middle, high)
    send_ref[pl.ds(0, quad), :] = jnp.where(odd == 0, middle, low)
    send_ref[pl.ds(quad, quad), :] = jnp.where(odd == 0, high, middle)
    drift = got_ref[0, pl.ds(2 * plan.block, 8), :]
    for j in range(1, pairs):
        drift = drift + got_ref[j, pl.ds(2 * plan.block, 8), :]
    keep_ref[pl.ds(2 * quad, 8), :] = drift
    send_ref[pl.ds(2 * quad, 8), :] = drift


def times(left, right):
    return (left[0] * right[0] - left[1] * right[1], left[0] * right[1] + left[1] * right[0])


def times_conj(left, right):
    return (left[0] * right[0] + left[1] * right[1], left[1] * right[0] - left[0] * right[1])


def rotation(fields):
    both, apart = fields[0], fields[1]
    a, b, e = 0.5 * (both + apart), 0.5 * (both - apart), -both
    u, v, w = (fields[2], fields[3]), (fields[4], fields[5]), (fields[6], fields[7])
    square = [x[0] * x[0] + x[1] * x[1] for x in (u, v, w)]
    a00, a11, a22 = square[2] - b * e, square[1] - a * e, square[0] - a * b
    vw, uw, vu = times_conj(v, w), times(u, w), times_conj(v, u)
    a01 = (e * u[1] - vw[0], -(e * u[0]) - vw[1])
    a02 = (uw[0] + b * v[1], uw[1] - b * v[0])
    a12 = (a * w[1] - vu[0], -(a * w[0]) - vu[1])
    turn = a * a00 + times_conj(u, a01)[1] + times_conj(v, a02)[1]
    real = 1.0 + (a00 + a11 + a22)
    scale = 2.0 / (real * real + turn * turn)
    factor = (real * scale, turn * scale)
    entries = [[None] * 3 for _ in range(3)]
    for i, (up, imag) in enumerate(((a00, a), (a11, b), (a22, e))):
        value = times((1.0 + up, imag), factor)
        entries[i][i] = (value[0] - 1.0, value[1])
    for (i, j), up, off in (((0, 1), a01, u), ((0, 2), a02, v), ((1, 2), a12, w)):
        entries[i][j] = times((up[0] + off[0], up[1] + off[1]), factor)
        entries[j][i] = times((up[0] - off[0], off[1] - up[1]), factor)
    return [entries[i][j][part] for part in range(2) for i in range(3) for j in range(3)]


def update_kernel(
    plan, steps, index_ref, keep_ref, got_ref, links_ref, fixed_ref, drift_ref, here, along_x, along_y, along_z
):
    rows, side = plan.rows, plan.side
    quad = 4 * rows
    size = rows // steps
    step = pl.program_id(0)

    @pl.when(step == 0)
    def _():
        odd = index_ref[0] % 2

        def turn(i, _):
            begin = pl.multiple_of(i * 8, 8)
            for q, target, lead in ((0, here, 8), (1, along_x, 0)):
                fields = [None] * 8
                for f in range(4):
                    place = pl.ds(pl.multiple_of(q * quad + f * rows + begin, 8), 8)
                    own, other = keep_ref[place, :], got_ref[place, :]
                    fields[f] = jnp.where(odd == 0, own, other)
                    fields[4 + f] = jnp.where(odd == 0, other, own)
                for n, value in enumerate(rotation(fields)):
                    target[n, pl.ds(begin + lead, 8), :] = value
            return 0

        lax.fori_loop(0, rows // 8, turn, 0)
        at_end = last_index(rows, side) == side - 1
        for n in range(18):
            wrap(here, n, rows)
            along_y[n] = moved(here, n, 8, rows, side)
            along_z[n] = jnp.where(
                at_end, moved(here, n, 8, rows, 1 - side), moved(here, n, 8, rows, 1)
            )
        total = keep_ref[pl.ds(2 * quad, 8), :] + got_ref[pl.ds(2 * quad, 8), :]
        drift_ref[0] = jnp.sum(total) * (1.0 / (9.0 * plan.count_x * plan.cells))

    def update(i, _):
        begin = pl.multiple_of(i * 8, 8)
        place = pl.multiple_of(step * size + i * 8, 8)

        def matrix(ref, lead):
            value = [ref[n, pl.ds(place + lead, 8), :] for n in range(18)]
            return [[(value[3 * r + c], value[9 + 3 * r + c]) for c in range(3)] for r in range(3)]

        for d, ahead_ref in enumerate((along_x, along_y, along_z)):
            own = matrix(here, 8)
            links = [
                [
                    tuple(links_ref[((d * 2 + part) * 3 + r) * 3 + c, pl.ds(begin, 8), :] for part in range(2))
                    for c in range(3)
                ]
                for r in range(3)
            ]
            ahead = matrix(ahead_ref, 0)
            for r in range(3):
                line = [
                    add(times(own[r][0], links[0][c]), times(own[r][1], links[1][c]), times(own[r][2], links[2][c]))
                    for c in range(3)
                ]
                for c in range(3):
                    value = add(*[times_conj(line[k], ahead[c][k]) for k in range(3)])
                    for part in range(2):
                        fixed_ref[((d * 2 + part) * 3 + r) * 3 + c, pl.ds(begin, 8), :] = value[part]
        return 0

    lax.fori_loop(0, size // 8, update, 0)


def add(first, second, third):
    return (first[0] + second[0] + third[0], first[1] + second[1] + third[1])


def whole_spec():
    return pl.BlockSpec(memory_space=pltpu.VMEM)


def scalar_spec():
    return pl.BlockSpec(memory_space=pltpu.SMEM)


def shape_of(*shape):
    return jax.ShapeDtypeStruct(shape, jnp.float32)


def local(gauge_links):
    count_x = lax.axis_size("gx")
    plan = Plan(count_x, SIDE)
    rows, pairs = plan.rows, plan.pairs
    table = tables(plan)
    index = lax.axis_index("gx").astype(jnp.int32).reshape(1)
    links = gauge_links.reshape(54, rows, LANES)
    steps = 3
    block = pl.BlockSpec((54, rows // steps, LANES), lambda i: (0, i, 0))
    quads = 8 * rows
    swap = [(i, i ^ 1) for i in range(count_x)]
    halo = [(2 * p, 2 * p - 1) for p in range(1, pairs)] + [(count_x - 1, 0)]
    same_core = [[c + 2 * p for p in sorted(range(pairs), key=plan.place.__getitem__)] for c in range(2)]

    keep, send, ahead, base = pl.pallas_call(
        functools.partial(divergence_kernel, plan),
        out_shape=(shape_of(quads, LANES),) * 4,
        in_specs=[scalar_spec(), whole_spec()],
        out_specs=(whole_spec(),) * 4,
        scratch_shapes=[
            pltpu.VMEM((8, rows + 16, LANES), jnp.float32),
            pltpu.VMEM((8, rows + 16, LANES), jnp.float32),
        ],
        compiler_params=params(),
        name="divergence",
    )(index, links)
    got = lax.ppermute(send, "gx", swap)
    beside = lax.ppermute(ahead, "gx", halo)
    sent, odd_part, odd_drift = pl.pallas_call(
        functools.partial(forward_kernel, plan),
        out_shape=(
            shape_of(pairs, plan.sent, LANES),
            shape_of(SIDE, 4 * LANES),
            shape_of(8, LANES),
        ),
        in_specs=[scalar_spec()] + [whole_spec()] * 5,
        out_specs=(whole_spec(),) * 3,
        scratch_shapes=[pltpu.VMEM((12 * rows, LANES), jnp.float32)],
        compiler_params=params(),
        name="forward",
    )(index, keep, got, table["last"], table["second"], table["inverse_side"])
    arrived = lax.all_to_all(
        sent, "gx", split_axis=0, concat_axis=0, tiled=True, axis_index_groups=same_core
    )
    drift_part = pl.pallas_call(
        functools.partial(drift_kernel, plan),
        out_shape=shape_of(8, LANES),
        in_specs=[scalar_spec()] + [whole_spec()] * 3,
        out_specs=whole_spec(),
        compiler_params=params(),
        cost_estimate=pl.CostEstimate(flops=5 * 10**10, bytes_accessed=5 * 10**7, transcendentals=0),
        name="drift",
    )(index, odd_drift, beside, base)
    back = pl.pallas_call(
        functools.partial(filter_kernel, plan),
        grid_spec=pltpu.PrefetchScalarGridSpec(
            num_scalar_prefetch=1,
            grid=(1,),
            in_specs=[
                pl.BlockSpec((pairs, plan.sent, LANES), lambda i, at: (0, 0, 0)),
                pl.BlockSpec((1, plan.block, LANES), lambda i, at: (at[0] // 2, 0, 0)),
                pl.BlockSpec((8, LANES), lambda i, at: (0, 0)),
            ],
            out_specs=pl.BlockSpec((pairs, plan.returned, LANES), lambda i, at: (0, 0, 0)),
        ),
        out_shape=shape_of(pairs, plan.returned, LANES),
        compiler_params=params(),
        name="filter",
    )(index, arrived, table["owner"], drift_part)
    returned = lax.all_to_all(
        back, "gx", split_axis=0, concat_axis=0, tiled=True, axis_index_groups=same_core
    )
    keep, send = pl.pallas_call(
        functools.partial(backward_kernel, plan),
        out_shape=(shape_of(quads + 8, LANES), shape_of(quads + 8, LANES)),
        in_specs=[scalar_spec()] + [whole_spec()] * 5,
        out_specs=(whole_spec(), whole_spec()),
        scratch_shapes=[
            pltpu.VMEM((2 * plan.tiles, SIDE, LANES), jnp.float32),
            pltpu.VMEM((12 * rows, LANES), jnp.float32),
        ],
        compiler_params=params(),
        name="backward",
    )(index, returned, odd_part, table["last_back"], table["second_back"], table["inverse_side"])
    got = lax.ppermute(send, "gx", swap)
    fixed, drift = pl.pallas_call(
        functools.partial(update_kernel, plan, steps),
        grid=(steps,),
        out_shape=(shape_of(54, rows, LANES), shape_of(1)),
        in_specs=[scalar_spec(), whole_spec(), whole_spec(), block],
        out_specs=(block, scalar_spec()),
        scratch_shapes=[
            pltpu.VMEM((18, rows + 16, LANES), jnp.float32),
            pltpu.VMEM((18, rows, LANES), jnp.float32),
            pltpu.VMEM((18, rows, LANES), jnp.float32),
            pltpu.VMEM((18, rows, LANES), jnp.float32),
        ],
        compiler_params=params(),
        name="update",
    )(index, keep, got, links)
    return fixed.reshape(gauge_links.shape), drift


def solution(mesh):
    in_specs = (P(None, None, None, None, ("ta", "gx"), None),)
    out_specs = (P(None, None, None, None, ("ta", "gx"), None), P("ta"))
    return jax.shard_map(local, mesh=mesh, in_specs=in_specs, out_specs=out_specs, check_vma=False)
```

```python
import functools
import math

import jax
import jax.numpy as jnp
import numpy as np
from jax import lax
from jax.experimental import pallas as pl
from jax.experimental.pallas import tpu as pltpu
from jax.sharding import PartitionSpec as P

SIDE = 96
LANES = 128

step_size = 0.08
peak_square = 12.0
gain = 0.5 * step_size * peak_square

params = functools.partial(pltpu.CompilerParams, vmem_limit_bytes=48 * 1024 * 1024)
drift_weights = (1.5, 0.5, 2.0, 2.0, 2.0, 2.0, 2.0, 2.0)


class Plan:
    def __init__(self, count_x, side):
        self.count_x, self.side = count_x, side
        self.cells = side * side
        self.rows = self.cells // LANES
        self.period = side * LANES // math.gcd(side, LANES)
        self.wide = self.period // LANES
        self.folds = self.period // side
        self.groups = self.cells // self.period
        self.pairs = count_x // 2
        self.share = side // self.pairs
        self.full = self.share // 8 * 8
        self.rest = self.share - self.full
        self.tiles = 4 * side // LANES
        self.block = self.tiles * self.share
        self.stride = -(-self.block // 8) * 8
        self.sent = -(-2 * self.block // 8) * 8
        self.place = [(p + self.pairs // 2) % self.pairs for p in range(self.pairs)]
        self.returned = -(-(2 * self.block + 8) // 8) * 8


def fourier(length):
    site = np.arange(length)
    basis = np.zeros((length, length))
    for k in range(length):
        angle = 2.0 * math.pi * (k * site % length) / length
        if k == 0 or 2 * k == length:
            basis[k] = np.cos(angle) / math.sqrt(length)
        elif 2 * k < length:
            basis[k] = np.cos(angle) * math.sqrt(2.0 / length)
        else:
            basis[k] = np.sin(angle) * math.sqrt(2.0 / length)
    return basis


def eigen(length):
    return 4.0 * np.sin(math.pi * np.arange(length) / length) ** 2


def split_table(table):
    high = table.astype(jnp.bfloat16)
    low = (table - high.astype(np.float64)).astype(jnp.bfloat16)
    return np.stack([high, low])


def stack_table(table):
    high, low = split_table(table)
    return np.block([[high, high], [low, np.zeros_like(low)]])


def tables(plan):
    side, folds, groups = plan.side, plan.folds, plan.groups
    basis = fourier(side)
    last = np.zeros((folds, side, folds, LANES))
    for j in range(folds):
        last[j, :, j, :side] = basis.T
    last = last.reshape(folds * side, folds * LANES)
    order = [plan.share * j + i for j in range(plan.pairs) for i in range(plan.full)]
    order += [plan.share * j + plan.full + i for j in range(plan.pairs) for i in range(plan.rest)]
    columns = [folds * g + j for j in range(folds) for g in range(groups)]
    second = basis[order][:, columns]
    value = eigen(side)
    inverse_side = np.zeros((side, LANES))
    inverse_side[:, :side] = 1.0 / (2.0 + value[order][:, None] + value[None, :])
    lane = np.arange(plan.tiles * LANES).reshape(plan.tiles, 1, LANES)
    owner = np.zeros((plan.pairs, plan.stride, LANES))
    for j in range(plan.pairs):
        parts = []
        for start, size in ((0, plan.full), (plan.full, plan.rest)):
            mode = plan.share * j + start + np.arange(size).reshape(1, size, 1)
            parts.append((value[mode] + value[lane % side]).reshape(plan.tiles * size, LANES))
        owner[j, : plan.block] = np.concatenate(parts)
    return {
        "last": np.stack([split_table(last[a:b, c:d]) for a, b, c, d in bands(plan)]),
        "last_back": np.stack([split_table(last[a:b, c:d].T) for a, b, c, d in bands(plan)]),
        "second": np.stack([stack_table(second), stack_table(second.T)]),
        "modes": np.concatenate([inverse_side, owner.reshape(-1, LANES)]).astype(np.float32),
    }


def halve(value):
    high = value.astype(jnp.bfloat16)
    low = (value - high.astype(jnp.float32)).astype(jnp.bfloat16)
    return high, low


def product(left, right):
    dot = functools.partial(jnp.dot, preferred_element_type=jnp.float32)
    return dot(left[0], right[0]) + (dot(left[0], right[1]) + dot(left[1], right[0]))


def stacked(table, value):
    both = jnp.dot(table, jnp.concatenate(halve(value), axis=0), preferred_element_type=jnp.float32)
    size = both.shape[0] // 2
    return both[:size] + both[size:]


def bands(plan):
    for j in range(0, plan.folds, 2):
        rows = min(2, plan.folds - j)
        begin, end = j * plan.side // LANES, -(-(j + rows) * plan.side // LANES)
        yield begin * LANES, end * LANES, j * LANES, (j + rows) * LANES


def lane_of(shape):
    return lax.broadcasted_iota(jnp.int32, shape, 1)


def moved(ref, field, start, size, distance):
    down, over = distance // LANES, distance % LANES
    here = ref[field, pl.ds(start + down, size), :]
    after = ref[field, pl.ds(start + down + 1, size), :]
    mixed = jnp.where(lane_of(here.shape) >= over, here, after)
    return pltpu.roll(mixed, LANES - over, 1)


def last_index(rows, side):
    row = lax.broadcasted_iota(jnp.int32, (rows, LANES), 0)
    return (row * LANES + lane_of((rows, LANES))) % side


def wrap(ref, field, rows):
    ref[field, pl.ds(0, 8), :] = ref[field, pl.ds(rows, 8), :]
    ref[field, pl.ds(8 + rows, 8), :] = ref[field, pl.ds(8, 8), :]


def projected(links, d):
    def entry(part, i, j):
        return links[((d * 2 + part) * 3 + i) * 3 + j]

    im00, im11, im22 = entry(1, 0, 0), entry(1, 1, 1), entry(1, 2, 2)
    fields = [(im00 + im11 - 2.0 * im22) * (1.0 / 3.0), im00 - im11]
    for i, j in ((0, 1), (0, 2), (1, 2)):
        fields.append(0.5 * (entry(0, i, j) - entry(0, j, i)))
        fields.append(0.5 * (entry(1, i, j) + entry(1, j, i)))
    return fields


def link_copies(links_ref, staged, semaphores):
    copies = []
    for n, d in enumerate((1, 2, 0)):
        for m, (begin, size) in enumerate(((1, 3), (5, 3), (9, 9))):
            place = pl.ds(d * 18 + begin, size)
            copies.append(
                pltpu.make_async_copy(links_ref.at[place], staged.at[place], semaphores.at[n, m])
            )
    return copies


def divergence_kernel(
    plan, index_ref, links_ref, keep_ref, send_ref, ahead_ref, base_ref, staged, second, third, semaphores
):
    rows, side = plan.rows, plan.side
    copies = link_copies(links_ref, staged, semaphores)
    for copy in copies:
        copy.start()
    odd = index_ref[0] % 2
    at_start = last_index(rows, side) == 0
    middle = pl.ds(8, rows)
    for copy in copies[:3]:
        copy.wait()
    for f, value in enumerate(projected(staged, 1)):
        second[f, middle, :] = value
        wrap(second, f, rows)
    diverge = [moved(second, f, 8, rows, -side) - second[f, middle, :] for f in range(8)]
    for copy in copies[3:6]:
        copy.wait()
    for f, value in enumerate(projected(staged, 2)):
        third[f, middle, :] = value
        wrap(third, f, rows)
    for f in range(8):
        beside = jnp.where(
            at_start, moved(third, f, 8, rows, side - 1), moved(third, f, 8, rows, -1)
        )
        diverge[f] = diverge[f] + (beside - third[f, middle, :])
        second[f, middle, :] = diverge[f]
    for copy in copies[6:]:
        copy.wait()
    direct = projected(staged, 0)
    index = index_ref[0]
    for f in range(8):
        place = pl.ds(f * rows, rows)
        total = second[f, middle, :] - direct[f]
        ahead_ref[place, :] = jnp.where(index == plan.count_x - 1, direct[f], total)
        base_ref[place, :] = jnp.where(index == 0, total, direct[f])
    for f in range(4):
        for part in range(2):
            place = pl.ds((part * 4 + f) * rows, rows)
            low, high = direct[f], direct[4 + f]
            if part == 0:
                low, high = second[f, middle, :] - low, second[4 + f, middle, :] - high
            keep_ref[place, :] = jnp.where(odd == 0, low, high)
            send_ref[place, :] = jnp.where(odd == 0, high, low)


def forward_kernel(
    plan, index_ref, keep_ref, got_ref, last_ref, second_ref, modes_ref, sent_ref, odd_ref, drift_ref, dense
):
    rows, groups, folds, side = plan.rows, plan.groups, plan.folds, plan.side
    odd = index_ref[0] % 2
    quad = 4 * rows
    square = jnp.zeros((rows, LANES), jnp.float32)
    for f in range(4):
        own_d, own_a = keep_ref[pl.ds(f * rows, rows), :], keep_ref[pl.ds(quad + f * rows, rows), :]
        got_d, got_a = got_ref[pl.ds(f * rows, rows), :], got_ref[pl.ds(quad + f * rows, rows), :]
        even_d, odd_d = jnp.where(odd == 0, own_d, got_d), jnp.where(odd == 0, got_d, own_d)
        even_a, odd_a = jnp.where(odd == 0, own_a, got_a), jnp.where(odd == 0, got_a, own_a)
        whole = odd_d + even_a
        for q, value in enumerate((even_d, whole, odd_a)):
            dense[pl.ds((q * 4 + f) * rows, rows), :] = value
        square = square + whole * whole * jnp.where(odd == 0, drift_weights[f], drift_weights[4 + f])
    drift_ref[...] = sum_tiles(square)
    count = 12 * groups
    wide = jnp.concatenate(
        [dense[pl.ds(s, count, stride=plan.wide), :] for s in range(plan.wide)], axis=1
    )
    high, low = halve(wide)
    waves = jnp.concatenate(
        [
            product(
                (high[:, begin:end], low[:, begin:end]),
                (last_ref[n, 0], last_ref[n, 1]),
            )
            for n, (begin, end, _, _) in enumerate(bands(plan))
        ],
        axis=1,
    )
    columns = []
    for pf in range(12):
        part = waves[pf * groups : (pf + 1) * groups]
        columns.append(
            jnp.concatenate([part[:, j * LANES : (j + 1) * LANES] for j in range(folds)], axis=0)
        )
    modes = stacked(second_ref[0], jnp.concatenate(columns, axis=1))
    inverse = modes_ref[:side]
    full, rest, pairs, tiles = plan.full, plan.rest, plan.pairs, plan.tiles
    lane = lane_of((side, LANES))
    zero = (lane == 0) & (lax.broadcasted_iota(jnp.int32, (side, LANES), 0) == 0)
    even, between, after = [
        [modes[:, (q * 4 + f) * LANES : (q * 4 + f + 1) * LANES] for f in range(4)] for q in range(3)
    ]
    shared = [value * inverse for value in between]
    for f in range(4):
        odd_ref[:, f * LANES : (f + 1) * LANES] = gain * shared[f]
    below = [even[f] + shared[f] for f in range(4)]
    above = [jnp.where(zero, between[f], after[f] + shared[f]) for f in range(4)]
    for q, fields in enumerate((below, above)):
        for t, value in enumerate(pack(fields, lane, side)):
            at = q * tiles + t
            for j in range(pairs):
                if full:
                    sent_ref[plan.place[j], pl.ds(at * full, full), :] = value[j * full : (j + 1) * full]
                if rest:
                    begin = pairs * full + j * rest
                    sent_ref[plan.place[j], pl.ds(2 * tiles * full + at * rest, rest), :] = value[
                        begin : begin + rest
                    ]
    spare = plan.sent - 2 * plan.block
    if spare:
        sent_ref[:, pl.ds(2 * plan.block, spare), :] = jnp.zeros((pairs, spare, LANES), jnp.float32)


def sum_tiles(value):
    total = value[:8]
    for i in range(1, value.shape[0] // 8):
        total = total + value[i * 8 : (i + 1) * 8]
    return total


def pack(fields, lane, side):
    rolled = [
        value if f * side % LANES == 0 else pltpu.roll(value, f * side % LANES, 1)
        for f, value in enumerate(fields)
    ]
    packed = []
    for t in range(4 * side // LANES):
        value = None
        for f in range(4):
            if f * side < (t + 1) * LANES and (f + 1) * side > t * LANES:
                value = rolled[f] if value is None else jnp.where(lane >= f * side - t * LANES, rolled[f], value)
        packed.append(value)
    return packed


def unpack(packed, lane, side):
    fields = []
    for f in range(4):
        begin = f * side // LANES
        end = ((f + 1) * side - 1) // LANES
        offset = f * side % LANES
        value = packed[begin]
        if end != begin:
            value = jnp.where(lane >= offset, packed[begin], packed[end])
        if offset:
            value = pltpu.roll(value, LANES - offset, 1)
        fields.append(jnp.where(lane < side, value, 0.0))
    return fields


def drift_kernel(plan, index_ref, odd_ref, beside_ref, base_ref, drift_ref):
    rows, count_x = plan.rows, plan.count_x
    index = index_ref[0]
    square = jnp.zeros((rows, LANES), jnp.float32)
    for f in range(8):
        place = pl.ds(f * rows, rows)
        value = beside_ref[place, :] + base_ref[place, :]
        square = square + value * value * drift_weights[f]
    complete = (index == 0) | ((index % 2 == 1) & (index < count_x - 1))
    drift_ref[...] = odd_ref[...] + jnp.where(complete, sum_tiles(square), 0.0)


def filter_kernel(plan, index_ref, got_ref, modes_ref, drift_ref, back_ref):
    pairs, tiles, count_x = plan.pairs, plan.tiles, plan.count_x
    half = pairs // 2
    drift = drift_ref[...]
    for part, (size, first) in enumerate(((plan.full, 0), (plan.rest, 2 * tiles * plan.full))):
        if not size:
            continue
        length = tiles * size
        own = pl.multiple_of(plan.side + index_ref[0] // 2 * plan.stride, 8)
        value = modes_ref[pl.ds(own, plan.stride), :][part * tiles * plan.full :][:length]
        low, high = pl.ds(first, length), pl.ds(first + length, length)
        inside = value > 0
        below = [got_ref[plan.place[p], low, :] for p in range(pairs)]
        above = [got_ref[plan.place[p], high, :] for p in range(pairs)]
        rhs = [
            below[p] + jnp.where(inside, above[(p - 1) % pairs], -below[(p - 1) % pairs])
            for p in range(pairs)
        ]
        plus = [rhs[d] + rhs[pairs - d] for d in range(1, half)]
        minus = [rhs[d] - rhs[pairs - d] for d in range(1, half)]
        cosines, sines = [], []
        for k in range(half + 1):
            total = rhs[0] + rhs[half] if k % 2 == 0 else rhs[0] - rhs[half]
            for d in range(1, half):
                total = total + plus[d - 1] * math.cos(2 * math.pi * (k * d % pairs) / pairs)
            root = 4.0 * math.sin(math.pi * k / count_x) ** 2
            split = (value + root) * (value + (4.0 - root))
            scale = gain / pairs * (1.0 if k in (0, half) else 2.0)
            if k == 0:
                factor = jnp.where(inside, scale * (2.0 + value) / jnp.where(inside, split, 1.0), 0.0)
                whole = above[0]
                for p in range(1, pairs):
                    whole = whole + above[p]
                mean = jnp.where(inside, 0.0, whole * (-0.25 * gain / pairs))
                cosines.append(total * factor + mean)
            else:
                factor = scale * (2.0 + value) / split
                cosines.append(total * factor)
                if k < half:
                    wave = jnp.zeros_like(value)
                    for d in range(1, half):
                        wave = wave + minus[d - 1] * math.sin(2 * math.pi * (k * d % pairs) / pairs)
                    sines.append(wave * factor)
        results = [None] * pairs
        for d in range(half + 1):
            even = cosines[0]
            for k in range(1, half + 1):
                even = even + cosines[k] * math.cos(2 * math.pi * (k * d % pairs) / pairs)
            if d in (0, half):
                results[d] = even
            else:
                wave = jnp.zeros_like(value)
                for k in range(1, half):
                    wave = wave + sines[k - 1] * math.sin(2 * math.pi * (k * d % pairs) / pairs)
                results[d] = even + wave
                results[pairs - d] = even - wave
        for p in range(pairs):
            back_ref[plan.place[p], low, :] = results[p]
            back_ref[plan.place[p], high, :] = results[(p + 1) % pairs]
    for p in range(pairs):
        back_ref[p, pl.ds(2 * plan.block, 8), :] = drift


def backward_kernel(
    plan, index_ref, got_ref, odd_ref, last_ref, second_ref, modes_ref, keep_ref, send_ref, packed, dense
):
    rows, groups, folds, side = plan.rows, plan.groups, plan.folds, plan.side
    full, rest, pairs, tiles = plan.full, plan.rest, plan.pairs, plan.tiles
    odd = index_ref[0] % 2
    for q in range(2):
        for t in range(tiles):
            at = q * tiles + t
            for j in range(pairs):
                if full:
                    packed[at, pl.ds(j * full, full), :] = got_ref[plan.place[j], pl.ds(at * full, full), :]
                if rest:
                    packed[at, pl.ds(pairs * full + j * rest, rest), :] = got_ref[
                        plan.place[j], pl.ds(2 * tiles * full + at * rest, rest), :
                    ]
    lane = lane_of((side, LANES))
    inverse = modes_ref[:side]
    even, after = [
        unpack([packed[q * tiles + t] for t in range(tiles)], lane, side) for q in range(2)
    ]
    between = [
        odd_ref[:, f * LANES : (f + 1) * LANES] + (even[f] + after[f]) * inverse for f in range(4)
    ]
    waves = stacked(second_ref[1], jnp.concatenate(even + between + after, axis=1))
    blocks = []
    for pf in range(12):
        part = waves[:, pf * LANES : (pf + 1) * LANES]
        blocks.append(
            jnp.concatenate([part[j * groups : (j + 1) * groups] for j in range(folds)], axis=1)
        )
    high, low = halve(jnp.concatenate(blocks, axis=0))
    wide = [None] * plan.wide
    for n, (begin, end, first, last) in enumerate(bands(plan)):
        part = product(
            (high[:, first:last], low[:, first:last]), (last_ref[n, 0], last_ref[n, 1])
        )
        for s in range(begin // LANES, end // LANES):
            tile = part[:, s * LANES - begin : (s + 1) * LANES - begin]
            wide[s] = tile if wide[s] is None else wide[s] + tile
    count = 12 * groups
    for s in range(plan.wide):
        dense[pl.ds(s, count, stride=plan.wide), :] = wide[s]
    quad = 4 * rows
    low, middle, high = [dense[pl.ds(q * quad, quad), :] for q in range(3)]
    keep_ref[pl.ds(0, quad), :] = jnp.where(odd == 0, low, middle)
    keep_ref[pl.ds(quad, quad), :] = jnp.where(odd == 0, middle, high)
    send_ref[pl.ds(0, quad), :] = jnp.where(odd == 0, middle, low)
    send_ref[pl.ds(quad, quad), :] = jnp.where(odd == 0, high, middle)
    drift = got_ref[0, pl.ds(2 * plan.block, 8), :]
    for j in range(1, pairs):
        drift = drift + got_ref[j, pl.ds(2 * plan.block, 8), :]
    keep_ref[pl.ds(2 * quad, 8), :] = drift
    send_ref[pl.ds(2 * quad, 8), :] = drift


def times(left, right):
    return (left[0] * right[0] - left[1] * right[1], left[0] * right[1] + left[1] * right[0])


def times_conj(left, right):
    return (left[0] * right[0] + left[1] * right[1], left[1] * right[0] - left[0] * right[1])


def rotation(fields):
    both, apart = fields[0], fields[1]
    a, b, e = 0.5 * (both + apart), 0.5 * (both - apart), -both
    u, v, w = (fields[2], fields[3]), (fields[4], fields[5]), (fields[6], fields[7])
    square = [x[0] * x[0] + x[1] * x[1] for x in (u, v, w)]
    a00, a11, a22 = square[2] - b * e, square[1] - a * e, square[0] - a * b
    vw, uw, vu = times_conj(v, w), times(u, w), times_conj(v, u)
    a01 = (e * u[1] - vw[0], -(e * u[0]) - vw[1])
    a02 = (uw[0] + b * v[1], uw[1] - b * v[0])
    a12 = (a * w[1] - vu[0], -(a * w[0]) - vu[1])
    turn = a * a00 + times_conj(u, a01)[1] + times_conj(v, a02)[1]
    real = 1.0 + (a00 + a11 + a22)
    scale = 2.0 / (real * real + turn * turn)
    factor = (real * scale, turn * scale)
    entries = [[None] * 3 for _ in range(3)]
    for i, (up, imag) in enumerate(((a00, a), (a11, b), (a22, e))):
        value = times((1.0 + up, imag), factor)
        entries[i][i] = (value[0] - 1.0, value[1])
    for (i, j), up, off in (((0, 1), a01, u), ((0, 2), a02, v), ((1, 2), a12, w)):
        entries[i][j] = times((up[0] + off[0], up[1] + off[1]), factor)
        entries[j][i] = times((up[0] - off[0], off[1] - up[1]), factor)
    return [entries[i][j][part] for part in range(2) for i in range(3) for j in range(3)]


def update_kernel(
    plan, unroll, index_ref, keep_ref, got_ref, links_ref, fixed_ref, drift_ref, here, along, staged, semaphores
):
    rows, side = plan.rows, plan.side
    quad = 4 * rows
    odd = index_ref[0] % 2

    def turn(i, _):
        begin = pl.multiple_of(i * 8, 8)
        for q, lead in ((0, 8), (1, 0)):
            fields = [None] * 8
            for f in range(4):
                place = pl.ds(pl.multiple_of(q * quad + f * rows + begin, 8), 8)
                own, other = keep_ref[place, :], got_ref[place, :]
                fields[f] = jnp.where(odd == 0, own, other)
                fields[4 + f] = jnp.where(odd == 0, other, own)
            for n, value in enumerate(rotation(fields)):
                if q == 0:
                    here[n, pl.ds(begin + lead, 8), :] = value
                else:
                    along[0, n, pl.ds(begin, 8), :] = value
        return 0

    lax.fori_loop(0, rows // 8, turn, 0, unroll=unroll[0])

    def update(d, i):
        begin = pl.multiple_of(i * 8, 8)

        def matrix(read):
            value = [read(n) for n in range(18)]
            return [[(value[3 * r + c], value[9 + 3 * r + c]) for c in range(3)] for r in range(3)]

        own = matrix(lambda n: here[n, pl.ds(begin + 8, 8), :])
        links = matrix(lambda n: links_ref[d * 18 + n, pl.ds(begin, 8), :])
        ahead = matrix(lambda n: along[d, n, pl.ds(begin, 8), :])
        for r in range(3):
            line = [
                add(times(own[r][0], links[0][c]), times(own[r][1], links[1][c]), times(own[r][2], links[2][c]))
                for c in range(3)
            ]
            for c in range(3):
                value = add(*[times_conj(line[k], ahead[c][k]) for k in range(3)])
                for part in range(2):
                    staged[d * 18 + part * 9 + r * 3 + c, pl.ds(begin, 8), :] = value[part]

    tiles = rows // 8
    copies = []

    def write(place, rows_place, n):
        copy = pltpu.make_async_copy(
            staged.at[place, rows_place], fixed_ref.at[place, rows_place], semaphores.at[n]
        )
        copy.start()
        copies.append(copy)

    for d in (1, 2, 0):
        if d == 1:
            for n in range(18):
                wrap(here, n, rows)
                along[1, n] = moved(here, n, 8, rows, side)
        if d == 2:
            at_end = last_index(rows, side) == side - 1
            for n in range(18):
                along[2, n] = jnp.where(
                    at_end, moved(here, n, 8, rows, 1 - side), moved(here, n, 8, rows, 1)
                )
        chunks = 1 if d else 3
        for m in range(chunks):
            part = tiles // chunks

            def step(i, _, d=d):
                update(d, i)
                return 0

            lax.fori_loop(m * part, (m + 1) * part, step, 0, unroll=unroll[1])
            write(pl.ds(d * 18, 18), pl.ds(m * part * 8, part * 8), len(copies))
    total = keep_ref[pl.ds(2 * quad, 8), :] + got_ref[pl.ds(2 * quad, 8), :]
    drift_ref[0] = jnp.sum(total) * (1.0 / (9.0 * plan.count_x * plan.cells))
    for copy in copies:
        copy.wait()


def add(first, second, third):
    return (first[0] + second[0] + third[0], first[1] + second[1] + third[1])


def whole_spec():
    return pl.BlockSpec(memory_space=pltpu.VMEM)


def scalar_spec():
    return pl.BlockSpec(memory_space=pltpu.SMEM)


def shape_of(*shape):
    return jax.ShapeDtypeStruct(shape, jnp.float32)


def local(gauge_links):
    count_x = lax.axis_size("gx")
    plan = Plan(count_x, SIDE)
    rows, pairs = plan.rows, plan.pairs
    table = tables(plan)
    index = lax.axis_index("gx").astype(jnp.int32).reshape(1)
    links = gauge_links.reshape(54, rows, LANES)
    quads = 8 * rows
    swap = [(i, i ^ 1) for i in range(count_x)]
    halo = [(2 * p, 2 * p - 1) for p in range(1, pairs)] + [(count_x - 1, 0)]
    same_core = [[c + 2 * p for p in sorted(range(pairs), key=plan.place.__getitem__)] for c in range(2)]

    keep, send, ahead, base = pl.pallas_call(
        functools.partial(divergence_kernel, plan),
        out_shape=(shape_of(quads, LANES),) * 4,
        in_specs=[scalar_spec(), pl.BlockSpec(memory_space=pltpu.HBM)],
        out_specs=(whole_spec(),) * 4,
        scratch_shapes=[
            pltpu.VMEM((54, rows, LANES), jnp.float32),
            pltpu.VMEM((8, rows + 16, LANES), jnp.float32),
            pltpu.VMEM((8, rows + 16, LANES), jnp.float32),
            pltpu.SemaphoreType.DMA((3, 3)),
        ],
        compiler_params=params(),
        name="divergence",
    )(index, pltpu.with_memory_space_constraint(links, pltpu.HBM))
    got = lax.ppermute(send, "gx", swap)
    beside = lax.ppermute(ahead, "gx", halo)
    sent, odd_part, odd_drift = pl.pallas_call(
        functools.partial(forward_kernel, plan),
        out_shape=(
            shape_of(pairs, plan.sent, LANES),
            shape_of(SIDE, 4 * LANES),
            shape_of(8, LANES),
        ),
        in_specs=[scalar_spec()] + [whole_spec()] * 5,
        out_specs=(whole_spec(),) * 3,
        scratch_shapes=[pltpu.VMEM((12 * rows, LANES), jnp.float32)],
        compiler_params=params(),
        name="forward",
    )(index, keep, got, table["last"], table["second"], table["modes"])
    arrived = lax.all_to_all(
        sent, "gx", split_axis=0, concat_axis=0, tiled=True, axis_index_groups=same_core
    )
    drift_part = pl.pallas_call(
        functools.partial(drift_kernel, plan),
        out_shape=shape_of(8, LANES),
        in_specs=[scalar_spec()] + [whole_spec()] * 3,
        out_specs=whole_spec(),
        compiler_params=params(),
        cost_estimate=pl.CostEstimate(flops=5 * 10**10, bytes_accessed=5 * 10**7, transcendentals=0),
        name="drift",
    )(index, odd_drift, beside, base)
    back = pl.pallas_call(
        functools.partial(filter_kernel, plan),
        out_shape=shape_of(pairs, plan.returned, LANES),
        in_specs=[scalar_spec()] + [whole_spec()] * 3,
        out_specs=whole_spec(),
        compiler_params=params(),
        name="filter",
    )(index, arrived, table["modes"], drift_part)
    returned = lax.all_to_all(
        back, "gx", split_axis=0, concat_axis=0, tiled=True, axis_index_groups=same_core
    )
    keep, send = pl.pallas_call(
        functools.partial(backward_kernel, plan),
        out_shape=(shape_of(quads + 8, LANES), shape_of(quads + 8, LANES)),
        in_specs=[scalar_spec()] + [whole_spec()] * 5,
        out_specs=(whole_spec(), whole_spec()),
        scratch_shapes=[
            pltpu.VMEM((2 * plan.tiles, SIDE, LANES), jnp.float32),
            pltpu.VMEM((12 * rows, LANES), jnp.float32),
        ],
        compiler_params=params(),
        name="backward",
    )(index, returned, odd_part, table["last_back"], table["second"], table["modes"])
    got = lax.ppermute(send, "gx", swap)
    fixed, drift = pl.pallas_call(
        functools.partial(update_kernel, plan, (3, 3)),
        out_shape=(shape_of(54, rows, LANES), shape_of(1)),
        in_specs=[scalar_spec()] + [whole_spec()] * 3,
        out_specs=(pl.BlockSpec(memory_space=pltpu.HBM), scalar_spec()),
        scratch_shapes=[
            pltpu.VMEM((18, rows + 16, LANES), jnp.float32),
            pltpu.VMEM((3, 18, rows, LANES), jnp.float32),
            pltpu.VMEM((54, rows, LANES), jnp.float32),
            pltpu.SemaphoreType.DMA((5,)),
        ],
        compiler_params=params(),
        name="update",
    )(index, keep, got, links)
    return fixed.reshape(gauge_links.shape), drift


def solution(mesh):
    in_specs = (P(None, None, None, None, ("ta", "gx"), None),)
    out_specs = (P(None, None, None, None, ("ta", "gx"), None), P("ta"))
    return jax.shard_map(local, mesh=mesh, in_specs=in_specs, out_specs=out_specs, check_vma=False)
```

```python
import functools
import math

import jax
import jax.numpy as jnp
import numpy as np
from jax import lax
from jax.experimental import pallas as pl
from jax.experimental.pallas import tpu as pltpu
from jax.sharding import PartitionSpec as P

SIDE = 96
LANES = 128

step_size = 0.08
peak_square = 12.0
gain = 0.5 * step_size * peak_square

params = functools.partial(pltpu.CompilerParams, vmem_limit_bytes=48 * 1024 * 1024)
drift_weights = (1.5, 0.5, 2.0, 2.0, 2.0, 2.0, 2.0, 2.0)


class Plan:
    def __init__(self, count_x, side):
        self.count_x, self.side = count_x, side
        self.cells = side * side
        self.rows = self.cells // LANES
        self.period = side * LANES // math.gcd(side, LANES)
        self.wide = self.period // LANES
        self.folds = self.period // side
        self.groups = self.cells // self.period
        self.pairs = count_x // 2
        self.share = side // self.pairs
        self.full = self.share // 8 * 8
        self.rest = self.share - self.full
        self.tiles = 4 * side // LANES
        self.block = self.tiles * self.share
        self.stride = -(-self.block // 8) * 8
        self.sent = -(-2 * self.block // 8) * 8
        self.place = [(p + self.pairs // 2) % self.pairs for p in range(self.pairs)]
        self.back_place = [(p + self.pairs // 2 - 1) % self.pairs for p in range(self.pairs)]
        self.returned = -(-(2 * self.block + 8) // 8) * 8


def fourier(length):
    site = np.arange(length)
    basis = np.zeros((length, length))
    for k in range(length):
        angle = 2.0 * math.pi * (k * site % length) / length
        if k == 0 or 2 * k == length:
            basis[k] = np.cos(angle) / math.sqrt(length)
        elif 2 * k < length:
            basis[k] = np.cos(angle) * math.sqrt(2.0 / length)
        else:
            basis[k] = np.sin(angle) * math.sqrt(2.0 / length)
    return basis


def eigen(length):
    return 4.0 * np.sin(math.pi * np.arange(length) / length) ** 2


def split_table(table):
    high = table.astype(jnp.bfloat16)
    low = (table - high.astype(np.float64)).astype(jnp.bfloat16)
    return np.stack([high, low])


def stack_table(table):
    high, low = split_table(table)
    return np.block([[high, high], [low, np.zeros_like(low)]])


def tables(plan):
    side, folds, groups = plan.side, plan.folds, plan.groups
    basis = fourier(side)
    last = np.zeros((folds, side, folds, LANES))
    for j in range(folds):
        last[j, :, j, :side] = basis.T
    last = last.reshape(folds * side, folds * LANES)
    order = [plan.share * j + i for j in range(plan.pairs) for i in range(plan.full)]
    order += [plan.share * j + plan.full + i for j in range(plan.pairs) for i in range(plan.rest)]
    columns = [folds * g + j for j in range(folds) for g in range(groups)]
    second = basis[order][:, columns]
    value = eigen(side)
    inverse_side = np.zeros((side, LANES))
    inverse_side[:, :side] = 1.0 / (2.0 + value[order][:, None] + value[None, :])
    lane = np.arange(plan.tiles * LANES).reshape(plan.tiles, 1, LANES)
    owner = np.zeros((plan.pairs, plan.stride, LANES))
    for j in range(plan.pairs):
        parts = []
        for start, size in ((0, plan.full), (plan.full, plan.rest)):
            mode = plan.share * j + start + np.arange(size).reshape(1, size, 1)
            parts.append((value[mode] + value[lane % side]).reshape(plan.tiles * size, LANES))
        owner[j, : plan.block] = np.concatenate(parts)
    return {
        "last": np.stack([split_table(last[a:b, c:d]) for a, b, c, d in bands(plan)]),
        "last_back": np.stack([split_table(last[a:b, c:d].T) for a, b, c, d in bands(plan)]),
        "second": np.stack([stack_table(second), stack_table(second.T)]),
        "modes": np.concatenate([inverse_side, owner.reshape(-1, LANES)]).astype(np.float32),
    }


def halve(value):
    high = value.astype(jnp.bfloat16)
    low = (value - high.astype(jnp.float32)).astype(jnp.bfloat16)
    return high, low


def product(left, right):
    dot = functools.partial(jnp.dot, preferred_element_type=jnp.float32)
    return dot(left[0], right[0]) + (dot(left[0], right[1]) + dot(left[1], right[0]))


def stacked(table, value):
    both = jnp.dot(table, jnp.concatenate(halve(value), axis=0), preferred_element_type=jnp.float32)
    size = both.shape[0] // 2
    return both[:size] + both[size:]


def bands(plan):
    for j in range(0, plan.folds, 2):
        rows = min(2, plan.folds - j)
        begin, end = j * plan.side // LANES, -(-(j + rows) * plan.side // LANES)
        yield begin * LANES, end * LANES, j * LANES, (j + rows) * LANES


def lane_of(shape):
    return lax.broadcasted_iota(jnp.int32, shape, 1)


def moved(ref, field, start, size, distance):
    down, over = distance // LANES, distance % LANES
    here = ref[field, pl.ds(start + down, size), :]
    after = ref[field, pl.ds(start + down + 1, size), :]
    mixed = jnp.where(lane_of(here.shape) >= over, here, after)
    return pltpu.roll(mixed, LANES - over, 1)


def last_index(rows, side):
    row = lax.broadcasted_iota(jnp.int32, (rows, LANES), 0)
    return (row * LANES + lane_of((rows, LANES))) % side


def wrap(ref, field, rows):
    ref[field, pl.ds(0, 8), :] = ref[field, pl.ds(rows, 8), :]
    ref[field, pl.ds(8 + rows, 8), :] = ref[field, pl.ds(8, 8), :]


def projected(links, d):
    def entry(part, i, j):
        return links[((d * 2 + part) * 3 + i) * 3 + j]

    im00, im11, im22 = entry(1, 0, 0), entry(1, 1, 1), entry(1, 2, 2)
    fields = [(im00 + im11 - 2.0 * im22) * (1.0 / 3.0), im00 - im11]
    for i, j in ((0, 1), (0, 2), (1, 2)):
        fields.append(0.5 * (entry(0, i, j) - entry(0, j, i)))
        fields.append(0.5 * (entry(1, i, j) + entry(1, j, i)))
    return fields


def link_copies(links_ref, staged, semaphores):
    copies = []
    for n, d in enumerate((1, 2, 0)):
        for m, (begin, size) in enumerate(((1, 3), (5, 3), (9, 9))):
            place = pl.ds(d * 18 + begin, size)
            copies.append(
                pltpu.make_async_copy(links_ref.at[place], staged.at[place], semaphores.at[n, m])
            )
    return copies


def divergence_kernel(
    plan, index_ref, links_ref, keep_ref, send_ref, ahead_ref, staged, second, third, semaphores
):
    rows, side = plan.rows, plan.side
    copies = link_copies(links_ref, staged, semaphores)
    for copy in copies:
        copy.start()
    odd = index_ref[0] % 2
    at_start = last_index(rows, side) == 0
    middle = pl.ds(8, rows)
    for copy in copies[:3]:
        copy.wait()
    for f, value in enumerate(projected(staged, 1)):
        second[f, middle, :] = value
        wrap(second, f, rows)
    diverge = [moved(second, f, 8, rows, -side) - second[f, middle, :] for f in range(8)]
    for copy in copies[3:6]:
        copy.wait()
    for f, value in enumerate(projected(staged, 2)):
        third[f, middle, :] = value
        wrap(third, f, rows)
    for f in range(8):
        beside = jnp.where(
            at_start, moved(third, f, 8, rows, side - 1), moved(third, f, 8, rows, -1)
        )
        diverge[f] = diverge[f] + (beside - third[f, middle, :])
        second[f, middle, :] = diverge[f]
    for copy in copies[6:]:
        copy.wait()
    direct = projected(staged, 0)
    index = index_ref[0]
    for f in range(8):
        place = pl.ds(f * rows, rows)
        total = second[f, middle, :] - direct[f]
        ahead_ref[place, :] = jnp.where(index == plan.count_x - 1, direct[f], total)
    for f in range(4):
        for part in range(2):
            place = pl.ds((part * 4 + f) * rows, rows)
            low, high = direct[f], direct[4 + f]
            if part == 0:
                low, high = second[f, middle, :] - low, second[4 + f, middle, :] - high
            keep_ref[place, :] = jnp.where(odd == 0, low, high)
            send_ref[place, :] = jnp.where(odd == 0, high, low)


def forward_kernel(
    plan, index_ref, keep_ref, got_ref, last_ref, second_ref, modes_ref, sent_ref, odd_ref, drift_ref, dense
):
    rows, groups, folds, side = plan.rows, plan.groups, plan.folds, plan.side
    odd = index_ref[0] % 2
    quad = 4 * rows
    square = jnp.zeros((rows, LANES), jnp.float32)
    for f in range(4):
        own_d, own_a = keep_ref[pl.ds(f * rows, rows), :], keep_ref[pl.ds(quad + f * rows, rows), :]
        got_d, got_a = got_ref[pl.ds(f * rows, rows), :], got_ref[pl.ds(quad + f * rows, rows), :]
        even_d, odd_d = jnp.where(odd == 0, own_d, got_d), jnp.where(odd == 0, got_d, own_d)
        even_a, odd_a = jnp.where(odd == 0, own_a, got_a), jnp.where(odd == 0, got_a, own_a)
        whole = odd_d + even_a
        for q, value in enumerate((even_d, whole, odd_a)):
            dense[pl.ds((q * 4 + f) * rows, rows), :] = value
        square = square + whole * whole * jnp.where(odd == 0, drift_weights[f], drift_weights[4 + f])
    drift_ref[...] = sum_tiles(square)
    count = 12 * groups
    wide = jnp.concatenate(
        [dense[pl.ds(s, count, stride=plan.wide), :] for s in range(plan.wide)], axis=1
    )
    high, low = halve(wide)
    waves = jnp.concatenate(
        [
            product(
                (high[:, begin:end], low[:, begin:end]),
                (last_ref[n, 0], last_ref[n, 1]),
            )
            for n, (begin, end, _, _) in enumerate(bands(plan))
        ],
        axis=1,
    )
    columns = []
    for pf in range(12):
        part = waves[pf * groups : (pf + 1) * groups]
        columns.append(
            jnp.concatenate([part[:, j * LANES : (j + 1) * LANES] for j in range(folds)], axis=0)
        )
    modes = stacked(second_ref[0], jnp.concatenate(columns, axis=1))
    inverse = modes_ref[:side]
    full, rest, pairs, tiles = plan.full, plan.rest, plan.pairs, plan.tiles
    lane = lane_of((side, LANES))
    zero = (lane == 0) & (lax.broadcasted_iota(jnp.int32, (side, LANES), 0) == 0)
    even, between, after = [
        [modes[:, (q * 4 + f) * LANES : (q * 4 + f + 1) * LANES] for f in range(4)] for q in range(3)
    ]
    shared = [value * inverse for value in between]
    for f in range(4):
        odd_ref[:, f * LANES : (f + 1) * LANES] = gain * shared[f]
    below = [even[f] + shared[f] for f in range(4)]
    above = [jnp.where(zero, between[f], after[f] + shared[f]) for f in range(4)]
    for q, fields in enumerate((below, above)):
        for t, value in enumerate(pack(fields, lane, side)):
            at = q * tiles + t
            for j in range(pairs):
                if full:
                    sent_ref[plan.place[j], pl.ds(at * full, full), :] = value[j * full : (j + 1) * full]
                if rest:
                    begin = pairs * full + j * rest
                    sent_ref[plan.place[j], pl.ds(2 * tiles * full + at * rest, rest), :] = value[
                        begin : begin + rest
                    ]
    spare = plan.sent - 2 * plan.block
    if spare:
        sent_ref[:, pl.ds(2 * plan.block, spare), :] = jnp.zeros((pairs, spare, LANES), jnp.float32)


def sum_tiles(value):
    total = value[:8]
    for i in range(1, value.shape[0] // 8):
        total = total + value[i * 8 : (i + 1) * 8]
    return total


def pack(fields, lane, side):
    rolled = [
        value if f * side % LANES == 0 else pltpu.roll(value, f * side % LANES, 1)
        for f, value in enumerate(fields)
    ]
    packed = []
    for t in range(4 * side // LANES):
        value = None
        for f in range(4):
            if f * side < (t + 1) * LANES and (f + 1) * side > t * LANES:
                value = rolled[f] if value is None else jnp.where(lane >= f * side - t * LANES, rolled[f], value)
        packed.append(value)
    return packed


def unpack(packed, lane, side):
    fields = []
    for f in range(4):
        begin = f * side // LANES
        end = ((f + 1) * side - 1) // LANES
        offset = f * side % LANES
        value = packed[begin]
        if end != begin:
            value = jnp.where(lane >= offset, packed[begin], packed[end])
        if offset:
            value = pltpu.roll(value, LANES - offset, 1)
        fields.append(jnp.where(lane < side, value, 0.0))
    return fields


def drift_kernel(plan, index_ref, odd_ref, beside_ref, keep_ref, send_ref, drift_ref):
    rows, count_x = plan.rows, plan.count_x
    index = index_ref[0]
    square = jnp.zeros((rows, LANES), jnp.float32)
    part = jnp.where(index == 0, 0, 4 * rows)
    for f in range(4):
        place = pl.ds(pl.multiple_of(part + f * rows, 8), rows)
        own, other = keep_ref[place, :], send_ref[place, :]
        low, high = jnp.where(index % 2 == 0, own, other), jnp.where(index % 2 == 0, other, own)
        for n, value in ((f, low), (4 + f, high)):
            total = beside_ref[pl.ds(n * rows, rows), :] + value
            square = square + total * total * drift_weights[n]
    complete = (index == 0) | ((index % 2 == 1) & (index < count_x - 1))
    drift_ref[...] = odd_ref[...] + jnp.where(complete, sum_tiles(square), 0.0)


def filter_kernel(plan, index_ref, got_ref, modes_ref, drift_ref, back_ref):
    pairs, tiles, count_x = plan.pairs, plan.tiles, plan.count_x
    half = pairs // 2
    drift = drift_ref[...]
    for part, (size, first) in enumerate(((plan.full, 0), (plan.rest, 2 * tiles * plan.full))):
        if not size:
            continue
        length = tiles * size
        own = pl.multiple_of(plan.side + index_ref[0] // 2 * plan.stride, 8)
        value = modes_ref[pl.ds(own, plan.stride), :][part * tiles * plan.full :][:length]
        low, high = pl.ds(first, length), pl.ds(first + length, length)
        inside = value > 0
        below = [got_ref[plan.place[p], low, :] for p in range(pairs)]
        above = [got_ref[plan.place[p], high, :] for p in range(pairs)]
        rhs = [
            below[p] + jnp.where(inside, above[(p - 1) % pairs], -below[(p - 1) % pairs])
            for p in range(pairs)
        ]
        plus = [rhs[d] + rhs[pairs - d] for d in range(1, half)]
        minus = [rhs[d] - rhs[pairs - d] for d in range(1, half)]
        cosines, sines = [], []
        for k in range(half + 1):
            total = rhs[0] + rhs[half] if k % 2 == 0 else rhs[0] - rhs[half]
            for d in range(1, half):
                total = total + plus[d - 1] * math.cos(2 * math.pi * (k * d % pairs) / pairs)
            root = 4.0 * math.sin(math.pi * k / count_x) ** 2
            split = (value + root) * (value + (4.0 - root))
            scale = gain / pairs * (1.0 if k in (0, half) else 2.0)
            if k == 0:
                factor = jnp.where(inside, scale * (2.0 + value) / jnp.where(inside, split, 1.0), 0.0)
                whole = above[0]
                for p in range(1, pairs):
                    whole = whole + above[p]
                mean = jnp.where(inside, 0.0, whole * (-0.25 * gain / pairs))
                cosines.append(total * factor + mean)
            else:
                factor = scale * (2.0 + value) / split
                cosines.append(total * factor)
                if k < half:
                    wave = jnp.zeros_like(value)
                    for d in range(1, half):
                        wave = wave + minus[d - 1] * math.sin(2 * math.pi * (k * d % pairs) / pairs)
                    sines.append(wave * factor)
        results = [None] * pairs
        for d in range(half + 1):
            even = cosines[0]
            for k in range(1, half + 1):
                even = even + cosines[k] * math.cos(2 * math.pi * (k * d % pairs) / pairs)
            if d in (0, half):
                results[d] = even
            else:
                wave = jnp.zeros_like(value)
                for k in range(1, half):
                    wave = wave + sines[k - 1] * math.sin(2 * math.pi * (k * d % pairs) / pairs)
                results[d] = even + wave
                results[pairs - d] = even - wave
        for p in range(pairs):
            back_ref[plan.back_place[p], low, :] = results[p]
            back_ref[plan.back_place[p], high, :] = results[(p + 1) % pairs]
    for p in range(pairs):
        back_ref[p, pl.ds(2 * plan.block, 8), :] = drift


def backward_kernel(
    plan, index_ref, got_ref, odd_ref, last_ref, second_ref, modes_ref, keep_ref, send_ref, packed, dense
):
    rows, groups, folds, side = plan.rows, plan.groups, plan.folds, plan.side
    full, rest, pairs, tiles = plan.full, plan.rest, plan.pairs, plan.tiles
    odd = index_ref[0] % 2
    for q in range(2):
        for t in range(tiles):
            at = q * tiles + t
            for j in range(pairs):
                if full:
                    packed[at, pl.ds(j * full, full), :] = got_ref[plan.back_place[j], pl.ds(at * full, full), :]
                if rest:
                    packed[at, pl.ds(pairs * full + j * rest, rest), :] = got_ref[
                        plan.back_place[j], pl.ds(2 * tiles * full + at * rest, rest), :
                    ]
    lane = lane_of((side, LANES))
    inverse = modes_ref[:side]
    even, after = [
        unpack([packed[q * tiles + t] for t in range(tiles)], lane, side) for q in range(2)
    ]
    between = [
        odd_ref[:, f * LANES : (f + 1) * LANES] + (even[f] + after[f]) * inverse for f in range(4)
    ]
    waves = stacked(second_ref[1], jnp.concatenate(even + between + after, axis=1))
    blocks = []
    for pf in range(12):
        part = waves[:, pf * LANES : (pf + 1) * LANES]
        blocks.append(
            jnp.concatenate([part[j * groups : (j + 1) * groups] for j in range(folds)], axis=1)
        )
    high, low = halve(jnp.concatenate(blocks, axis=0))
    wide = [None] * plan.wide
    for n, (begin, end, first, last) in enumerate(bands(plan)):
        part = product(
            (high[:, first:last], low[:, first:last]), (last_ref[n, 0], last_ref[n, 1])
        )
        for s in range(begin // LANES, end // LANES):
            tile = part[:, s * LANES - begin : (s + 1) * LANES - begin]
            wide[s] = tile if wide[s] is None else wide[s] + tile
    count = 12 * groups
    for s in range(plan.wide):
        dense[pl.ds(s, count, stride=plan.wide), :] = wide[s]
    quad = 4 * rows
    low, middle, high = [dense[pl.ds(q * quad, quad), :] for q in range(3)]
    keep_ref[pl.ds(0, quad), :] = jnp.where(odd == 0, low, middle)
    keep_ref[pl.ds(quad, quad), :] = jnp.where(odd == 0, middle, high)
    send_ref[pl.ds(0, quad), :] = jnp.where(odd == 0, middle, low)
    send_ref[pl.ds(quad, quad), :] = jnp.where(odd == 0, high, middle)
    drift = got_ref[0, pl.ds(2 * plan.block, 8), :]
    for j in range(1, pairs):
        drift = drift + got_ref[j, pl.ds(2 * plan.block, 8), :]
    keep_ref[pl.ds(2 * quad, 8), :] = drift
    send_ref[pl.ds(2 * quad, 8), :] = drift


def times(left, right):
    return (left[0] * right[0] - left[1] * right[1], left[0] * right[1] + left[1] * right[0])


def times_conj(left, right):
    return (left[0] * right[0] + left[1] * right[1], left[1] * right[0] - left[0] * right[1])


def rotation(fields):
    both, apart = fields[0], fields[1]
    a, b, e = 0.5 * (both + apart), 0.5 * (both - apart), -both
    u, v, w = (fields[2], fields[3]), (fields[4], fields[5]), (fields[6], fields[7])
    square = [x[0] * x[0] + x[1] * x[1] for x in (u, v, w)]
    a00, a11, a22 = square[2] - b * e, square[1] - a * e, square[0] - a * b
    vw, uw, vu = times_conj(v, w), times(u, w), times_conj(v, u)
    a01 = (e * u[1] - vw[0], -(e * u[0]) - vw[1])
    a02 = (uw[0] + b * v[1], uw[1] - b * v[0])
    a12 = (a * w[1] - vu[0], -(a * w[0]) - vu[1])
    turn = a * a00 + times_conj(u, a01)[1] + times_conj(v, a02)[1]
    real = 1.0 + (a00 + a11 + a22)
    scale = 2.0 / (real * real + turn * turn)
    factor = (real * scale, turn * scale)
    entries = [[None] * 3 for _ in range(3)]
    for i, (up, imag) in enumerate(((a00, a), (a11, b), (a22, e))):
        value = times((1.0 + up, imag), factor)
        entries[i][i] = (value[0] - 1.0, value[1])
    for (i, j), up, off in (((0, 1), a01, u), ((0, 2), a02, v), ((1, 2), a12, w)):
        entries[i][j] = times((up[0] + off[0], up[1] + off[1]), factor)
        entries[j][i] = times((up[0] - off[0], off[1] - up[1]), factor)
    return [entries[i][j][part] for part in range(2) for i in range(3) for j in range(3)]


def update_kernel(
    plan, index_ref, keep_ref, got_ref, links_ref, fixed_ref, drift_ref, here, along, staged, semaphores
):
    rows, side = plan.rows, plan.side
    quad = 4 * rows
    odd = index_ref[0] % 2

    def turn(i, _):
        begin = pl.multiple_of(i * 8, 8)
        for q, lead in ((0, 8), (1, 0)):
            fields = [None] * 8
            for f in range(4):
                place = pl.ds(pl.multiple_of(q * quad + f * rows + begin, 8), 8)
                own, other = keep_ref[place, :], got_ref[place, :]
                fields[f] = jnp.where(odd == 0, own, other)
                fields[4 + f] = jnp.where(odd == 0, other, own)
            for n, value in enumerate(rotation(fields)):
                if q == 0:
                    here[n, pl.ds(begin + lead, 8), :] = value
                else:
                    along[n, pl.ds(begin, 8), :] = value
        return 0

    lax.fori_loop(0, rows // 8, turn, 0, unroll=3)

    def update(d, i):
        begin = i * 8

        def matrix(read):
            value = [read(n) for n in range(18)]
            return [[(value[3 * r + c], value[9 + 3 * r + c]) for c in range(3)] for r in range(3)]

        own = matrix(lambda n: here[n, pl.ds(begin + 8, 8), :])
        links = matrix(lambda n: links_ref[d * 18 + n, pl.ds(begin, 8), :])
        if d == 0:
            ahead = matrix(lambda n: along[n, pl.ds(begin, 8), :])
        elif d == 1:
            ahead = matrix(lambda n: moved(here, n, 8 + begin, 8, side))
        else:
            at_end = (last_index(8, side) + begin * LANES) % side == side - 1
            ahead = matrix(
                lambda n: jnp.where(
                    at_end,
                    moved(here, n, 8 + begin, 8, 1 - side),
                    moved(here, n, 8 + begin, 8, 1),
                )
            )
        for r in range(3):
            line = [
                add(times(own[r][0], links[0][c]), times(own[r][1], links[1][c]), times(own[r][2], links[2][c]))
                for c in range(3)
            ]
            for c in range(3):
                value = add(*[times_conj(line[k], ahead[c][k]) for k in range(3)])
                for part in range(2):
                    staged[d * 18 + part * 9 + r * 3 + c, pl.ds(begin, 8), :] = value[part]

    tiles = rows // 8
    copies = []

    def write(place, rows_place, n):
        copy = pltpu.make_async_copy(
            staged.at[place, rows_place], fixed_ref.at[place, rows_place], semaphores.at[n]
        )
        copy.start()
        copies.append(copy)

    for n in range(18):
        wrap(here, n, rows)
    for d in (1, 2, 0):
        chunks = 1 if d else 3
        for m in range(chunks):
            part = tiles // chunks

            for i in range(m * part, (m + 1) * part):
                update(d, i)
            write(pl.ds(d * 18, 18), pl.ds(m * part * 8, part * 8), len(copies))
    total = keep_ref[pl.ds(2 * quad, 8), :] + got_ref[pl.ds(2 * quad, 8), :]
    drift_ref[0] = jnp.sum(total) * (1.0 / (9.0 * plan.count_x * plan.cells))
    for copy in copies:
        copy.wait()


def add(first, second, third):
    return (first[0] + second[0] + third[0], first[1] + second[1] + third[1])


def whole_spec():
    return pl.BlockSpec(memory_space=pltpu.VMEM)


def scalar_spec():
    return pl.BlockSpec(memory_space=pltpu.SMEM)


def shape_of(*shape):
    return jax.ShapeDtypeStruct(shape, jnp.float32)


def local(gauge_links):
    count_x = lax.axis_size("gx")
    plan = Plan(count_x, SIDE)
    rows, pairs = plan.rows, plan.pairs
    table = tables(plan)
    index = lax.axis_index("gx").astype(jnp.int32).reshape(1)
    links = gauge_links.reshape(54, rows, LANES)
    quads = 8 * rows
    swap = [(i, i ^ 1) for i in range(count_x)]
    halo = [(2 * p, 2 * p - 1) for p in range(1, pairs)] + [(count_x - 1, 0)]
    same_core, same_core_back = [
        [[c + 2 * p for p in sorted(range(pairs), key=place.__getitem__)] for c in range(2)]
        for place in (plan.place, plan.back_place)
    ]

    keep, send, ahead = pl.pallas_call(
        functools.partial(divergence_kernel, plan),
        out_shape=(shape_of(quads, LANES),) * 3,
        in_specs=[scalar_spec(), pl.BlockSpec(memory_space=pltpu.HBM)],
        out_specs=(whole_spec(),) * 3,
        scratch_shapes=[
            pltpu.VMEM((54, rows, LANES), jnp.float32),
            pltpu.VMEM((8, rows + 16, LANES), jnp.float32),
            pltpu.VMEM((8, rows + 16, LANES), jnp.float32),
            pltpu.SemaphoreType.DMA((3, 3)),
        ],
        compiler_params=params(),
        name="divergence",
    )(index, pltpu.with_memory_space_constraint(links, pltpu.HBM))
    got = lax.ppermute(send, "gx", swap)
    beside = lax.ppermute(ahead, "gx", halo)
    sent, odd_part, odd_drift = pl.pallas_call(
        functools.partial(forward_kernel, plan),
        out_shape=(
            shape_of(pairs, plan.sent, LANES),
            shape_of(SIDE, 4 * LANES),
            shape_of(8, LANES),
        ),
        in_specs=[scalar_spec()] + [whole_spec()] * 5,
        out_specs=(whole_spec(),) * 3,
        scratch_shapes=[pltpu.VMEM((12 * rows, LANES), jnp.float32)],
        compiler_params=params(),
        name="forward",
    )(index, keep, got, table["last"], table["second"], table["modes"])
    arrived = lax.all_to_all(
        sent, "gx", split_axis=0, concat_axis=0, tiled=True, axis_index_groups=same_core
    )
    drift_part = pl.pallas_call(
        functools.partial(drift_kernel, plan),
        out_shape=shape_of(8, LANES),
        in_specs=[scalar_spec()] + [whole_spec()] * 4,
        out_specs=whole_spec(),
        compiler_params=params(),
        cost_estimate=pl.CostEstimate(flops=5 * 10**10, bytes_accessed=5 * 10**7, transcendentals=0),
        name="drift",
    )(index, odd_drift, beside, keep, send)
    back = pl.pallas_call(
        functools.partial(filter_kernel, plan),
        out_shape=shape_of(pairs, plan.returned, LANES),
        in_specs=[scalar_spec()] + [whole_spec()] * 3,
        out_specs=whole_spec(),
        compiler_params=params(),
        name="filter",
    )(index, arrived, table["modes"], drift_part)
    returned = lax.all_to_all(
        back, "gx", split_axis=0, concat_axis=0, tiled=True, axis_index_groups=same_core_back
    )
    keep, send = pl.pallas_call(
        functools.partial(backward_kernel, plan),
        out_shape=(shape_of(quads + 8, LANES), shape_of(quads + 8, LANES)),
        in_specs=[scalar_spec()] + [whole_spec()] * 5,
        out_specs=(whole_spec(), whole_spec()),
        scratch_shapes=[
            pltpu.VMEM((2 * plan.tiles, SIDE, LANES), jnp.float32),
            pltpu.VMEM((12 * rows, LANES), jnp.float32),
        ],
        compiler_params=params(),
        name="backward",
    )(index, returned, odd_part, table["last_back"], table["second"], table["modes"])
    got = lax.ppermute(send, "gx", swap)
    fixed, drift = pl.pallas_call(
        functools.partial(update_kernel, plan),
        out_shape=(shape_of(54, rows, LANES), shape_of(1)),
        in_specs=[scalar_spec()] + [whole_spec()] * 3,
        out_specs=(pl.BlockSpec(memory_space=pltpu.HBM), scalar_spec()),
        scratch_shapes=[
            pltpu.VMEM((18, rows + 16, LANES), jnp.float32),
            pltpu.VMEM((18, rows, LANES), jnp.float32),
            pltpu.VMEM((54, rows, LANES), jnp.float32),
            pltpu.SemaphoreType.DMA((5,)),
        ],
        compiler_params=params(),
        name="update",
    )(index, keep, got, links)
    return fixed.reshape(gauge_links.shape), drift


def solution(mesh):
    in_specs = (P(None, None, None, None, ("ta", "gx"), None),)
    out_specs = (P(None, None, None, None, ("ta", "gx"), None), P("ta"))
    return jax.shard_map(local, mesh=mesh, in_specs=in_specs, out_specs=out_specs, check_vma=False)
```

```python
import functools
import math

import jax
import jax.numpy as jnp
import numpy as np
from jax import lax
from jax.experimental import pallas as pl
from jax.experimental.pallas import tpu as pltpu
from jax.sharding import PartitionSpec as P

SIDE = 96
LANES = 128

step_size = 0.08
peak_square = 12.0
gain = 0.5 * step_size * peak_square

params = functools.partial(pltpu.CompilerParams, vmem_limit_bytes=48 * 1024 * 1024)
drift_weights = (1.5, 0.5, 2.0, 2.0, 2.0, 2.0, 2.0, 2.0)


class Plan:
    def __init__(self, count_x, side):
        self.count_x, self.side = count_x, side
        self.cells = side * side
        self.rows = self.cells // LANES
        self.period = side * LANES // math.gcd(side, LANES)
        self.wide = self.period // LANES
        self.folds = self.period // side
        self.groups = self.cells // self.period
        self.pairs = count_x // 2
        self.share = side // self.pairs
        self.full = self.share // 8 * 8
        self.rest = self.share - self.full
        self.tiles = 4 * side // LANES
        self.block = self.tiles * self.share
        self.stride = -(-self.block // 8) * 8
        self.sent = -(-2 * self.block // 8) * 8
        half = self.pairs // 2
        there = [(p + half) % self.pairs for p in range(self.pairs)]
        back = [p ^ (1 - half % 2) for p in range(half, self.pairs)] + list(range(half))[::-1]
        self.place = [there.index(p) for p in range(self.pairs)]
        self.back_place = [back.index(p) for p in range(self.pairs)]
        self.returned = -(-(2 * self.block + 8) // 8) * 8


def fourier(length):
    site = np.arange(length)
    basis = np.zeros((length, length))
    for k in range(length):
        angle = 2.0 * math.pi * (k * site % length) / length
        if k == 0 or 2 * k == length:
            basis[k] = np.cos(angle) / math.sqrt(length)
        elif 2 * k < length:
            basis[k] = np.cos(angle) * math.sqrt(2.0 / length)
        else:
            basis[k] = np.sin(angle) * math.sqrt(2.0 / length)
    return basis


def eigen(length):
    return 4.0 * np.sin(math.pi * np.arange(length) / length) ** 2


def split_table(table):
    high = table.astype(jnp.bfloat16)
    low = (table - high.astype(np.float64)).astype(jnp.bfloat16)
    return np.stack([high, low])


def stack_table(table):
    high, low = split_table(table)
    return np.block([[high, high], [low, np.zeros_like(low)]])


def tables(plan):
    side, folds, groups = plan.side, plan.folds, plan.groups
    basis = fourier(side)
    last = np.zeros((folds, side, folds, LANES))
    for j in range(folds):
        last[j, :, j, :side] = basis.T
    last = last.reshape(folds * side, folds * LANES)
    order = [plan.share * j + i for j in range(plan.pairs) for i in range(plan.full)]
    order += [plan.share * j + plan.full + i for j in range(plan.pairs) for i in range(plan.rest)]
    columns = [folds * g + j for j in range(folds) for g in range(groups)]
    second = basis[order][:, columns]
    value = eigen(side)
    inverse_side = np.zeros((side, LANES))
    inverse_side[:, :side] = 1.0 / (2.0 + value[order][:, None] + value[None, :])
    lane = np.arange(plan.tiles * LANES).reshape(plan.tiles, 1, LANES)
    owner = np.zeros((plan.pairs, plan.stride, LANES))
    for j in range(plan.pairs):
        parts = []
        for start, size in ((0, plan.full), (plan.full, plan.rest)):
            mode = plan.share * j + start + np.arange(size).reshape(1, size, 1)
            parts.append((value[mode] + value[lane % side]).reshape(plan.tiles * size, LANES))
        owner[j, : plan.block] = np.concatenate(parts)
    return {
        "last": np.stack([split_table(last[a:b, c:d]) for a, b, c, d in bands(plan)]),
        "last_back": np.stack([split_table(last[a:b, c:d].T) for a, b, c, d in bands(plan)]),
        "second": np.stack([stack_table(second), stack_table(second.T)]),
        "modes": np.concatenate([inverse_side, owner.reshape(-1, LANES)]).astype(np.float32),
    }


def halve(value):
    high = value.astype(jnp.bfloat16)
    low = (value - high.astype(jnp.float32)).astype(jnp.bfloat16)
    return high, low


def product(left, right):
    dot = functools.partial(jnp.dot, preferred_element_type=jnp.float32)
    both = dot(jnp.concatenate(left, axis=0), right[0])
    size = left[0].shape[0]
    return both[:size] + (both[size:] + dot(left[0], right[1]))


def stacked(table, value):
    both = jnp.dot(table, jnp.concatenate(halve(value), axis=0), preferred_element_type=jnp.float32)
    size = both.shape[0] // 2
    return both[:size] + both[size:]


def bands(plan):
    for j in range(0, plan.folds, 2):
        rows = min(2, plan.folds - j)
        begin, end = j * plan.side // LANES, -(-(j + rows) * plan.side // LANES)
        yield begin * LANES, end * LANES, j * LANES, (j + rows) * LANES


def lane_of(shape):
    return lax.broadcasted_iota(jnp.int32, shape, 1)


def moved(ref, field, start, size, distance):
    down, over = distance // LANES, distance % LANES
    here = ref[field, pl.ds(start + down, size), :]
    after = ref[field, pl.ds(start + down + 1, size), :]
    mixed = jnp.where(lane_of(here.shape) >= over, here, after)
    return pltpu.roll(mixed, LANES - over, 1)


def last_index(rows, side):
    row = lax.broadcasted_iota(jnp.int32, (rows, LANES), 0)
    return (row * LANES + lane_of((rows, LANES))) % side


def wrap(ref, field, rows):
    ref[field, pl.ds(0, 8), :] = ref[field, pl.ds(rows, 8), :]
    ref[field, pl.ds(8 + rows, 8), :] = ref[field, pl.ds(8, 8), :]


def projected(links, d):
    def entry(part, i, j):
        return links[((d * 2 + part) * 3 + i) * 3 + j]

    im00, im11, im22 = entry(1, 0, 0), entry(1, 1, 1), entry(1, 2, 2)
    fields = [(im00 + im11 - 2.0 * im22) * (1.0 / 3.0), im00 - im11]
    for i, j in ((0, 1), (0, 2), (1, 2)):
        fields.append(0.5 * (entry(0, i, j) - entry(0, j, i)))
        fields.append(0.5 * (entry(1, i, j) + entry(1, j, i)))
    return fields


def link_copies(links_ref, staged, semaphores):
    copies = []
    for n, d in enumerate((1, 2, 0)):
        for m, (begin, size) in enumerate(((1, 3), (5, 3), (9, 9))):
            place = pl.ds(d * 18 + begin, size)
            copies.append(
                pltpu.make_async_copy(links_ref.at[place], staged.at[place], semaphores.at[n, m])
            )
    return copies


def divergence_kernel(
    plan, index_ref, links_ref, keep_ref, send_ref, ahead_ref, staged, second, third, semaphores
):
    rows, side = plan.rows, plan.side
    copies = link_copies(links_ref, staged, semaphores)
    for copy in copies:
        copy.start()
    odd = index_ref[0] % 2
    at_start = last_index(rows, side) == 0
    middle = pl.ds(8, rows)
    for copy in copies[:3]:
        copy.wait()
    for f, value in enumerate(projected(staged, 1)):
        second[f, middle, :] = value
        wrap(second, f, rows)
    diverge = [moved(second, f, 8, rows, -side) - second[f, middle, :] for f in range(8)]
    for copy in copies[3:6]:
        copy.wait()
    for f, value in enumerate(projected(staged, 2)):
        third[f, middle, :] = value
        wrap(third, f, rows)
    for f in range(8):
        beside = jnp.where(
            at_start, moved(third, f, 8, rows, side - 1), moved(third, f, 8, rows, -1)
        )
        diverge[f] = diverge[f] + (beside - third[f, middle, :])
        second[f, middle, :] = diverge[f]
    for copy in copies[6:]:
        copy.wait()
    direct = projected(staged, 0)
    index = index_ref[0]
    for f in range(8):
        place = pl.ds(f * rows, rows)
        total = second[f, middle, :] - direct[f]
        ahead_ref[place, :] = jnp.where(index == plan.count_x - 1, direct[f], total)
    for f in range(4):
        for part in range(2):
            place = pl.ds((part * 4 + f) * rows, rows)
            low, high = direct[f], direct[4 + f]
            if part == 0:
                low, high = second[f, middle, :] - low, second[4 + f, middle, :] - high
            keep_ref[place, :] = jnp.where(odd == 0, low, high)
            send_ref[place, :] = jnp.where(odd == 0, high, low)


def forward_kernel(
    plan, index_ref, keep_ref, got_ref, last_ref, second_ref, modes_ref, sent_ref, odd_ref, drift_ref
):
    rows, groups, folds, side = plan.rows, plan.groups, plan.folds, plan.side
    odd = index_ref[0] % 2
    quad = 4 * rows
    count = 4 * groups
    square = jnp.zeros((8, LANES), jnp.float32)
    wide = []
    for s in range(plan.wide):
        own_d, own_a, got_d, got_a = [
            ref[pl.ds(begin + s, count, stride=plan.wide), :]
            for ref in (keep_ref, got_ref)
            for begin in (0, quad)
        ]
        even_d, odd_d = jnp.where(odd == 0, own_d, got_d), jnp.where(odd == 0, got_d, own_d)
        even_a, odd_a = jnp.where(odd == 0, own_a, got_a), jnp.where(odd == 0, got_a, own_a)
        whole = odd_d + even_a
        for f in range(4):
            part = whole[f * groups : (f + 1) * groups]
            square = square + sum_tiles(part * part) * jnp.where(
                odd == 0, drift_weights[f], drift_weights[4 + f]
            )
        wide.append(jnp.concatenate([even_d, whole, odd_a], axis=0))
    drift_ref[...] = square
    wide = jnp.concatenate(wide, axis=1)
    high, low = halve(wide)
    waves = jnp.concatenate(
        [
            product(
                (high[:, begin:end], low[:, begin:end]),
                (last_ref[n, 0], last_ref[n, 1]),
            )
            for n, (begin, end, _, _) in enumerate(bands(plan))
        ],
        axis=1,
    )
    columns = []
    for pf in range(12):
        part = waves[pf * groups : (pf + 1) * groups]
        columns.append(
            jnp.concatenate([part[:, j * LANES : (j + 1) * LANES] for j in range(folds)], axis=0)
        )
    modes = stacked(second_ref[0], jnp.concatenate(columns, axis=1))
    inverse = modes_ref[:side]
    full, rest, pairs, tiles = plan.full, plan.rest, plan.pairs, plan.tiles
    lane = lane_of((side, LANES))
    zero = (lane == 0) & (lax.broadcasted_iota(jnp.int32, (side, LANES), 0) == 0)
    even, between, after = [
        [modes[:, (q * 4 + f) * LANES : (q * 4 + f + 1) * LANES] for f in range(4)] for q in range(3)
    ]
    shared = [value * inverse for value in between]
    for f in range(4):
        odd_ref[:, f * LANES : (f + 1) * LANES] = gain * shared[f]
    below = [even[f] + shared[f] for f in range(4)]
    above = [jnp.where(zero, between[f], after[f] + shared[f]) for f in range(4)]
    for q, fields in enumerate((below, above)):
        for t, value in enumerate(pack(fields, lane, side)):
            at = q * tiles + t
            for j in range(pairs):
                if full:
                    sent_ref[plan.place[j], pl.ds(at * full, full), :] = value[j * full : (j + 1) * full]
                if rest:
                    begin = pairs * full + j * rest
                    sent_ref[plan.place[j], pl.ds(2 * tiles * full + at * rest, rest), :] = value[
                        begin : begin + rest
                    ]
    spare = plan.sent - 2 * plan.block
    if spare:
        sent_ref[:, pl.ds(2 * plan.block, spare), :] = jnp.zeros((pairs, spare, LANES), jnp.float32)


def sum_tiles(value):
    total = value[:8]
    for i in range(1, value.shape[0] // 8):
        total = total + value[i * 8 : (i + 1) * 8]
    return total


def pack(fields, lane, side):
    rolled = [
        value if f * side % LANES == 0 else pltpu.roll(value, f * side % LANES, 1)
        for f, value in enumerate(fields)
    ]
    packed = []
    for t in range(4 * side // LANES):
        value = None
        for f in range(4):
            if f * side < (t + 1) * LANES and (f + 1) * side > t * LANES:
                value = rolled[f] if value is None else jnp.where(lane >= f * side - t * LANES, rolled[f], value)
        packed.append(value)
    return packed


def unpack(packed, lane, side):
    fields = []
    for f in range(4):
        begin = f * side // LANES
        end = ((f + 1) * side - 1) // LANES
        offset = f * side % LANES
        value = packed[begin]
        if end != begin:
            value = jnp.where(lane >= offset, packed[begin], packed[end])
        if offset:
            value = pltpu.roll(value, LANES - offset, 1)
        fields.append(jnp.where(lane < side, value, 0.0))
    return fields


def drift_kernel(plan, index_ref, odd_ref, beside_ref, keep_ref, send_ref, drift_ref):
    rows, count_x = plan.rows, plan.count_x
    index = index_ref[0]
    square = jnp.zeros((rows, LANES), jnp.float32)
    part = jnp.where(index == 0, 0, 4 * rows)
    for f in range(4):
        place = pl.ds(pl.multiple_of(part + f * rows, 8), rows)
        own, other = keep_ref[place, :], send_ref[place, :]
        low, high = jnp.where(index % 2 == 0, own, other), jnp.where(index % 2 == 0, other, own)
        for n, value in ((f, low), (4 + f, high)):
            total = beside_ref[pl.ds(n * rows, rows), :] + value
            square = square + total * total * drift_weights[n]
    complete = (index == 0) | ((index % 2 == 1) & (index < count_x - 1))
    drift_ref[...] = odd_ref[...] + jnp.where(complete, sum_tiles(square), 0.0)


def filter_kernel(plan, index_ref, got_ref, modes_ref, drift_ref, back_ref):
    pairs, tiles, count_x = plan.pairs, plan.tiles, plan.count_x
    half = pairs // 2
    drift = drift_ref[...]
    for part, (size, first) in enumerate(((plan.full, 0), (plan.rest, 2 * tiles * plan.full))):
        if not size:
            continue
        length = tiles * size
        own = pl.multiple_of(plan.side + index_ref[0] // 2 * plan.stride, 8)
        value = modes_ref[pl.ds(own, plan.stride), :][part * tiles * plan.full :][:length]
        low, high = pl.ds(first, length), pl.ds(first + length, length)
        inside = value > 0
        below = [got_ref[plan.place[p], low, :] for p in range(pairs)]
        above = [got_ref[plan.place[p], high, :] for p in range(pairs)]
        rhs = [
            below[p] + jnp.where(inside, above[(p - 1) % pairs], -below[(p - 1) % pairs])
            for p in range(pairs)
        ]
        plus = [rhs[d] + rhs[pairs - d] for d in range(1, half)]
        minus = [rhs[d] - rhs[pairs - d] for d in range(1, half)]
        cosines, sines = [], []
        for k in range(half + 1):
            total = rhs[0] + rhs[half] if k % 2 == 0 else rhs[0] - rhs[half]
            for d in range(1, half):
                total = total + plus[d - 1] * math.cos(2 * math.pi * (k * d % pairs) / pairs)
            root = 4.0 * math.sin(math.pi * k / count_x) ** 2
            split = (value + root) * (value + (4.0 - root))
            scale = gain / pairs * (1.0 if k in (0, half) else 2.0)
            if k == 0:
                factor = jnp.where(inside, scale * (2.0 + value) / jnp.where(inside, split, 1.0), 0.0)
                whole = above[0]
                for p in range(1, pairs):
                    whole = whole + above[p]
                mean = jnp.where(inside, 0.0, whole * (-0.25 * gain / pairs))
                cosines.append(total * factor + mean)
            else:
                factor = scale * (2.0 + value) / split
                cosines.append(total * factor)
                if k < half:
                    wave = jnp.zeros_like(value)
                    for d in range(1, half):
                        wave = wave + minus[d - 1] * math.sin(2 * math.pi * (k * d % pairs) / pairs)
                    sines.append(wave * factor)
        results = [None] * pairs
        for d in range(half + 1):
            even = cosines[0]
            for k in range(1, half + 1):
                even = even + cosines[k] * math.cos(2 * math.pi * (k * d % pairs) / pairs)
            if d in (0, half):
                results[d] = even
            else:
                wave = jnp.zeros_like(value)
                for k in range(1, half):
                    wave = wave + sines[k - 1] * math.sin(2 * math.pi * (k * d % pairs) / pairs)
                results[d] = even + wave
                results[pairs - d] = even - wave
        for p in range(pairs):
            back_ref[plan.back_place[p], low, :] = results[p]
            back_ref[plan.back_place[p], high, :] = results[(p + 1) % pairs]
    for p in range(pairs):
        back_ref[p, pl.ds(2 * plan.block, 8), :] = drift


def backward_kernel(
    plan, index_ref, got_ref, odd_ref, last_ref, second_ref, modes_ref, keep_ref, send_ref, packed
):
    rows, groups, folds, side = plan.rows, plan.groups, plan.folds, plan.side
    full, rest, pairs, tiles = plan.full, plan.rest, plan.pairs, plan.tiles
    odd = index_ref[0] % 2
    for q in range(2):
        for t in range(tiles):
            at = q * tiles + t
            for j in range(pairs):
                if full:
                    packed[at, pl.ds(j * full, full), :] = got_ref[plan.back_place[j], pl.ds(at * full, full), :]
                if rest:
                    packed[at, pl.ds(pairs * full + j * rest, rest), :] = got_ref[
                        plan.back_place[j], pl.ds(2 * tiles * full + at * rest, rest), :
                    ]
    lane = lane_of((side, LANES))
    inverse = modes_ref[:side]
    even, after = [
        unpack([packed[q * tiles + t] for t in range(tiles)], lane, side) for q in range(2)
    ]
    between = [
        odd_ref[:, f * LANES : (f + 1) * LANES] + (even[f] + after[f]) * inverse for f in range(4)
    ]
    waves = stacked(second_ref[1], jnp.concatenate(even + between + after, axis=1))
    blocks = []
    for pf in range(12):
        part = waves[:, pf * LANES : (pf + 1) * LANES]
        blocks.append(
            jnp.concatenate([part[j * groups : (j + 1) * groups] for j in range(folds)], axis=1)
        )
    high, low = halve(jnp.concatenate(blocks, axis=0))
    wide = [None] * plan.wide
    for n, (begin, end, first, last) in enumerate(bands(plan)):
        part = product(
            (high[:, first:last], low[:, first:last]), (last_ref[n, 0], last_ref[n, 1])
        )
        for s in range(begin // LANES, end // LANES):
            tile = part[:, s * LANES - begin : (s + 1) * LANES - begin]
            wide[s] = tile if wide[s] is None else wide[s] + tile
    quad, count = 4 * rows, 4 * groups
    for s in range(plan.wide):
        low, middle, high = [wide[s][q * count : (q + 1) * count] for q in range(3)]
        here, ahead = pl.ds(s, count, stride=plan.wide), pl.ds(quad + s, count, stride=plan.wide)
        keep_ref[here, :] = jnp.where(odd == 0, low, middle)
        keep_ref[ahead, :] = jnp.where(odd == 0, middle, high)
        send_ref[here, :] = jnp.where(odd == 0, middle, low)
        send_ref[ahead, :] = jnp.where(odd == 0, high, middle)
    drift = got_ref[0, pl.ds(2 * plan.block, 8), :]
    for j in range(1, pairs):
        drift = drift + got_ref[j, pl.ds(2 * plan.block, 8), :]
    keep_ref[pl.ds(2 * quad, 8), :] = drift
    send_ref[pl.ds(2 * quad, 8), :] = drift


def times(left, right):
    return (left[0] * right[0] - left[1] * right[1], left[0] * right[1] + left[1] * right[0])


def times_conj(left, right):
    return (left[0] * right[0] + left[1] * right[1], left[1] * right[0] - left[0] * right[1])


def rotation(fields):
    both, apart = fields[0], fields[1]
    a, b, e = 0.5 * (both + apart), 0.5 * (both - apart), -both
    u, v, w = (fields[2], fields[3]), (fields[4], fields[5]), (fields[6], fields[7])
    square = [x[0] * x[0] + x[1] * x[1] for x in (u, v, w)]
    a00, a11, a22 = square[2] - b * e, square[1] - a * e, square[0] - a * b
    vw, uw, vu = times_conj(v, w), times(u, w), times_conj(v, u)
    a01 = (e * u[1] - vw[0], -(e * u[0]) - vw[1])
    a02 = (uw[0] + b * v[1], uw[1] - b * v[0])
    a12 = (a * w[1] - vu[0], -(a * w[0]) - vu[1])
    turn = a * a00 + times_conj(u, a01)[1] + times_conj(v, a02)[1]
    real = 1.0 + (a00 + a11 + a22)
    scale = 2.0 / (real * real + turn * turn)
    factor = (real * scale, turn * scale)
    entries = [[None] * 3 for _ in range(3)]
    for i, (up, imag) in enumerate(((a00, a), (a11, b), (a22, e))):
        value = times((1.0 + up, imag), factor)
        entries[i][i] = (value[0] - 1.0, value[1])
    for (i, j), up, off in (((0, 1), a01, u), ((0, 2), a02, v), ((1, 2), a12, w)):
        entries[i][j] = times((up[0] + off[0], up[1] + off[1]), factor)
        entries[j][i] = times((up[0] - off[0], off[1] - up[1]), factor)
    return [entries[i][j][part] for part in range(2) for i in range(3) for j in range(3)]


def update_kernel(
    plan, index_ref, keep_ref, got_ref, links_ref, fixed_ref, drift_ref, here, along, staged, semaphores
):
    rows, side = plan.rows, plan.side
    quad = 4 * rows
    odd = index_ref[0] % 2

    def turn(i, _):
        begin = pl.multiple_of(i * 8, 8)
        for q, lead in ((0, 8), (1, 0)):
            fields = [None] * 8
            for f in range(4):
                place = pl.ds(pl.multiple_of(q * quad + f * rows + begin, 8), 8)
                own, other = keep_ref[place, :], got_ref[place, :]
                fields[f] = jnp.where(odd == 0, own, other)
                fields[4 + f] = jnp.where(odd == 0, other, own)
            for n, value in enumerate(rotation(fields)):
                if q == 0:
                    here[n, pl.ds(begin + lead, 8), :] = value
                else:
                    along[n, pl.ds(begin, 8), :] = value
        return 0

    lax.fori_loop(0, rows // 8, turn, 0, unroll=3)

    def update(d, i):
        begin = i * 8

        def matrix(read):
            value = [read(n) for n in range(18)]
            return [[(value[3 * r + c], value[9 + 3 * r + c]) for c in range(3)] for r in range(3)]

        own = matrix(lambda n: here[n, pl.ds(begin + 8, 8), :])
        links = matrix(lambda n: links_ref[d * 18 + n, pl.ds(begin, 8), :])
        if d == 0:
            ahead = matrix(lambda n: along[n, pl.ds(begin, 8), :])
        elif d == 1:
            ahead = matrix(lambda n: moved(here, n, 8 + begin, 8, side))
        else:
            at_end = (last_index(8, side) + begin * LANES) % side == side - 1
            ahead = matrix(
                lambda n: jnp.where(
                    at_end,
                    moved(here, n, 8 + begin, 8, 1 - side),
                    moved(here, n, 8 + begin, 8, 1),
                )
            )
        for r in range(3):
            line = [
                add(times(own[r][0], links[0][c]), times(own[r][1], links[1][c]), times(own[r][2], links[2][c]))
                for c in range(3)
            ]
            for c in range(3):
                value = add(*[times_conj(line[k], ahead[c][k]) for k in range(3)])
                for part in range(2):
                    staged[d * 18 + part * 9 + r * 3 + c, pl.ds(begin, 8), :] = value[part]

    tiles = rows // 8
    copies = []

    def write(place, rows_place, n):
        copy = pltpu.make_async_copy(
            staged.at[place, rows_place], fixed_ref.at[place, rows_place], semaphores.at[n]
        )
        copy.start()
        copies.append(copy)

    for n in range(18):
        wrap(here, n, rows)
    for d in (1, 2, 0):
        chunks = 1 if d else 3
        for m in range(chunks):
            part = tiles // chunks

            for i in range(m * part, (m + 1) * part):
                update(d, i)
            write(pl.ds(d * 18, 18), pl.ds(m * part * 8, part * 8), len(copies))
    total = keep_ref[pl.ds(2 * quad, 8), :] + got_ref[pl.ds(2 * quad, 8), :]
    drift_ref[0] = jnp.sum(total) * (1.0 / (9.0 * plan.count_x * plan.cells))
    for copy in copies:
        copy.wait()


def add(first, second, third):
    return (first[0] + second[0] + third[0], first[1] + second[1] + third[1])


def whole_spec():
    return pl.BlockSpec(memory_space=pltpu.VMEM)


def scalar_spec():
    return pl.BlockSpec(memory_space=pltpu.SMEM)


def shape_of(*shape):
    return jax.ShapeDtypeStruct(shape, jnp.float32)


def local(gauge_links):
    count_x = lax.axis_size("gx")
    plan = Plan(count_x, SIDE)
    rows, pairs = plan.rows, plan.pairs
    table = tables(plan)
    index = lax.axis_index("gx").astype(jnp.int32).reshape(1)
    links = gauge_links.reshape(54, rows, LANES)
    quads = 8 * rows
    swap = [(i, i ^ 1) for i in range(count_x)]
    halo = [(2 * p, 2 * p - 1) for p in range(1, pairs)] + [(count_x - 1, 0)]
    same_core, same_core_back = [
        [[c + 2 * p for p in sorted(range(pairs), key=place.__getitem__)] for c in range(2)]
        for place in (plan.place, plan.back_place)
    ]

    keep, send, ahead = pl.pallas_call(
        functools.partial(divergence_kernel, plan),
        out_shape=(shape_of(quads, LANES),) * 3,
        in_specs=[scalar_spec(), pl.BlockSpec(memory_space=pltpu.HBM)],
        out_specs=(whole_spec(),) * 3,
        scratch_shapes=[
            pltpu.VMEM((54, rows, LANES), jnp.float32),
            pltpu.VMEM((8, rows + 16, LANES), jnp.float32),
            pltpu.VMEM((8, rows + 16, LANES), jnp.float32),
            pltpu.SemaphoreType.DMA((3, 3)),
        ],
        compiler_params=params(),
        name="divergence",
    )(index, pltpu.with_memory_space_constraint(links, pltpu.HBM))
    got = lax.ppermute(send, "gx", swap)
    beside = lax.ppermute(ahead, "gx", halo)
    sent, odd_part, odd_drift = pl.pallas_call(
        functools.partial(forward_kernel, plan),
        out_shape=(
            shape_of(pairs, plan.sent, LANES),
            shape_of(SIDE, 4 * LANES),
            shape_of(8, LANES),
        ),
        in_specs=[scalar_spec()] + [whole_spec()] * 5,
        out_specs=(whole_spec(),) * 3,
        compiler_params=params(),
        name="forward",
    )(index, keep, got, table["last"], table["second"], table["modes"])
    arrived = lax.all_to_all(
        sent, "gx", split_axis=0, concat_axis=0, tiled=True, axis_index_groups=same_core
    )
    drift_part = pl.pallas_call(
        functools.partial(drift_kernel, plan),
        out_shape=shape_of(8, LANES),
        in_specs=[scalar_spec()] + [whole_spec()] * 4,
        out_specs=whole_spec(),
        compiler_params=params(),
        cost_estimate=pl.CostEstimate(flops=5 * 10**10, bytes_accessed=5 * 10**7, transcendentals=0),
        name="drift",
    )(index, odd_drift, beside, keep, send)
    back = pl.pallas_call(
        functools.partial(filter_kernel, plan),
        out_shape=shape_of(pairs, plan.returned, LANES),
        in_specs=[scalar_spec()] + [whole_spec()] * 3,
        out_specs=whole_spec(),
        compiler_params=params(),
        name="filter",
    )(index, arrived, table["modes"], drift_part)
    returned = lax.all_to_all(
        back, "gx", split_axis=0, concat_axis=0, tiled=True, axis_index_groups=same_core_back
    )
    keep, send = pl.pallas_call(
        functools.partial(backward_kernel, plan),
        out_shape=(shape_of(quads + 8, LANES), shape_of(quads + 8, LANES)),
        in_specs=[scalar_spec()] + [whole_spec()] * 5,
        out_specs=(whole_spec(), whole_spec()),
        scratch_shapes=[
            pltpu.VMEM((2 * plan.tiles, SIDE, LANES), jnp.float32),
        ],
        compiler_params=params(),
        name="backward",
    )(index, returned, odd_part, table["last_back"], table["second"], table["modes"])
    got = lax.ppermute(send, "gx", swap)
    fixed, drift = pl.pallas_call(
        functools.partial(update_kernel, plan),
        out_shape=(shape_of(54, rows, LANES), shape_of(1)),
        in_specs=[scalar_spec()] + [whole_spec()] * 3,
        out_specs=(pl.BlockSpec(memory_space=pltpu.HBM), scalar_spec()),
        scratch_shapes=[
            pltpu.VMEM((18, rows + 16, LANES), jnp.float32),
            pltpu.VMEM((18, rows, LANES), jnp.float32),
            pltpu.VMEM((54, rows, LANES), jnp.float32),
            pltpu.SemaphoreType.DMA((5,)),
        ],
        compiler_params=params(),
        name="update",
    )(index, keep, got, links)
    return fixed.reshape(gauge_links.shape), drift


def solution(mesh):
    in_specs = (P(None, None, None, None, ("ta", "gx"), None),)
    out_specs = (P(None, None, None, None, ("ta", "gx"), None), P("ta"))
    return jax.shard_map(local, mesh=mesh, in_specs=in_specs, out_specs=out_specs, check_vma=False)
```

```python
import functools
import math

import jax
import jax.numpy as jnp
import numpy as np
from jax import lax
from jax.experimental import pallas as pl
from jax.experimental.pallas import tpu as pltpu
from jax.sharding import PartitionSpec as P

SIDE = 96
LANES = 128

step_size = 0.08
peak_square = 12.0
gain = 0.5 * step_size * peak_square

params = functools.partial(pltpu.CompilerParams, vmem_limit_bytes=48 * 1024 * 1024)
drift_weights = (1.5, 0.5, 2.0, 2.0, 2.0, 2.0, 2.0, 2.0)


class Plan:
    def __init__(self, count_x, side):
        self.count_x, self.side = count_x, side
        self.cells = side * side
        self.rows = self.cells // LANES
        self.period = side * LANES // math.gcd(side, LANES)
        self.wide = self.period // LANES
        self.folds = self.period // side
        self.groups = self.cells // self.period
        self.pairs = count_x // 2
        self.share = side // self.pairs
        self.full = self.share // 8 * 8
        self.rest = self.share - self.full
        self.tiles = 4 * side // LANES
        self.block = self.tiles * self.share
        self.sent = -(-2 * self.block // 8) * 8
        half = self.pairs // 2
        there = [(p + half) % self.pairs for p in range(self.pairs)]
        back = [p ^ (1 - half % 2) for p in range(half, self.pairs)] + list(range(half))[::-1]
        self.place = [there.index(p) for p in range(self.pairs)]
        self.back_place = [back.index(p) for p in range(self.pairs)]
        self.returned = -(-(2 * self.block + 8) // 8) * 8


def fourier(length):
    site = np.arange(length)
    basis = np.zeros((length, length))
    for k in range(length):
        angle = 2.0 * math.pi * (k * site % length) / length
        if k == 0 or 2 * k == length:
            basis[k] = np.cos(angle) / math.sqrt(length)
        elif 2 * k < length:
            basis[k] = np.cos(angle) * math.sqrt(2.0 / length)
        else:
            basis[k] = np.sin(angle) * math.sqrt(2.0 / length)
    return basis


def eigen(length):
    return 4.0 * np.sin(math.pi * np.arange(length) / length) ** 2


def split_table(table):
    high = table.astype(jnp.bfloat16)
    low = (table - high.astype(np.float64)).astype(jnp.bfloat16)
    return np.stack([high, low])


def stack_table(table):
    high, low = split_table(table)
    return np.block([[high, high], [low, np.zeros_like(low)]])


def tables(plan):
    side, folds, groups = plan.side, plan.folds, plan.groups
    basis = fourier(side)
    last = np.zeros((folds, side, folds, LANES))
    for j in range(folds):
        last[j, :, j, :side] = basis.T
    last = last.reshape(folds * side, folds * LANES)
    order = [plan.share * j + i for j in range(plan.pairs) for i in range(plan.full)]
    order += [plan.share * j + plan.full + i for j in range(plan.pairs) for i in range(plan.rest)]
    columns = [folds * g + j for j in range(folds) for g in range(groups)]
    second = basis[order][:, columns]
    value = eigen(side)
    inverse_side = np.zeros((side, LANES))
    inverse_side[:, :side] = 1.0 / (2.0 + value[order][:, None] + value[None, :])
    return {
        "last": np.stack([split_table(last[a:b, c:d]) for a, b, c, d in bands(plan)]),
        "last_back": np.stack([split_table(last[a:b, c:d].T) for a, b, c, d in bands(plan)]),
        "second": np.stack([stack_table(second), stack_table(second.T)]),
        "modes": inverse_side.astype(np.float32),
    }


def halve(value):
    high = value.astype(jnp.bfloat16)
    low = (value - high.astype(jnp.float32)).astype(jnp.bfloat16)
    return high, low


def product(left, right):
    dot = functools.partial(jnp.dot, preferred_element_type=jnp.float32)
    both = dot(jnp.concatenate(left, axis=0), right[0])
    size = left[0].shape[0]
    return both[:size] + (both[size:] + dot(left[0], right[1]))


def stacked(table, value):
    both = jnp.dot(table, jnp.concatenate(halve(value), axis=0), preferred_element_type=jnp.float32)
    size = both.shape[0] // 2
    return both[:size] + both[size:]


def bands(plan):
    for j in range(0, plan.folds, 2):
        rows = min(2, plan.folds - j)
        begin, end = j * plan.side // LANES, -(-(j + rows) * plan.side // LANES)
        yield begin * LANES, end * LANES, j * LANES, (j + rows) * LANES


def lane_of(shape):
    return lax.broadcasted_iota(jnp.int32, shape, 1)


def moved(ref, field, start, size, distance):
    down, over = distance // LANES, distance % LANES
    here = ref[field, pl.ds(start + down, size), :]
    after = ref[field, pl.ds(start + down + 1, size), :]
    mixed = jnp.where(lane_of(here.shape) >= over, here, after)
    return pltpu.roll(mixed, LANES - over, 1)


def last_index(rows, side):
    row = lax.broadcasted_iota(jnp.int32, (rows, LANES), 0)
    return (row * LANES + lane_of((rows, LANES))) % side


def wrap(ref, field, rows):
    ref[field, pl.ds(0, 8), :] = ref[field, pl.ds(rows, 8), :]
    ref[field, pl.ds(8 + rows, 8), :] = ref[field, pl.ds(8, 8), :]


def projected(links, d):
    def entry(part, i, j):
        return links[((d * 2 + part) * 3 + i) * 3 + j]

    im00, im11, im22 = entry(1, 0, 0), entry(1, 1, 1), entry(1, 2, 2)
    fields = [(im00 + im11 - 2.0 * im22) * (1.0 / 3.0), im00 - im11]
    for i, j in ((0, 1), (0, 2), (1, 2)):
        fields.append(0.5 * (entry(0, i, j) - entry(0, j, i)))
        fields.append(0.5 * (entry(1, i, j) + entry(1, j, i)))
    return fields


def link_copies(links_ref, staged, semaphores):
    copies = []
    for n, d in enumerate((1, 2, 0)):
        for m, (begin, size) in enumerate(((1, 3), (5, 3), (9, 9))):
            place = pl.ds(d * 18 + begin, size)
            copies.append(
                pltpu.make_async_copy(links_ref.at[place], staged.at[place], semaphores.at[n, m])
            )
    return copies


def divergence_kernel(
    plan, index_ref, links_ref, keep_ref, send_ref, ahead_ref, staged, second, third, semaphores
):
    rows, side = plan.rows, plan.side
    copies = link_copies(links_ref, staged, semaphores)
    for copy in copies:
        copy.start()
    odd = index_ref[0] % 2
    at_start = last_index(rows, side) == 0
    middle = pl.ds(8, rows)
    for copy in copies[:3]:
        copy.wait()
    for f, value in enumerate(projected(staged, 1)):
        second[f, middle, :] = value
        wrap(second, f, rows)
    diverge = [moved(second, f, 8, rows, -side) - second[f, middle, :] for f in range(8)]
    for copy in copies[3:6]:
        copy.wait()
    for f, value in enumerate(projected(staged, 2)):
        third[f, middle, :] = value
        wrap(third, f, rows)
    for f in range(8):
        beside = jnp.where(
            at_start, moved(third, f, 8, rows, side - 1), moved(third, f, 8, rows, -1)
        )
        diverge[f] = diverge[f] + (beside - third[f, middle, :])
        second[f, middle, :] = diverge[f]
    for copy in copies[6:]:
        copy.wait()
    direct = projected(staged, 0)
    index = index_ref[0]
    for f in range(8):
        place = pl.ds(f * rows, rows)
        total = second[f, middle, :] - direct[f]
        ahead_ref[place, :] = jnp.where(index == plan.count_x - 1, direct[f], total)
    for f in range(4):
        for part in range(2):
            place = pl.ds((part * 4 + f) * rows, rows)
            low, high = direct[f], direct[4 + f]
            if part == 0:
                low, high = second[f, middle, :] - low, second[4 + f, middle, :] - high
            keep_ref[place, :] = jnp.where(odd == 0, low, high)
            send_ref[place, :] = jnp.where(odd == 0, high, low)


def forward_kernel(
    plan, index_ref, keep_ref, got_ref, last_ref, second_ref, modes_ref, sent_ref, odd_ref, drift_ref
):
    rows, groups, folds, side = plan.rows, plan.groups, plan.folds, plan.side
    odd = index_ref[0] % 2
    quad = 4 * rows
    count = 4 * groups
    square = jnp.zeros((8, LANES), jnp.float32)
    wide = []
    for s in range(plan.wide):
        own_d, own_a, got_d, got_a = [
            ref[pl.ds(begin + s, count, stride=plan.wide), :]
            for ref in (keep_ref, got_ref)
            for begin in (0, quad)
        ]
        even_d, odd_d = jnp.where(odd == 0, own_d, got_d), jnp.where(odd == 0, got_d, own_d)
        even_a, odd_a = jnp.where(odd == 0, own_a, got_a), jnp.where(odd == 0, got_a, own_a)
        whole = odd_d + even_a
        for f in range(4):
            part = whole[f * groups : (f + 1) * groups]
            square = square + sum_tiles(part * part) * jnp.where(
                odd == 0, drift_weights[f], drift_weights[4 + f]
            )
        wide.append(jnp.concatenate([even_d, whole, odd_a], axis=0))
    drift_ref[...] = square
    wide = jnp.concatenate(wide, axis=1)
    high, low = halve(wide)
    waves = jnp.concatenate(
        [
            product(
                (high[:, begin:end], low[:, begin:end]),
                (last_ref[n, 0], last_ref[n, 1]),
            )
            for n, (begin, end, _, _) in enumerate(bands(plan))
        ],
        axis=1,
    )
    columns = []
    for pf in range(12):
        part = waves[pf * groups : (pf + 1) * groups]
        columns.append(
            jnp.concatenate([part[:, j * LANES : (j + 1) * LANES] for j in range(folds)], axis=0)
        )
    modes = stacked(second_ref[0], jnp.concatenate(columns, axis=1))
    inverse = modes_ref[:side]
    full, rest, pairs, tiles = plan.full, plan.rest, plan.pairs, plan.tiles
    lane = lane_of((side, LANES))
    zero = (lane == 0) & (lax.broadcasted_iota(jnp.int32, (side, LANES), 0) == 0)
    even, between, after = [
        [modes[:, (q * 4 + f) * LANES : (q * 4 + f + 1) * LANES] for f in range(4)] for q in range(3)
    ]
    shared = [value * inverse for value in between]
    for f in range(4):
        odd_ref[:, f * LANES : (f + 1) * LANES] = gain * shared[f]
    below = [even[f] + shared[f] for f in range(4)]
    above = [jnp.where(zero, between[f], after[f] + shared[f]) for f in range(4)]
    for q, fields in enumerate((below, above)):
        for t, value in enumerate(pack(fields, lane, side)):
            at = q * tiles + t
            for j in range(pairs):
                if full:
                    sent_ref[plan.place[j], pl.ds(at * full, full), :] = value[j * full : (j + 1) * full]
                if rest:
                    begin = pairs * full + j * rest
                    sent_ref[plan.place[j], pl.ds(2 * tiles * full + at * rest, rest), :] = value[
                        begin : begin + rest
                    ]
    spare = plan.sent - 2 * plan.block
    if spare:
        sent_ref[:, pl.ds(2 * plan.block, spare), :] = jnp.zeros((pairs, spare, LANES), jnp.float32)


def sum_tiles(value):
    total = value[:8]
    for i in range(1, value.shape[0] // 8):
        total = total + value[i * 8 : (i + 1) * 8]
    return total


def pack(fields, lane, side):
    rolled = [
        value if f * side % LANES == 0 else pltpu.roll(value, f * side % LANES, 1)
        for f, value in enumerate(fields)
    ]
    packed = []
    for t in range(4 * side // LANES):
        value = None
        for f in range(4):
            if f * side < (t + 1) * LANES and (f + 1) * side > t * LANES:
                value = rolled[f] if value is None else jnp.where(lane >= f * side - t * LANES, rolled[f], value)
        packed.append(value)
    return packed


def unpack(packed, lane, side):
    fields = []
    for f in range(4):
        begin = f * side // LANES
        end = ((f + 1) * side - 1) // LANES
        offset = f * side % LANES
        value = packed[begin]
        if end != begin:
            value = jnp.where(lane >= offset, packed[begin], packed[end])
        if offset:
            value = pltpu.roll(value, LANES - offset, 1)
        fields.append(jnp.where(lane < side, value, 0.0))
    return fields


def eigenvalues(plan, first, size):
    side = plan.side
    row = lax.broadcasted_iota(jnp.int32, (plan.tiles * size, LANES), 0)
    tile = row // size
    total = 0.0
    for mode in (first + row - tile * size, (tile * LANES + lane_of(row.shape)) % side):
        near = jnp.minimum(mode, side - mode).astype(jnp.float32)
        sine = jnp.sin(near * (math.pi / side))
        total = total + 4.0 * sine * sine
    return total


def drift_kernel(
    plan, index_ref, odd_ref, beside_ref, keep_ref, send_ref, links_ref, drift_ref, turns_ref, own_ref, loaded, arrivals
):
    rows, count_x = plan.rows, plan.count_x
    loads = []
    for d in range(3):
        place = pl.ds(d * 18, 18)
        loads.append(pltpu.make_async_copy(links_ref.at[place], loaded.at[place], arrivals.at[d]))
        loads[d].start()
    index = index_ref[0]
    square = jnp.zeros((rows, LANES), jnp.float32)
    part = jnp.where(index == 0, 0, 4 * rows)
    for f in range(4):
        place = pl.ds(pl.multiple_of(part + f * rows, 8), rows)
        own, other = keep_ref[place, :], send_ref[place, :]
        low, high = jnp.where(index % 2 == 0, own, other), jnp.where(index % 2 == 0, other, own)
        for n, value in ((f, low), (4 + f, high)):
            total = beside_ref[pl.ds(n * rows, rows), :] + value
            square = square + total * total * drift_weights[n]
    complete = (index == 0) | ((index % 2 == 1) & (index < count_x - 1))
    drift_ref[...] = odd_ref[...] + jnp.where(complete, sum_tiles(square), 0.0)
    for start, size in ((0, plan.full), (plan.full, plan.rest)):
        if size:
            own_ref[pl.ds(plan.tiles * start, plan.tiles * size), :] = eigenvalues(
                plan, index // 2 * plan.share + start, size
            )
    for d in range(3):
        loads[d].wait()
        link = [[tuple(loaded[((d * 2 + part) * 3 + r) * 3 + c] for part in range(2)) for c in range(3)] for r in range(3)]
        value = add(*[times(link[0][c], cross(link[1], link[2], c)) for c in range(3)])
        for part in range(2):
            turns_ref[d * 2 + part] = value[part]


def filter_kernel(plan, index_ref, got_ref, drift_ref, own_ref, back_ref):
    pairs, tiles, count_x = plan.pairs, plan.tiles, plan.count_x
    half = pairs // 2
    drift = drift_ref[...]
    for part, (size, first) in enumerate(((plan.full, 0), (plan.rest, 2 * tiles * plan.full))):
        if not size:
            continue
        length = tiles * size
        value = own_ref[pl.ds(part * tiles * plan.full, length), :]
        low, high = pl.ds(first, length), pl.ds(first + length, length)
        inside = value > 0
        below = [got_ref[plan.place[p], low, :] for p in range(pairs)]
        above = [got_ref[plan.place[p], high, :] for p in range(pairs)]
        rhs = [
            below[p] + jnp.where(inside, above[(p - 1) % pairs], -below[(p - 1) % pairs])
            for p in range(pairs)
        ]
        plus = [rhs[d] + rhs[pairs - d] for d in range(1, half)]
        minus = [rhs[d] - rhs[pairs - d] for d in range(1, half)]
        cosines, sines = [], []
        for k in range(half + 1):
            total = rhs[0] + rhs[half] if k % 2 == 0 else rhs[0] - rhs[half]
            for d in range(1, half):
                total = total + plus[d - 1] * math.cos(2 * math.pi * (k * d % pairs) / pairs)
            root = 4.0 * math.sin(math.pi * k / count_x) ** 2
            split = (value + root) * (value + (4.0 - root))
            scale = gain / pairs * (1.0 if k in (0, half) else 2.0)
            if k == 0:
                factor = jnp.where(inside, scale * (2.0 + value) / jnp.where(inside, split, 1.0), 0.0)
                whole = above[0]
                for p in range(1, pairs):
                    whole = whole + above[p]
                mean = jnp.where(inside, 0.0, whole * (-0.25 * gain / pairs))
                cosines.append(total * factor + mean)
            else:
                factor = scale * (2.0 + value) / split
                cosines.append(total * factor)
                if k < half:
                    wave = jnp.zeros_like(value)
                    for d in range(1, half):
                        wave = wave + minus[d - 1] * math.sin(2 * math.pi * (k * d % pairs) / pairs)
                    sines.append(wave * factor)
        results = [None] * pairs
        for d in range(half + 1):
            even = cosines[0]
            for k in range(1, half + 1):
                even = even + cosines[k] * math.cos(2 * math.pi * (k * d % pairs) / pairs)
            if d in (0, half):
                results[d] = even
            else:
                wave = jnp.zeros_like(value)
                for k in range(1, half):
                    wave = wave + sines[k - 1] * math.sin(2 * math.pi * (k * d % pairs) / pairs)
                results[d] = even + wave
                results[pairs - d] = even - wave
        for p in range(pairs):
            back_ref[plan.back_place[p], low, :] = results[p]
            back_ref[plan.back_place[p], high, :] = results[(p + 1) % pairs]
    for p in range(pairs):
        back_ref[p, pl.ds(2 * plan.block, 8), :] = drift


def backward_kernel(
    plan, index_ref, got_ref, odd_ref, last_ref, second_ref, modes_ref, keep_ref, send_ref, packed
):
    rows, groups, folds, side = plan.rows, plan.groups, plan.folds, plan.side
    full, rest, pairs, tiles = plan.full, plan.rest, plan.pairs, plan.tiles
    odd = index_ref[0] % 2
    for q in range(2):
        for t in range(tiles):
            at = q * tiles + t
            for j in range(pairs):
                if full:
                    packed[at, pl.ds(j * full, full), :] = got_ref[plan.back_place[j], pl.ds(at * full, full), :]
                if rest:
                    packed[at, pl.ds(pairs * full + j * rest, rest), :] = got_ref[
                        plan.back_place[j], pl.ds(2 * tiles * full + at * rest, rest), :
                    ]
    lane = lane_of((side, LANES))
    inverse = modes_ref[:side]
    even, after = [
        unpack([packed[q * tiles + t] for t in range(tiles)], lane, side) for q in range(2)
    ]
    between = [
        odd_ref[:, f * LANES : (f + 1) * LANES] + (even[f] + after[f]) * inverse for f in range(4)
    ]
    waves = stacked(second_ref[1], jnp.concatenate(even + between + after, axis=1))
    blocks = []
    for pf in range(12):
        part = waves[:, pf * LANES : (pf + 1) * LANES]
        blocks.append(
            jnp.concatenate([part[j * groups : (j + 1) * groups] for j in range(folds)], axis=1)
        )
    high, low = halve(jnp.concatenate(blocks, axis=0))
    wide = [None] * plan.wide
    for n, (begin, end, first, last) in enumerate(bands(plan)):
        part = product(
            (high[:, first:last], low[:, first:last]), (last_ref[n, 0], last_ref[n, 1])
        )
        for s in range(begin // LANES, end // LANES):
            tile = part[:, s * LANES - begin : (s + 1) * LANES - begin]
            wide[s] = tile if wide[s] is None else wide[s] + tile
    quad, count = 4 * rows, 4 * groups
    for s in range(plan.wide):
        low, middle, high = [wide[s][q * count : (q + 1) * count] for q in range(3)]
        here, ahead = pl.ds(s, count, stride=plan.wide), pl.ds(quad + s, count, stride=plan.wide)
        keep_ref[here, :] = jnp.where(odd == 0, low, middle)
        keep_ref[ahead, :] = jnp.where(odd == 0, middle, high)
        send_ref[here, :] = jnp.where(odd == 0, middle, low)
        send_ref[ahead, :] = jnp.where(odd == 0, high, middle)
    drift = got_ref[0, pl.ds(2 * plan.block, 8), :]
    for j in range(1, pairs):
        drift = drift + got_ref[j, pl.ds(2 * plan.block, 8), :]
    keep_ref[pl.ds(2 * quad, 8), :] = drift
    send_ref[pl.ds(2 * quad, 8), :] = drift


def times(left, right):
    return (left[0] * right[0] - left[1] * right[1], left[0] * right[1] + left[1] * right[0])


def times_conj(left, right):
    return (left[0] * right[0] + left[1] * right[1], left[1] * right[0] - left[0] * right[1])


def rotation(fields):
    both, apart = fields[0], fields[1]
    a, b, e = 0.5 * (both + apart), 0.5 * (both - apart), -both
    u, v, w = (fields[2], fields[3]), (fields[4], fields[5]), (fields[6], fields[7])
    square = [x[0] * x[0] + x[1] * x[1] for x in (u, v, w)]
    a00, a11, a22 = square[2] - b * e, square[1] - a * e, square[0] - a * b
    vw, uw, vu = times_conj(v, w), times(u, w), times_conj(v, u)
    a01 = (e * u[1] - vw[0], -(e * u[0]) - vw[1])
    a02 = (uw[0] + b * v[1], uw[1] - b * v[0])
    a12 = (a * w[1] - vu[0], -(a * w[0]) - vu[1])
    turn = a * a00 + times_conj(u, a01)[1] + times_conj(v, a02)[1]
    real = 1.0 + (a00 + a11 + a22)
    scale = 2.0 / (real * real + turn * turn)
    factor = (real * scale, turn * scale)
    entries = [[None] * 3 for _ in range(3)]
    for i, (up, imag) in enumerate(((a00, a), (a11, b), (a22, e))):
        value = times((1.0 + up, imag), factor)
        entries[i][i] = (value[0] - 1.0, value[1])
    for (i, j), up, off in (((0, 1), a01, u), ((0, 2), a02, v), ((1, 2), a12, w)):
        entries[i][j] = times((up[0] + off[0], up[1] + off[1]), factor)
        entries[j][i] = times((up[0] - off[0], off[1] - up[1]), factor)
    whole = (0.5 * (real * factor[0] - turn * factor[1]), real * factor[1])
    return [entries[i][j][part] for part in range(2) for i in range(3) for j in range(3)] + list(whole)


def update_kernel(
    plan, index_ref, keep_ref, got_ref, links_ref, turns_ref, fixed_ref, drift_ref, here, along, staged, semaphores
):
    rows, side = plan.rows, plan.side
    quad = 4 * rows
    odd = index_ref[0] % 2

    def turn(i, _):
        begin = pl.multiple_of(i * 8, 8)
        for q, lead in ((0, 8), (1, 0)):
            fields = [None] * 8
            for f in range(4):
                place = pl.ds(pl.multiple_of(q * quad + f * rows + begin, 8), 8)
                own, other = keep_ref[place, :], got_ref[place, :]
                fields[f] = jnp.where(odd == 0, own, other)
                fields[4 + f] = jnp.where(odd == 0, other, own)
            for n, value in enumerate(rotation(fields)):
                if q == 0:
                    here[n, pl.ds(begin + lead, 8), :] = value
                else:
                    along[n, pl.ds(begin, 8), :] = value
        return 0

    lax.fori_loop(0, rows // 8, turn, 0, unroll=3)

    def update(d, i):
        begin = i * 8

        def matrix(read):
            value = [read(n) for n in range(18)]
            return [[(value[3 * r + c], value[9 + 3 * r + c]) for c in range(3)] for r in range(3)]

        if d == 0:

            def shifted(n):
                return along[n, pl.ds(begin, 8), :]

        elif d == 1:

            def shifted(n):
                return moved(here, n, 8 + begin, 8, side)

        else:
            at_end = (last_index(8, side) + begin * LANES) % side == side - 1

            def shifted(n):
                return jnp.where(
                    at_end,
                    moved(here, n, 8 + begin, 8, 1 - side),
                    moved(here, n, 8 + begin, 8, 1),
                )

        def own(r, c):
            return tuple(here[9 * part + 3 * r + c, pl.ds(begin + 8, 8), :] for part in range(2))

        links = matrix(lambda n: links_ref[d * 18 + n, pl.ds(begin, 8), :])
        ahead = matrix(shifted)
        moved_rows = []
        for r in range(2):
            left = [own(r, k) for k in range(3)]
            line = [add(*[times(left[k], links[k][c]) for k in range(3)]) for c in range(3)]
            moved_rows.append(
                [add(*[times_conj(line[k], ahead[c][k]) for k in range(3)]) for c in range(3)]
            )
        whole = tuple(turns_ref[d * 2 + part, pl.ds(begin, 8), :] for part in range(2))
        whole = times(whole, tuple(here[18 + part, pl.ds(begin + 8, 8), :] for part in range(2)))
        whole = times_conj(whole, (shifted(18), shifted(19)))
        moved_rows.append([times_conj(whole, cross(*moved_rows, c)) for c in range(3)])
        for r in range(3):
            for c in range(3):
                for part in range(2):
                    staged[d * 18 + part * 9 + r * 3 + c, pl.ds(begin, 8), :] = moved_rows[r][c][part]

    tiles = rows // 8
    copies = []

    def write(place, rows_place, n):
        copy = pltpu.make_async_copy(
            staged.at[place, rows_place], fixed_ref.at[place, rows_place], semaphores.at[n]
        )
        copy.start()
        copies.append(copy)

    for n in range(20):
        wrap(here, n, rows)
    for d in (1, 2, 0):
        chunks = 1 if d else 3
        for m in range(chunks):
            part = tiles // chunks

            for i in range(m * part, (m + 1) * part):
                update(d, i)
            write(pl.ds(d * 18, 18), pl.ds(m * part * 8, part * 8), len(copies))
    total = keep_ref[pl.ds(2 * quad, 8), :] + got_ref[pl.ds(2 * quad, 8), :]
    drift_ref[0] = jnp.sum(total) * (1.0 / (9.0 * plan.count_x * plan.cells))
    for copy in copies:
        copy.wait()


def cross(first, second, c):
    one = times(first[(c + 1) % 3], second[(c + 2) % 3])
    two = times(first[(c + 2) % 3], second[(c + 1) % 3])
    return (one[0] - two[0], one[1] - two[1])


def add(first, second, third):
    return (first[0] + second[0] + third[0], first[1] + second[1] + third[1])


def whole_spec():
    return pl.BlockSpec(memory_space=pltpu.VMEM)


def scalar_spec():
    return pl.BlockSpec(memory_space=pltpu.SMEM)


def shape_of(*shape):
    return jax.ShapeDtypeStruct(shape, jnp.float32)


def local(gauge_links):
    count_x = lax.axis_size("gx")
    plan = Plan(count_x, SIDE)
    rows, pairs = plan.rows, plan.pairs
    table = tables(plan)
    index = lax.axis_index("gx").astype(jnp.int32).reshape(1)
    links = gauge_links.reshape(54, rows, LANES)
    held = pltpu.with_memory_space_constraint(links, pltpu.HBM)
    quads = 8 * rows
    swap = [(i, i ^ 1) for i in range(count_x)]
    halo = [(2 * p, 2 * p - 1) for p in range(1, pairs)] + [(count_x - 1, 0)]
    same_core, same_core_back = [
        [[c + 2 * p for p in sorted(range(pairs), key=place.__getitem__)] for c in range(2)]
        for place in (plan.place, plan.back_place)
    ]

    keep, send, ahead = pl.pallas_call(
        functools.partial(divergence_kernel, plan),
        out_shape=(shape_of(quads, LANES),) * 3,
        in_specs=[scalar_spec(), pl.BlockSpec(memory_space=pltpu.HBM)],
        out_specs=(whole_spec(),) * 3,
        scratch_shapes=[
            pltpu.VMEM((54, rows, LANES), jnp.float32),
            pltpu.VMEM((8, rows + 16, LANES), jnp.float32),
            pltpu.VMEM((8, rows + 16, LANES), jnp.float32),
            pltpu.SemaphoreType.DMA((3, 3)),
        ],
        compiler_params=params(),
        name="divergence",
    )(index, held)
    got = lax.ppermute(send, "gx", swap)
    beside = lax.ppermute(ahead, "gx", halo)
    sent, odd_part, odd_drift = pl.pallas_call(
        functools.partial(forward_kernel, plan),
        out_shape=(
            shape_of(pairs, plan.sent, LANES),
            shape_of(SIDE, 4 * LANES),
            shape_of(8, LANES),
        ),
        in_specs=[scalar_spec()] + [whole_spec()] * 5,
        out_specs=(whole_spec(),) * 3,
        compiler_params=params(),
        name="forward",
    )(index, keep, got, table["last"], table["second"], table["modes"])
    arrived = lax.all_to_all(
        sent, "gx", split_axis=0, concat_axis=0, tiled=True, axis_index_groups=same_core
    )
    drift_part, turns, own_modes = pl.pallas_call(
        functools.partial(drift_kernel, plan),
        out_shape=(shape_of(8, LANES), shape_of(6, rows, LANES), shape_of(plan.block, LANES)),
        in_specs=[scalar_spec()] + [whole_spec()] * 4 + [pl.BlockSpec(memory_space=pltpu.HBM)],
        out_specs=(whole_spec(),) * 3,
        scratch_shapes=[pltpu.VMEM((54, rows, LANES), jnp.float32), pltpu.SemaphoreType.DMA((3,))],
        compiler_params=params(),
        cost_estimate=pl.CostEstimate(flops=5 * 10**10, bytes_accessed=5 * 10**7, transcendentals=0),
        name="drift",
    )(index, odd_drift, beside, keep, send, held)
    back = pl.pallas_call(
        functools.partial(filter_kernel, plan),
        out_shape=shape_of(pairs, plan.returned, LANES),
        in_specs=[scalar_spec()] + [whole_spec()] * 3,
        out_specs=whole_spec(),
        compiler_params=params(),
        name="filter",
    )(index, arrived, drift_part, own_modes)
    returned = lax.all_to_all(
        back, "gx", split_axis=0, concat_axis=0, tiled=True, axis_index_groups=same_core_back
    )
    keep, send = pl.pallas_call(
        functools.partial(backward_kernel, plan),
        out_shape=(shape_of(quads + 8, LANES), shape_of(quads + 8, LANES)),
        in_specs=[scalar_spec()] + [whole_spec()] * 5,
        out_specs=(whole_spec(), whole_spec()),
        scratch_shapes=[
            pltpu.VMEM((2 * plan.tiles, SIDE, LANES), jnp.float32),
        ],
        compiler_params=params(),
        name="backward",
    )(index, returned, odd_part, table["last_back"], table["second"], table["modes"])
    got = lax.ppermute(send, "gx", swap)
    fixed, drift = pl.pallas_call(
        functools.partial(update_kernel, plan),
        out_shape=(shape_of(54, rows, LANES), shape_of(1)),
        in_specs=[scalar_spec()] + [whole_spec()] * 4,
        out_specs=(pl.BlockSpec(memory_space=pltpu.HBM), scalar_spec()),
        scratch_shapes=[
            pltpu.VMEM((20, rows + 16, LANES), jnp.float32),
            pltpu.VMEM((20, rows, LANES), jnp.float32),
            pltpu.VMEM((54, rows, LANES), jnp.float32),
            pltpu.SemaphoreType.DMA((5,)),
        ],
        compiler_params=params(),
        name="update",
    )(index, keep, got, links, turns)
    return fixed.reshape(gauge_links.shape), drift


def solution(mesh):
    in_specs = (P(None, None, None, None, ("ta", "gx"), None),)
    out_specs = (P(None, None, None, None, ("ta", "gx"), None), P("ta"))
    return jax.shard_map(local, mesh=mesh, in_specs=in_specs, out_specs=out_specs, check_vma=False)
```

```python
import functools
import math

import jax
import jax.numpy as jnp
import numpy as np
from jax import lax
from jax.experimental import pallas as pl
from jax.experimental.pallas import tpu as pltpu
from jax.sharding import PartitionSpec as P

SIDE = 96
LANES = 128

step_size = 0.08
peak_square = 12.0
gain = 0.5 * step_size * peak_square

params = functools.partial(pltpu.CompilerParams, vmem_limit_bytes=48 * 1024 * 1024)
drift_weights = (1.5, 0.5, 2.0, 2.0, 2.0, 2.0, 2.0, 2.0)


class Plan:
    def __init__(self, count_x, side):
        self.count_x, self.side = count_x, side
        self.cells = side * side
        self.rows = self.cells // LANES
        self.period = side * LANES // math.gcd(side, LANES)
        self.wide = self.period // LANES
        self.folds = self.period // side
        self.groups = self.cells // self.period
        self.pairs = count_x // 2
        self.share = side // self.pairs
        self.full = self.share // 8 * 8
        self.rest = self.share - self.full
        self.tiles = 4 * side // LANES
        self.block = self.tiles * self.share
        self.sent = -(-2 * self.block // 8) * 8
        half = self.pairs // 2
        there = [(p + half) % self.pairs for p in range(self.pairs)]
        back = [p ^ (1 - half % 2) for p in range(half, self.pairs)] + list(range(half))[::-1]
        self.place = [there.index(p) for p in range(self.pairs)]
        self.back_place = [back.index(p) for p in range(self.pairs)]
        self.returned = -(-(2 * self.block + 8) // 8) * 8


def fourier(length):
    site = np.arange(length)
    basis = np.zeros((length, length))
    for k in range(length):
        angle = 2.0 * math.pi * (k * site % length) / length
        if k == 0 or 2 * k == length:
            basis[k] = np.cos(angle) / math.sqrt(length)
        elif 2 * k < length:
            basis[k] = np.cos(angle) * math.sqrt(2.0 / length)
        else:
            basis[k] = np.sin(angle) * math.sqrt(2.0 / length)
    return basis


def eigen(length):
    return 4.0 * np.sin(math.pi * np.arange(length) / length) ** 2


def split_table(table):
    high = table.astype(jnp.bfloat16)
    low = (table - high.astype(np.float64)).astype(jnp.bfloat16)
    return np.stack([high, low])


def stack_table(table):
    high, low = split_table(table)
    return np.block([[high, high], [low, np.zeros_like(low)]])


def tables(plan):
    side, folds, groups = plan.side, plan.folds, plan.groups
    basis = fourier(side)
    last = np.zeros((folds, side, folds, LANES))
    for j in range(folds):
        last[j, :, j, :side] = basis.T
    last = last.reshape(folds * side, folds * LANES)
    order = [plan.share * j + i for j in range(plan.pairs) for i in range(plan.full)]
    order += [plan.share * j + plan.full + i for j in range(plan.pairs) for i in range(plan.rest)]
    columns = [folds * g + j for j in range(folds) for g in range(groups)]
    second = basis[order][:, columns]
    value = eigen(side)
    inverse_side = np.zeros((side, LANES))
    inverse_side[:, :side] = 1.0 / (2.0 + value[order][:, None] + value[None, :])
    return {
        "last": np.stack([split_table(last[a:b, c:d]) for a, b, c, d in bands(plan)]),
        "last_back": np.stack([split_table(last[a:b, c:d].T) for a, b, c, d in bands(plan)]),
        "second": np.stack([stack_table(second), stack_table(second.T)]),
        "modes": inverse_side.astype(np.float32),
    }


def halve(value):
    high = value.astype(jnp.bfloat16)
    low = (value - high.astype(jnp.float32)).astype(jnp.bfloat16)
    return high, low


def product(left, right):
    dot = functools.partial(jnp.dot, preferred_element_type=jnp.float32)
    both = dot(jnp.concatenate(left, axis=0), right[0])
    size = left[0].shape[0]
    return both[:size] + (both[size:] + dot(left[0], right[1]))


def stacked(table, value):
    both = jnp.dot(table, jnp.concatenate(halve(value), axis=0), preferred_element_type=jnp.float32)
    size = both.shape[0] // 2
    return both[:size] + both[size:]


def bands(plan):
    for j in range(0, plan.folds, 2):
        rows = min(2, plan.folds - j)
        begin, end = j * plan.side // LANES, -(-(j + rows) * plan.side // LANES)
        yield begin * LANES, end * LANES, j * LANES, (j + rows) * LANES


def lane_of(shape):
    return lax.broadcasted_iota(jnp.int32, shape, 1)


def moved(ref, field, start, size, distance):
    down, over = distance // LANES, distance % LANES
    here = ref[field, pl.ds(start + down, size), :]
    after = ref[field, pl.ds(start + down + 1, size), :]
    mixed = jnp.where(lane_of(here.shape) >= over, here, after)
    return pltpu.roll(mixed, LANES - over, 1)


def last_index(rows, side):
    row = lax.broadcasted_iota(jnp.int32, (rows, LANES), 0)
    return (row * LANES + lane_of((rows, LANES))) % side


def wrap(ref, field, rows):
    ref[field, pl.ds(0, 8), :] = ref[field, pl.ds(rows, 8), :]
    ref[field, pl.ds(8 + rows, 8), :] = ref[field, pl.ds(8, 8), :]


def projected(links, d):
    def entry(part, i, j):
        return links[((d * 2 + part) * 3 + i) * 3 + j]

    im00, im11, im22 = entry(1, 0, 0), entry(1, 1, 1), entry(1, 2, 2)
    fields = [(im00 + im11 - 2.0 * im22) * (1.0 / 3.0), im00 - im11]
    for i, j in ((0, 1), (0, 2), (1, 2)):
        fields.append(0.5 * (entry(0, i, j) - entry(0, j, i)))
        fields.append(0.5 * (entry(1, i, j) + entry(1, j, i)))
    return fields


def link_copies(links_ref, staged, semaphores):
    copies = []
    for n, d in enumerate((1, 2, 0)):
        for m, (begin, size) in enumerate(((1, 3), (5, 3), (9, 9))):
            place = pl.ds(d * 18 + begin, size)
            copies.append(
                pltpu.make_async_copy(links_ref.at[place], staged.at[place], semaphores.at[n, m])
            )
    return copies


def divergence_kernel(
    plan, index_ref, links_ref, keep_ref, send_ref, ahead_ref, staged, second, third, semaphores
):
    rows, side = plan.rows, plan.side
    copies = link_copies(links_ref, staged, semaphores)
    for copy in copies:
        copy.start()
    odd = index_ref[0] % 2
    at_start = last_index(rows, side) == 0
    middle = pl.ds(8, rows)
    for copy in copies[:3]:
        copy.wait()
    for f, value in enumerate(projected(staged, 1)):
        second[f, middle, :] = value
        wrap(second, f, rows)
    diverge = [moved(second, f, 8, rows, -side) - second[f, middle, :] for f in range(8)]
    for copy in copies[3:6]:
        copy.wait()
    for f, value in enumerate(projected(staged, 2)):
        third[f, middle, :] = value
        wrap(third, f, rows)
    for f in range(8):
        beside = jnp.where(
            at_start, moved(third, f, 8, rows, side - 1), moved(third, f, 8, rows, -1)
        )
        diverge[f] = diverge[f] + (beside - third[f, middle, :])
        second[f, middle, :] = diverge[f]
    for copy in copies[6:]:
        copy.wait()
    direct = projected(staged, 0)
    index = index_ref[0]
    for f in range(8):
        place = pl.ds(f * rows, rows)
        total = second[f, middle, :] - direct[f]
        ahead_ref[place, :] = jnp.where(index == plan.count_x - 1, direct[f], total)
    for f in range(4):
        for part in range(2):
            place = pl.ds((part * 4 + f) * rows, rows)
            low, high = direct[f], direct[4 + f]
            if part == 0:
                low, high = second[f, middle, :] - low, second[4 + f, middle, :] - high
            keep_ref[place, :] = jnp.where(odd == 0, low, high)
            send_ref[place, :] = jnp.where(odd == 0, high, low)


def forward_kernel(
    plan, index_ref, keep_ref, got_ref, last_ref, second_ref, modes_ref, sent_ref, odd_ref, drift_ref, staged, departures
):
    rows, groups, folds, side = plan.rows, plan.groups, plan.folds, plan.side
    odd = index_ref[0] % 2
    quad = 4 * rows
    count = 4 * groups
    square = jnp.zeros((8, LANES), jnp.float32)
    wide = []
    for s in range(plan.wide):
        own_d, own_a, got_d, got_a = [
            ref[pl.ds(begin + s, count, stride=plan.wide), :]
            for ref in (keep_ref, got_ref)
            for begin in (0, quad)
        ]
        even_d, odd_d = jnp.where(odd == 0, own_d, got_d), jnp.where(odd == 0, got_d, own_d)
        even_a, odd_a = jnp.where(odd == 0, own_a, got_a), jnp.where(odd == 0, got_a, own_a)
        whole = odd_d + even_a
        for f in range(4):
            part = whole[f * groups : (f + 1) * groups]
            square = square + sum_tiles(part * part) * jnp.where(
                odd == 0, drift_weights[f], drift_weights[4 + f]
            )
        wide.append(jnp.concatenate([even_d, whole, odd_a], axis=0))
    drift_ref[...] = square
    wide = jnp.concatenate(wide, axis=1)
    high, low = halve(wide)
    waves = jnp.concatenate(
        [
            product(
                (high[:, begin:end], low[:, begin:end]),
                (last_ref[n, 0], last_ref[n, 1]),
            )
            for n, (begin, end, _, _) in enumerate(bands(plan))
        ],
        axis=1,
    )
    columns = []
    for pf in range(12):
        part = waves[pf * groups : (pf + 1) * groups]
        columns.append(
            jnp.concatenate([part[:, j * LANES : (j + 1) * LANES] for j in range(folds)], axis=0)
        )
    modes = stacked(second_ref[0], jnp.concatenate(columns, axis=1))
    inverse = modes_ref[:side]
    full, rest, pairs, tiles = plan.full, plan.rest, plan.pairs, plan.tiles
    lane = lane_of((side, LANES))
    zero = (lane == 0) & (lax.broadcasted_iota(jnp.int32, (side, LANES), 0) == 0)
    even, between, after = [
        [modes[:, (q * 4 + f) * LANES : (q * 4 + f + 1) * LANES] for f in range(4)] for q in range(3)
    ]
    shared = [value * inverse for value in between]
    for f in range(4):
        odd_ref[:, f * LANES : (f + 1) * LANES] = gain * shared[f]
    below = [even[f] + shared[f] for f in range(4)]
    above = [jnp.where(zero, between[f], after[f] + shared[f]) for f in range(4)]
    early = tiles * full
    copies = []

    def leave(begin, size):
        place = (slice(None), pl.ds(begin, size))
        copy = pltpu.make_async_copy(staged.at[place], sent_ref.at[place], departures.at[len(copies)])
        copy.start()
        copies.append(copy)

    for q, fields in enumerate((below, above)):
        for t, value in enumerate(pack(fields, lane, side)):
            at = q * tiles + t
            for j in range(pairs):
                if full:
                    staged[plan.place[j], pl.ds(at * full, full), :] = value[j * full : (j + 1) * full]
                if rest:
                    begin = pairs * full + j * rest
                    staged[plan.place[j], pl.ds(2 * tiles * full + at * rest, rest), :] = value[
                        begin : begin + rest
                    ]
        if q == 0 and early:
            leave(0, early)
    spare = plan.sent - 2 * plan.block
    if spare:
        staged[:, pl.ds(2 * plan.block, spare), :] = jnp.zeros((pairs, spare, LANES), jnp.float32)
    leave(early, plan.sent - early)
    for copy in copies:
        copy.wait()


def sum_tiles(value):
    total = value[:8]
    for i in range(1, value.shape[0] // 8):
        total = total + value[i * 8 : (i + 1) * 8]
    return total


def pack(fields, lane, side):
    rolled = [
        value if f * side % LANES == 0 else pltpu.roll(value, f * side % LANES, 1)
        for f, value in enumerate(fields)
    ]
    packed = []
    for t in range(4 * side // LANES):
        value = None
        for f in range(4):
            if f * side < (t + 1) * LANES and (f + 1) * side > t * LANES:
                value = rolled[f] if value is None else jnp.where(lane >= f * side - t * LANES, rolled[f], value)
        packed.append(value)
    return packed


def unpack(packed, lane, side):
    fields = []
    for f in range(4):
        begin = f * side // LANES
        end = ((f + 1) * side - 1) // LANES
        offset = f * side % LANES
        value = packed[begin]
        if end != begin:
            value = jnp.where(lane >= offset, packed[begin], packed[end])
        if offset:
            value = pltpu.roll(value, LANES - offset, 1)
        fields.append(jnp.where(lane < side, value, 0.0))
    return fields


def eigenvalues(plan, first, size):
    side = plan.side
    row = lax.broadcasted_iota(jnp.int32, (plan.tiles * size, LANES), 0)
    tile = row // size
    total = 0.0
    for mode in (first + row - tile * size, (tile * LANES + lane_of(row.shape)) % side):
        near = jnp.minimum(mode, side - mode).astype(jnp.float32)
        sine = jnp.sin(near * (math.pi / side))
        total = total + 4.0 * sine * sine
    return total


def drift_kernel(
    plan, index_ref, odd_ref, beside_ref, keep_ref, send_ref, links_ref, drift_ref, turns_ref, own_ref, loaded, arrivals
):
    rows, count_x = plan.rows, plan.count_x
    loads = []
    for d in range(3):
        place = pl.ds(d * 18, 18)
        loads.append(pltpu.make_async_copy(links_ref.at[place], loaded.at[place], arrivals.at[d]))
        loads[d].start()
    index = index_ref[0]
    square = jnp.zeros((rows, LANES), jnp.float32)
    part = jnp.where(index == 0, 0, 4 * rows)
    for f in range(4):
        place = pl.ds(pl.multiple_of(part + f * rows, 8), rows)
        own, other = keep_ref[place, :], send_ref[place, :]
        low, high = jnp.where(index % 2 == 0, own, other), jnp.where(index % 2 == 0, other, own)
        for n, value in ((f, low), (4 + f, high)):
            total = beside_ref[pl.ds(n * rows, rows), :] + value
            square = square + total * total * drift_weights[n]
    complete = (index == 0) | ((index % 2 == 1) & (index < count_x - 1))
    drift_ref[...] = odd_ref[...] + jnp.where(complete, sum_tiles(square), 0.0)
    for start, size in ((0, plan.full), (plan.full, plan.rest)):
        if size:
            own_ref[pl.ds(plan.tiles * start, plan.tiles * size), :] = eigenvalues(
                plan, index // 2 * plan.share + start, size
            )
    for d in range(3):
        loads[d].wait()
        link = [[tuple(loaded[((d * 2 + part) * 3 + r) * 3 + c] for part in range(2)) for c in range(3)] for r in range(3)]
        value = add(*[times(link[0][c], cross(link[1], link[2], c)) for c in range(3)])
        for part in range(2):
            turns_ref[d * 2 + part] = value[part]


def filter_kernel(plan, index_ref, got_ref, drift_ref, own_ref, back_ref):
    pairs, tiles, count_x = plan.pairs, plan.tiles, plan.count_x
    half = pairs // 2
    drift = drift_ref[...]
    for part, (size, first) in enumerate(((plan.full, 0), (plan.rest, 2 * tiles * plan.full))):
        if not size:
            continue
        length = tiles * size
        value = own_ref[pl.ds(part * tiles * plan.full, length), :]
        low, high = pl.ds(first, length), pl.ds(first + length, length)
        inside = value > 0
        below = [got_ref[plan.place[p], low, :] for p in range(pairs)]
        above = [got_ref[plan.place[p], high, :] for p in range(pairs)]
        rhs = [
            below[p] + jnp.where(inside, above[(p - 1) % pairs], -below[(p - 1) % pairs])
            for p in range(pairs)
        ]
        plus = [rhs[d] + rhs[pairs - d] for d in range(1, half)]
        minus = [rhs[d] - rhs[pairs - d] for d in range(1, half)]
        cosines, sines = [], []
        for k in range(half + 1):
            total = rhs[0] + rhs[half] if k % 2 == 0 else rhs[0] - rhs[half]
            for d in range(1, half):
                total = total + plus[d - 1] * math.cos(2 * math.pi * (k * d % pairs) / pairs)
            root = 4.0 * math.sin(math.pi * k / count_x) ** 2
            split = (value + root) * (value + (4.0 - root))
            scale = gain / pairs * (1.0 if k in (0, half) else 2.0)
            if k == 0:
                factor = jnp.where(inside, scale * (2.0 + value) / jnp.where(inside, split, 1.0), 0.0)
                whole = above[0]
                for p in range(1, pairs):
                    whole = whole + above[p]
                mean = jnp.where(inside, 0.0, whole * (-0.25 * gain / pairs))
                cosines.append(total * factor + mean)
            else:
                factor = scale * (2.0 + value) / split
                cosines.append(total * factor)
                if k < half:
                    wave = jnp.zeros_like(value)
                    for d in range(1, half):
                        wave = wave + minus[d - 1] * math.sin(2 * math.pi * (k * d % pairs) / pairs)
                    sines.append(wave * factor)
        results = [None] * pairs
        for d in range(half + 1):
            even = cosines[0]
            for k in range(1, half + 1):
                even = even + cosines[k] * math.cos(2 * math.pi * (k * d % pairs) / pairs)
            if d in (0, half):
                results[d] = even
            else:
                wave = jnp.zeros_like(value)
                for k in range(1, half):
                    wave = wave + sines[k - 1] * math.sin(2 * math.pi * (k * d % pairs) / pairs)
                results[d] = even + wave
                results[pairs - d] = even - wave
        for p in range(pairs):
            back_ref[plan.back_place[p], low, :] = results[p]
            back_ref[plan.back_place[p], high, :] = results[(p + 1) % pairs]
    for p in range(pairs):
        back_ref[p, pl.ds(2 * plan.block, 8), :] = drift


def backward_kernel(
    plan, index_ref, got_ref, odd_ref, last_ref, second_ref, modes_ref, keep_ref, send_ref, packed
):
    rows, groups, folds, side = plan.rows, plan.groups, plan.folds, plan.side
    full, rest, pairs, tiles = plan.full, plan.rest, plan.pairs, plan.tiles
    odd = index_ref[0] % 2
    for q in range(2):
        for t in range(tiles):
            at = q * tiles + t
            for j in range(pairs):
                if full:
                    packed[at, pl.ds(j * full, full), :] = got_ref[plan.back_place[j], pl.ds(at * full, full), :]
                if rest:
                    packed[at, pl.ds(pairs * full + j * rest, rest), :] = got_ref[
                        plan.back_place[j], pl.ds(2 * tiles * full + at * rest, rest), :
                    ]
    lane = lane_of((side, LANES))
    inverse = modes_ref[:side]
    even, after = [
        unpack([packed[q * tiles + t] for t in range(tiles)], lane, side) for q in range(2)
    ]
    between = [
        odd_ref[:, f * LANES : (f + 1) * LANES] + (even[f] + after[f]) * inverse for f in range(4)
    ]
    waves = stacked(second_ref[1], jnp.concatenate(even + between + after, axis=1))
    blocks = []
    for pf in range(12):
        part = waves[:, pf * LANES : (pf + 1) * LANES]
        blocks.append(
            jnp.concatenate([part[j * groups : (j + 1) * groups] for j in range(folds)], axis=1)
        )
    high, low = halve(jnp.concatenate(blocks, axis=0))
    wide = [None] * plan.wide
    for n, (begin, end, first, last) in enumerate(bands(plan)):
        part = product(
            (high[:, first:last], low[:, first:last]), (last_ref[n, 0], last_ref[n, 1])
        )
        for s in range(begin // LANES, end // LANES):
            tile = part[:, s * LANES - begin : (s + 1) * LANES - begin]
            wide[s] = tile if wide[s] is None else wide[s] + tile
    quad, count = 4 * rows, 4 * groups
    for s in range(plan.wide):
        low, middle, high = [wide[s][q * count : (q + 1) * count] for q in range(3)]
        here, ahead = pl.ds(s, count, stride=plan.wide), pl.ds(quad + s, count, stride=plan.wide)
        keep_ref[here, :] = jnp.where(odd == 0, low, middle)
        keep_ref[ahead, :] = jnp.where(odd == 0, middle, high)
        send_ref[here, :] = jnp.where(odd == 0, middle, low)
        send_ref[ahead, :] = jnp.where(odd == 0, high, middle)
    drift = got_ref[0, pl.ds(2 * plan.block, 8), :]
    for j in range(1, pairs):
        drift = drift + got_ref[j, pl.ds(2 * plan.block, 8), :]
    keep_ref[pl.ds(2 * quad, 8), :] = drift
    send_ref[pl.ds(2 * quad, 8), :] = drift


def times(left, right):
    return (left[0] * right[0] - left[1] * right[1], left[0] * right[1] + left[1] * right[0])


def times_conj(left, right):
    return (left[0] * right[0] + left[1] * right[1], left[1] * right[0] - left[0] * right[1])


def rotation(fields):
    both, apart = fields[0], fields[1]
    a, b, e = 0.5 * (both + apart), 0.5 * (both - apart), -both
    u, v, w = (fields[2], fields[3]), (fields[4], fields[5]), (fields[6], fields[7])
    square = [x[0] * x[0] + x[1] * x[1] for x in (u, v, w)]
    a00, a11, a22 = square[2] - b * e, square[1] - a * e, square[0] - a * b
    vw, uw, vu = times_conj(v, w), times(u, w), times_conj(v, u)
    a01 = (e * u[1] - vw[0], -(e * u[0]) - vw[1])
    a02 = (uw[0] + b * v[1], uw[1] - b * v[0])
    a12 = (a * w[1] - vu[0], -(a * w[0]) - vu[1])
    turn = a * a00 + times_conj(u, a01)[1] + times_conj(v, a02)[1]
    real = 1.0 + (a00 + a11 + a22)
    scale = 2.0 / (real * real + turn * turn)
    factor = (real * scale, turn * scale)
    entries = [[None] * 3 for _ in range(3)]
    for i, (up, imag) in enumerate(((a00, a), (a11, b), (a22, e))):
        value = times((1.0 + up, imag), factor)
        entries[i][i] = (value[0] - 1.0, value[1])
    for (i, j), up, off in (((0, 1), a01, u), ((0, 2), a02, v), ((1, 2), a12, w)):
        entries[i][j] = times((up[0] + off[0], up[1] + off[1]), factor)
        entries[j][i] = times((up[0] - off[0], off[1] - up[1]), factor)
    whole = (0.5 * (real * factor[0] - turn * factor[1]), real * factor[1])
    return [entries[i][j][part] for part in range(2) for i in range(3) for j in range(3)] + list(whole)


def update_kernel(
    plan, index_ref, keep_ref, got_ref, links_ref, turns_ref, fixed_ref, drift_ref, here, along, staged, semaphores
):
    rows, side = plan.rows, plan.side
    quad = 4 * rows
    odd = index_ref[0] % 2

    def turn(i, _):
        begin = pl.multiple_of(i * 8, 8)
        for q, lead in ((0, 8), (1, 0)):
            fields = [None] * 8
            for f in range(4):
                place = pl.ds(pl.multiple_of(q * quad + f * rows + begin, 8), 8)
                own, other = keep_ref[place, :], got_ref[place, :]
                fields[f] = jnp.where(odd == 0, own, other)
                fields[4 + f] = jnp.where(odd == 0, other, own)
            for n, value in enumerate(rotation(fields)):
                if q == 0:
                    here[n, pl.ds(begin + lead, 8), :] = value
                else:
                    along[n, pl.ds(begin, 8), :] = value
        return 0

    lax.fori_loop(0, rows // 8, turn, 0, unroll=3)

    def update(d, i):
        begin = i * 8

        def matrix(read):
            value = [read(n) for n in range(18)]
            return [[(value[3 * r + c], value[9 + 3 * r + c]) for c in range(3)] for r in range(3)]

        if d == 0:

            def shifted(n):
                return along[n, pl.ds(begin, 8), :]

        elif d == 1:

            def shifted(n):
                return moved(here, n, 8 + begin, 8, side)

        else:
            at_end = (last_index(8, side) + begin * LANES) % side == side - 1

            def shifted(n):
                return jnp.where(
                    at_end,
                    moved(here, n, 8 + begin, 8, 1 - side),
                    moved(here, n, 8 + begin, 8, 1),
                )

        def own(r, c):
            return tuple(here[9 * part + 3 * r + c, pl.ds(begin + 8, 8), :] for part in range(2))

        links = matrix(lambda n: links_ref[d * 18 + n, pl.ds(begin, 8), :])
        ahead = matrix(shifted)
        moved_rows = []
        for r in range(2):
            left = [own(r, k) for k in range(3)]
            line = [add(*[times(left[k], links[k][c]) for k in range(3)]) for c in range(3)]
            moved_rows.append(
                [add(*[times_conj(line[k], ahead[c][k]) for k in range(3)]) for c in range(3)]
            )
        whole = tuple(turns_ref[d * 2 + part, pl.ds(begin, 8), :] for part in range(2))
        whole = times(whole, tuple(here[18 + part, pl.ds(begin + 8, 8), :] for part in range(2)))
        whole = times_conj(whole, (shifted(18), shifted(19)))
        moved_rows.append([times_conj(whole, cross(*moved_rows, c)) for c in range(3)])
        for r in range(3):
            for c in range(3):
                for part in range(2):
                    staged[d * 18 + part * 9 + r * 3 + c, pl.ds(begin, 8), :] = moved_rows[r][c][part]

    tiles = rows // 8
    copies = []

    def write(place, rows_place, n):
        copy = pltpu.make_async_copy(
            staged.at[place, rows_place], fixed_ref.at[place, rows_place], semaphores.at[n]
        )
        copy.start()
        copies.append(copy)

    for n in range(20):
        wrap(here, n, rows)
    for d in (1, 2, 0):
        chunks = 1 if d else 3
        for m in range(chunks):
            part = tiles // chunks

            for i in range(m * part, (m + 1) * part):
                update(d, i)
            write(pl.ds(d * 18, 18), pl.ds(m * part * 8, part * 8), len(copies))
    total = keep_ref[pl.ds(2 * quad, 8), :] + got_ref[pl.ds(2 * quad, 8), :]
    drift_ref[0] = jnp.sum(total) * (1.0 / (9.0 * plan.count_x * plan.cells))
    for copy in copies:
        copy.wait()


def cross(first, second, c):
    one = times(first[(c + 1) % 3], second[(c + 2) % 3])
    two = times(first[(c + 2) % 3], second[(c + 1) % 3])
    return (one[0] - two[0], one[1] - two[1])


def add(first, second, third):
    return (first[0] + second[0] + third[0], first[1] + second[1] + third[1])


def whole_spec():
    return pl.BlockSpec(memory_space=pltpu.VMEM)


def scalar_spec():
    return pl.BlockSpec(memory_space=pltpu.SMEM)


def shape_of(*shape):
    return jax.ShapeDtypeStruct(shape, jnp.float32)


def local(gauge_links):
    count_x = lax.axis_size("gx")
    plan = Plan(count_x, SIDE)
    rows, pairs = plan.rows, plan.pairs
    table = tables(plan)
    index = lax.axis_index("gx").astype(jnp.int32).reshape(1)
    links = gauge_links.reshape(54, rows, LANES)
    held = pltpu.with_memory_space_constraint(links, pltpu.HBM)
    quads = 8 * rows
    swap = [(i, i ^ 1) for i in range(count_x)]
    halo = [(2 * p, 2 * p - 1) for p in range(1, pairs)] + [(count_x - 1, 0)]
    same_core, same_core_back = [
        [[c + 2 * p for p in sorted(range(pairs), key=place.__getitem__)] for c in range(2)]
        for place in (plan.place, plan.back_place)
    ]

    keep, send, ahead = pl.pallas_call(
        functools.partial(divergence_kernel, plan),
        out_shape=(shape_of(quads, LANES),) * 3,
        in_specs=[scalar_spec(), pl.BlockSpec(memory_space=pltpu.HBM)],
        out_specs=(whole_spec(),) * 3,
        scratch_shapes=[
            pltpu.VMEM((54, rows, LANES), jnp.float32),
            pltpu.VMEM((8, rows + 16, LANES), jnp.float32),
            pltpu.VMEM((8, rows + 16, LANES), jnp.float32),
            pltpu.SemaphoreType.DMA((3, 3)),
        ],
        compiler_params=params(),
        name="divergence",
    )(index, held)
    got = lax.ppermute(send, "gx", swap)
    beside = lax.ppermute(ahead, "gx", halo)
    sent, odd_part, odd_drift = pl.pallas_call(
        functools.partial(forward_kernel, plan),
        out_shape=(
            shape_of(pairs, plan.sent, LANES),
            shape_of(SIDE, 4 * LANES),
            shape_of(8, LANES),
        ),
        in_specs=[scalar_spec()] + [whole_spec()] * 5,
        out_specs=(pl.BlockSpec(memory_space=pltpu.HBM), whole_spec(), whole_spec()),
        scratch_shapes=[
            pltpu.VMEM((pairs, plan.sent, LANES), jnp.float32),
            pltpu.SemaphoreType.DMA((2,)),
        ],
        compiler_params=params(),
        name="forward",
    )(index, keep, got, table["last"], table["second"], table["modes"])
    arrived = lax.all_to_all(
        sent, "gx", split_axis=0, concat_axis=0, tiled=True, axis_index_groups=same_core
    )
    drift_part, turns, own_modes = pl.pallas_call(
        functools.partial(drift_kernel, plan),
        out_shape=(shape_of(8, LANES), shape_of(6, rows, LANES), shape_of(plan.block, LANES)),
        in_specs=[scalar_spec()] + [whole_spec()] * 4 + [pl.BlockSpec(memory_space=pltpu.HBM)],
        out_specs=(whole_spec(),) * 3,
        scratch_shapes=[pltpu.VMEM((54, rows, LANES), jnp.float32), pltpu.SemaphoreType.DMA((3,))],
        compiler_params=params(),
        cost_estimate=pl.CostEstimate(flops=5 * 10**10, bytes_accessed=5 * 10**7, transcendentals=0),
        name="drift",
    )(index, odd_drift, beside, keep, send, held)
    back = pl.pallas_call(
        functools.partial(filter_kernel, plan),
        out_shape=shape_of(pairs, plan.returned, LANES),
        in_specs=[scalar_spec()] + [whole_spec()] * 3,
        out_specs=whole_spec(),
        compiler_params=params(),
        name="filter",
    )(index, arrived, drift_part, own_modes)
    returned = lax.all_to_all(
        back, "gx", split_axis=0, concat_axis=0, tiled=True, axis_index_groups=same_core_back
    )
    keep, send = pl.pallas_call(
        functools.partial(backward_kernel, plan),
        out_shape=(shape_of(quads + 8, LANES), shape_of(quads + 8, LANES)),
        in_specs=[scalar_spec()] + [whole_spec()] * 5,
        out_specs=(whole_spec(), whole_spec()),
        scratch_shapes=[
            pltpu.VMEM((2 * plan.tiles, SIDE, LANES), jnp.float32),
        ],
        compiler_params=params(),
        name="backward",
    )(index, returned, odd_part, table["last_back"], table["second"], table["modes"])
    got = lax.ppermute(send, "gx", swap)
    fixed, drift = pl.pallas_call(
        functools.partial(update_kernel, plan),
        out_shape=(shape_of(54, rows, LANES), shape_of(1)),
        in_specs=[scalar_spec()] + [whole_spec()] * 4,
        out_specs=(pl.BlockSpec(memory_space=pltpu.HBM), scalar_spec()),
        scratch_shapes=[
            pltpu.VMEM((20, rows + 16, LANES), jnp.float32),
            pltpu.VMEM((20, rows, LANES), jnp.float32),
            pltpu.VMEM((54, rows, LANES), jnp.float32),
            pltpu.SemaphoreType.DMA((5,)),
        ],
        compiler_params=params(),
        name="update",
    )(index, keep, got, links, turns)
    return fixed.reshape(gauge_links.shape), drift


def solution(mesh):
    in_specs = (P(None, None, None, None, ("ta", "gx"), None),)
    out_specs = (P(None, None, None, None, ("ta", "gx"), None), P("ta"))
    return jax.shard_map(local, mesh=mesh, in_specs=in_specs, out_specs=out_specs, check_vma=False)
```

```python
import functools
import math

import jax
import jax.numpy as jnp
import numpy as np
from jax import lax
from jax.experimental import pallas as pl
from jax.experimental.pallas import tpu as pltpu
from jax.sharding import PartitionSpec as P

SIDE = 96
LANES = 128

step_size = 0.08
peak_square = 12.0
gain = 0.5 * step_size * peak_square

params = functools.partial(pltpu.CompilerParams, vmem_limit_bytes=48 * 1024 * 1024)
drift_weights = (1.5, 0.5, 2.0, 2.0, 2.0, 2.0, 2.0, 2.0)


class Plan:
    def __init__(self, count_x, side):
        self.count_x, self.side = count_x, side
        self.cells = side * side
        self.rows = self.cells // LANES
        self.period = side * LANES // math.gcd(side, LANES)
        self.wide = self.period // LANES
        self.folds = self.period // side
        self.groups = self.cells // self.period
        self.pairs = count_x // 2
        self.share = side // self.pairs
        self.full = self.share // 8 * 8
        self.rest = self.share - self.full
        self.tiles = 4 * side // LANES
        self.block = self.tiles * self.share
        self.sent = -(-2 * self.block // 8) * 8
        half = self.pairs // 2
        there = [(p + half) % self.pairs for p in range(self.pairs)]
        back = [p ^ (1 - half % 2) for p in range(half, self.pairs)] + list(range(half))[::-1]
        self.place = [there.index(p) for p in range(self.pairs)]
        self.back_place = [back.index(p) for p in range(self.pairs)]
        self.returned = -(-(2 * self.block + 8) // 8) * 8


def fourier(length):
    site = np.arange(length)
    basis = np.zeros((length, length))
    for k in range(length):
        angle = 2.0 * math.pi * (k * site % length) / length
        if k == 0 or 2 * k == length:
            basis[k] = np.cos(angle) / math.sqrt(length)
        elif 2 * k < length:
            basis[k] = np.cos(angle) * math.sqrt(2.0 / length)
        else:
            basis[k] = np.sin(angle) * math.sqrt(2.0 / length)
    return basis


def eigen(length):
    return 4.0 * np.sin(math.pi * np.arange(length) / length) ** 2


def split_table(table):
    high = table.astype(jnp.bfloat16)
    low = (table - high.astype(np.float64)).astype(jnp.bfloat16)
    return np.stack([high, low])


def stack_table(table):
    high, low = split_table(table)
    return np.block([[high, high], [low, np.zeros_like(low)]])


def tables(plan):
    side, folds, groups = plan.side, plan.folds, plan.groups
    basis = fourier(side)
    last = np.zeros((folds, side, folds, LANES))
    for j in range(folds):
        last[j, :, j, :side] = basis.T
    last = last.reshape(folds * side, folds * LANES)
    order = [plan.share * j + i for j in range(plan.pairs) for i in range(plan.full)]
    order += [plan.share * j + plan.full + i for j in range(plan.pairs) for i in range(plan.rest)]
    columns = [folds * g + j for j in range(folds) for g in range(groups)]
    second = basis[order][:, columns]
    value = eigen(side)
    inverse_side = np.zeros((side, LANES))
    inverse_side[:, :side] = 1.0 / (2.0 + value[order][:, None] + value[None, :])
    return {
        "last": np.stack([split_table(last[a:b, c:d]) for a, b, c, d in bands(plan)]),
        "last_back": np.stack([split_table(last[a:b, c:d].T) for a, b, c, d in bands(plan)]),
        "second": np.stack([stack_table(second), stack_table(second.T)]),
        "modes": inverse_side.astype(np.float32),
    }


def halve(value):
    high = value.astype(jnp.bfloat16)
    low = (value - high.astype(jnp.float32)).astype(jnp.bfloat16)
    return high, low


def product(left, right):
    dot = functools.partial(jnp.dot, preferred_element_type=jnp.float32)
    both = dot(jnp.concatenate(left, axis=0), right[0])
    size = left[0].shape[0]
    return both[:size] + (both[size:] + dot(left[0], right[1]))


def stacked(table, value):
    both = jnp.dot(table, jnp.concatenate(halve(value), axis=0), preferred_element_type=jnp.float32)
    size = both.shape[0] // 2
    return both[:size] + both[size:]


def bands(plan):
    for j in range(0, plan.folds, 2):
        rows = min(2, plan.folds - j)
        begin, end = j * plan.side // LANES, -(-(j + rows) * plan.side // LANES)
        yield begin * LANES, end * LANES, j * LANES, (j + rows) * LANES


def lane_of(shape):
    return lax.broadcasted_iota(jnp.int32, shape, 1)


def moved(ref, field, start, size, distance):
    down, over = distance // LANES, distance % LANES
    here = ref[field, pl.ds(start + down, size), :]
    after = ref[field, pl.ds(start + down + 1, size), :]
    mixed = jnp.where(lane_of(here.shape) >= over, here, after)
    return pltpu.roll(mixed, LANES - over, 1)


def last_index(rows, side):
    row = lax.broadcasted_iota(jnp.int32, (rows, LANES), 0)
    return (row * LANES + lane_of((rows, LANES))) % side


def wrap(ref, field, rows):
    ref[field, pl.ds(0, 8), :] = ref[field, pl.ds(rows, 8), :]
    ref[field, pl.ds(8 + rows, 8), :] = ref[field, pl.ds(8, 8), :]


def projected(links, d):
    def entry(part, i, j):
        return links[((d * 2 + part) * 3 + i) * 3 + j]

    im00, im11, im22 = entry(1, 0, 0), entry(1, 1, 1), entry(1, 2, 2)
    fields = [(im00 + im11 - 2.0 * im22) * (1.0 / 3.0), im00 - im11]
    for i, j in ((0, 1), (0, 2), (1, 2)):
        fields.append(0.5 * (entry(0, i, j) - entry(0, j, i)))
        fields.append(0.5 * (entry(1, i, j) + entry(1, j, i)))
    return fields


def link_copies(links_ref, staged, semaphores):
    copies = []
    for n, d in enumerate((1, 2, 0)):
        for m, (begin, size) in enumerate(((1, 3), (5, 3), (9, 9))):
            place = pl.ds(d * 18 + begin, size)
            copies.append(
                pltpu.make_async_copy(links_ref.at[place], staged.at[place], semaphores.at[n, m])
            )
    return copies


def divergence_kernel(
    plan, index_ref, links_ref, keep_ref, send_ref, ahead_ref, staged, second, third, semaphores
):
    rows, side = plan.rows, plan.side
    copies = link_copies(links_ref, staged, semaphores)
    for copy in copies:
        copy.start()
    odd = index_ref[0] % 2
    at_start = last_index(rows, side) == 0
    middle = pl.ds(8, rows)
    for copy in copies[:3]:
        copy.wait()
    for f, value in enumerate(projected(staged, 1)):
        second[f, middle, :] = value
        wrap(second, f, rows)
    diverge = [moved(second, f, 8, rows, -side) - second[f, middle, :] for f in range(8)]
    for copy in copies[3:6]:
        copy.wait()
    for f, value in enumerate(projected(staged, 2)):
        third[f, middle, :] = value
        wrap(third, f, rows)
    for f in range(8):
        beside = jnp.where(
            at_start, moved(third, f, 8, rows, side - 1), moved(third, f, 8, rows, -1)
        )
        diverge[f] = diverge[f] + (beside - third[f, middle, :])
        second[f, middle, :] = diverge[f]
    for copy in copies[6:]:
        copy.wait()
    direct = projected(staged, 0)
    index = index_ref[0]
    for f in range(8):
        place = pl.ds(f * rows, rows)
        total = second[f, middle, :] - direct[f]
        ahead_ref[place, :] = jnp.where(index == plan.count_x - 1, direct[f], total)
    for f in range(4):
        for part in range(2):
            place = pl.ds((part * 4 + f) * rows, rows)
            low, high = direct[f], direct[4 + f]
            if part == 0:
                low, high = second[f, middle, :] - low, second[4 + f, middle, :] - high
            keep_ref[place, :] = jnp.where(odd == 0, low, high)
            send_ref[place, :] = jnp.where(odd == 0, high, low)


def forward_kernel(
    plan, index_ref, keep_ref, got_ref, last_ref, second_ref, modes_ref, sent_ref, odd_ref, drift_ref, staged, departures
):
    rows, groups, folds, side = plan.rows, plan.groups, plan.folds, plan.side
    odd = index_ref[0] % 2
    quad = 4 * rows
    count = 4 * groups
    square = jnp.zeros((8, LANES), jnp.float32)
    wide = []
    for s in range(plan.wide):
        own_d, own_a, got_d, got_a = [
            ref[pl.ds(begin + s, count, stride=plan.wide), :]
            for ref in (keep_ref, got_ref)
            for begin in (0, quad)
        ]
        even_d, odd_d = jnp.where(odd == 0, own_d, got_d), jnp.where(odd == 0, got_d, own_d)
        even_a, odd_a = jnp.where(odd == 0, own_a, got_a), jnp.where(odd == 0, got_a, own_a)
        whole = odd_d + even_a
        for f in range(4):
            part = whole[f * groups : (f + 1) * groups]
            square = square + sum_tiles(part * part) * jnp.where(
                odd == 0, drift_weights[f], drift_weights[4 + f]
            )
        wide.append(jnp.concatenate([even_d, whole, odd_a], axis=0))
    drift_ref[...] = square
    wide = jnp.concatenate(wide, axis=1)
    high, low = halve(wide)
    waves = jnp.concatenate(
        [
            product(
                (high[:, begin:end], low[:, begin:end]),
                (last_ref[n, 0], last_ref[n, 1]),
            )
            for n, (begin, end, _, _) in enumerate(bands(plan))
        ],
        axis=1,
    )
    columns = []
    for pf in range(12):
        part = waves[pf * groups : (pf + 1) * groups]
        columns.append(
            jnp.concatenate([part[:, j * LANES : (j + 1) * LANES] for j in range(folds)], axis=0)
        )
    modes = stacked(second_ref[0], jnp.concatenate(columns, axis=1))
    inverse = modes_ref[:side]
    full, rest, pairs, tiles = plan.full, plan.rest, plan.pairs, plan.tiles
    lane = lane_of((side, LANES))
    zero = (lane == 0) & (lax.broadcasted_iota(jnp.int32, (side, LANES), 0) == 0)
    even, between, after = [
        [modes[:, (q * 4 + f) * LANES : (q * 4 + f + 1) * LANES] for f in range(4)] for q in range(3)
    ]
    shared = [value * inverse for value in between]
    for f in range(4):
        odd_ref[:, f * LANES : (f + 1) * LANES] = gain * shared[f]
    below = [even[f] + shared[f] for f in range(4)]
    above = [jnp.where(zero, between[f], after[f] + shared[f]) for f in range(4)]
    early = tiles * full
    copies = []

    def leave(begin, size):
        place = (slice(None), pl.ds(begin, size))
        copy = pltpu.make_async_copy(staged.at[place], sent_ref.at[place], departures.at[len(copies)])
        copy.start()
        copies.append(copy)

    for q, fields in enumerate((below, above)):
        for t, value in enumerate(pack(fields, lane, side)):
            at = q * tiles + t
            for j in range(pairs):
                if full:
                    staged[plan.place[j], pl.ds(at * full, full), :] = value[j * full : (j + 1) * full]
                if rest:
                    begin = pairs * full + j * rest
                    staged[plan.place[j], pl.ds(2 * tiles * full + at * rest, rest), :] = value[
                        begin : begin + rest
                    ]
        if q == 0 and early:
            leave(0, early)
    spare = plan.sent - 2 * plan.block
    if spare:
        staged[:, pl.ds(2 * plan.block, spare), :] = jnp.zeros((pairs, spare, LANES), jnp.float32)
    leave(early, plan.sent - early)
    for copy in copies:
        copy.wait()


def sum_tiles(value):
    total = value[:8]
    for i in range(1, value.shape[0] // 8):
        total = total + value[i * 8 : (i + 1) * 8]
    return total


def pack(fields, lane, side):
    rolled = [
        value if f * side % LANES == 0 else pltpu.roll(value, f * side % LANES, 1)
        for f, value in enumerate(fields)
    ]
    packed = []
    for t in range(4 * side // LANES):
        value = None
        for f in range(4):
            if f * side < (t + 1) * LANES and (f + 1) * side > t * LANES:
                value = rolled[f] if value is None else jnp.where(lane >= f * side - t * LANES, rolled[f], value)
        packed.append(value)
    return packed


def unpack(packed, lane, side):
    fields = []
    for f in range(4):
        begin = f * side // LANES
        end = ((f + 1) * side - 1) // LANES
        offset = f * side % LANES
        value = packed[begin]
        if end != begin:
            value = jnp.where(lane >= offset, packed[begin], packed[end])
        if offset:
            value = pltpu.roll(value, LANES - offset, 1)
        fields.append(jnp.where(lane < side, value, 0.0))
    return fields


def eigenvalues(plan, first, size):
    side = plan.side
    row = lax.broadcasted_iota(jnp.int32, (plan.tiles * size, LANES), 0)
    tile = row // size
    total = 0.0
    for mode in (first + row - tile * size, (tile * LANES + lane_of(row.shape)) % side):
        near = jnp.minimum(mode, side - mode).astype(jnp.float32)
        sine = jnp.sin(near * (math.pi / side))
        total = total + 4.0 * sine * sine
    return total


def drift_kernel(
    plan, index_ref, odd_ref, beside_ref, keep_ref, send_ref, links_ref, drift_ref, turns_ref, own_ref, loaded, arrivals
):
    rows, count_x = plan.rows, plan.count_x
    loads = []
    for d in range(3):
        place = pl.ds(d * 18, 18)
        loads.append(pltpu.make_async_copy(links_ref.at[place], loaded.at[place], arrivals.at[d]))
        loads[d].start()
    index = index_ref[0]
    square = jnp.zeros((rows, LANES), jnp.float32)
    part = jnp.where(index == 0, 0, 4 * rows)
    for f in range(4):
        place = pl.ds(pl.multiple_of(part + f * rows, 8), rows)
        own, other = keep_ref[place, :], send_ref[place, :]
        low, high = jnp.where(index % 2 == 0, own, other), jnp.where(index % 2 == 0, other, own)
        for n, value in ((f, low), (4 + f, high)):
            total = beside_ref[pl.ds(n * rows, rows), :] + value
            square = square + total * total * drift_weights[n]
    complete = (index == 0) | ((index % 2 == 1) & (index < count_x - 1))
    drift_ref[...] = odd_ref[...] + jnp.where(complete, sum_tiles(square), 0.0)
    for start, size in ((0, plan.full), (plan.full, plan.rest)):
        if size:
            own_ref[pl.ds(plan.tiles * start, plan.tiles * size), :] = eigenvalues(
                plan, index // 2 * plan.share + start, size
            )
    for d in range(3):
        loads[d].wait()
        link = [[tuple(loaded[((d * 2 + part) * 3 + r) * 3 + c] for part in range(2)) for c in range(3)] for r in range(3)]
        value = add(*[times(link[0][c], cross(link[1], link[2], c)) for c in range(3)])
        for part in range(2):
            turns_ref[d * 2 + part] = value[part]


def filter_kernel(plan, index_ref, got_ref, drift_ref, own_ref, back_ref):
    pairs, tiles, count_x = plan.pairs, plan.tiles, plan.count_x
    half = pairs // 2
    drift = drift_ref[...]
    for part, (size, first) in enumerate(((plan.full, 0), (plan.rest, 2 * tiles * plan.full))):
        if not size:
            continue
        length = tiles * size
        value = own_ref[pl.ds(part * tiles * plan.full, length), :]
        low, high = pl.ds(first, length), pl.ds(first + length, length)
        inside = value > 0
        below = [got_ref[plan.place[p], low, :] for p in range(pairs)]
        above = [got_ref[plan.place[p], high, :] for p in range(pairs)]
        rhs = [
            below[p] + jnp.where(inside, above[(p - 1) % pairs], -below[(p - 1) % pairs])
            for p in range(pairs)
        ]
        plus = [rhs[d] + rhs[pairs - d] for d in range(1, half)]
        minus = [rhs[d] - rhs[pairs - d] for d in range(1, half)]
        cosines, sines = [], []
        for k in range(half + 1):
            total = rhs[0] + rhs[half] if k % 2 == 0 else rhs[0] - rhs[half]
            for d in range(1, half):
                total = total + plus[d - 1] * math.cos(2 * math.pi * (k * d % pairs) / pairs)
            root = 4.0 * math.sin(math.pi * k / count_x) ** 2
            split = (value + root) * (value + (4.0 - root))
            scale = gain / pairs * (1.0 if k in (0, half) else 2.0)
            if k == 0:
                factor = jnp.where(inside, scale * (2.0 + value) / jnp.where(inside, split, 1.0), 0.0)
                whole = above[0]
                for p in range(1, pairs):
                    whole = whole + above[p]
                mean = jnp.where(inside, 0.0, whole * (-0.25 * gain / pairs))
                cosines.append(total * factor + mean)
            else:
                factor = scale * (2.0 + value) / split
                cosines.append(total * factor)
                if k < half:
                    wave = jnp.zeros_like(value)
                    for d in range(1, half):
                        wave = wave + minus[d - 1] * math.sin(2 * math.pi * (k * d % pairs) / pairs)
                    sines.append(wave * factor)
        results = [None] * pairs
        for d in range(half + 1):
            even = cosines[0]
            for k in range(1, half + 1):
                even = even + cosines[k] * math.cos(2 * math.pi * (k * d % pairs) / pairs)
            if d in (0, half):
                results[d] = even
            else:
                wave = jnp.zeros_like(value)
                for k in range(1, half):
                    wave = wave + sines[k - 1] * math.sin(2 * math.pi * (k * d % pairs) / pairs)
                results[d] = even + wave
                results[pairs - d] = even - wave
        for p in range(pairs):
            back_ref[plan.back_place[p], low, :] = results[p]
            back_ref[plan.back_place[p], high, :] = results[(p + 1) % pairs]
    for p in range(pairs):
        back_ref[p, pl.ds(2 * plan.block, 8), :] = drift


def backward_kernel(
    plan, index_ref, got_ref, odd_ref, last_ref, second_ref, modes_ref, keep_ref, send_ref, packed
):
    rows, groups, folds, side = plan.rows, plan.groups, plan.folds, plan.side
    full, rest, pairs, tiles = plan.full, plan.rest, plan.pairs, plan.tiles
    odd = index_ref[0] % 2
    for q in range(2):
        for t in range(tiles):
            at = q * tiles + t
            for j in range(pairs):
                if full:
                    packed[at, pl.ds(j * full, full), :] = got_ref[plan.back_place[j], pl.ds(at * full, full), :]
                if rest:
                    packed[at, pl.ds(pairs * full + j * rest, rest), :] = got_ref[
                        plan.back_place[j], pl.ds(2 * tiles * full + at * rest, rest), :
                    ]
    lane = lane_of((side, LANES))
    inverse = modes_ref[:side]
    even, after = [
        unpack([packed[q * tiles + t] for t in range(tiles)], lane, side) for q in range(2)
    ]
    between = [
        odd_ref[:, f * LANES : (f + 1) * LANES] + (even[f] + after[f]) * inverse for f in range(4)
    ]
    waves = stacked(second_ref[1], jnp.concatenate(even + between + after, axis=1))
    blocks = []
    for pf in range(12):
        part = waves[:, pf * LANES : (pf + 1) * LANES]
        blocks.append(
            jnp.concatenate([part[j * groups : (j + 1) * groups] for j in range(folds)], axis=1)
        )
    high, low = halve(jnp.concatenate(blocks, axis=0))
    wide = [None] * plan.wide
    for n, (begin, end, first, last) in enumerate(bands(plan)):
        part = product(
            (high[:, first:last], low[:, first:last]), (last_ref[n, 0], last_ref[n, 1])
        )
        for s in range(begin // LANES, end // LANES):
            tile = part[:, s * LANES - begin : (s + 1) * LANES - begin]
            wide[s] = tile if wide[s] is None else wide[s] + tile
    quad, count = 4 * rows, 4 * groups
    for s in range(plan.wide):
        low, middle, high = [wide[s][q * count : (q + 1) * count] for q in range(3)]
        here, ahead = pl.ds(s, count, stride=plan.wide), pl.ds(quad + s, count, stride=plan.wide)
        keep_ref[here, :] = jnp.where(odd == 0, low, middle)
        keep_ref[ahead, :] = jnp.where(odd == 0, middle, high)
        send_ref[here, :] = jnp.where(odd == 0, middle, low)
        send_ref[ahead, :] = jnp.where(odd == 0, high, middle)
    drift = got_ref[0, pl.ds(2 * plan.block, 8), :]
    for j in range(1, pairs):
        drift = drift + got_ref[j, pl.ds(2 * plan.block, 8), :]
    keep_ref[pl.ds(2 * quad, 8), :] = drift
    send_ref[pl.ds(2 * quad, 8), :] = drift


def times(left, right):
    return (left[0] * right[0] - left[1] * right[1], left[0] * right[1] + left[1] * right[0])


def times_conj(left, right):
    return (left[0] * right[0] + left[1] * right[1], left[1] * right[0] - left[0] * right[1])


def rotation(fields):
    both, apart = fields[0], fields[1]
    a, b, e = 0.5 * (both + apart), 0.5 * (both - apart), -both
    u, v, w = (fields[2], fields[3]), (fields[4], fields[5]), (fields[6], fields[7])
    square = [x[0] * x[0] + x[1] * x[1] for x in (u, v, w)]
    a00, a11, a22 = square[2] - b * e, square[1] - a * e, square[0] - a * b
    vw, uw, vu = times_conj(v, w), times(u, w), times_conj(v, u)
    a01 = (e * u[1] - vw[0], -(e * u[0]) - vw[1])
    a02 = (uw[0] + b * v[1], uw[1] - b * v[0])
    a12 = (a * w[1] - vu[0], -(a * w[0]) - vu[1])
    turn = a * a00 + times_conj(u, a01)[1] + times_conj(v, a02)[1]
    real = 1.0 + (a00 + a11 + a22)
    scale = 2.0 / (real * real + turn * turn)
    factor = (real * scale, turn * scale)
    entries = [[None] * 3 for _ in range(3)]
    for i, (up, imag) in enumerate(((a00, a), (a11, b), (a22, e))):
        value = times((1.0 + up, imag), factor)
        entries[i][i] = (value[0] - 1.0, value[1])
    for (i, j), up, off in (((0, 1), a01, u), ((0, 2), a02, v), ((1, 2), a12, w)):
        entries[i][j] = times((up[0] + off[0], up[1] + off[1]), factor)
        entries[j][i] = times((up[0] - off[0], off[1] - up[1]), factor)
    whole = (0.5 * (real * factor[0] - turn * factor[1]), real * factor[1])
    return [entries[i][j][part] for part in range(2) for i in range(3) for j in range(3)] + list(whole)


def update_kernel(
    plan, index_ref, keep_ref, got_ref, links_ref, turns_ref, fixed_ref, drift_ref, here, along, staged, semaphores
):
    rows, side = plan.rows, plan.side
    quad = 4 * rows
    odd = index_ref[0] % 2

    def turn(i, _):
        begin = pl.multiple_of(i * 8, 8)
        for q, lead in ((0, 8), (1, 0)):
            fields = [None] * 8
            for f in range(4):
                place = pl.ds(pl.multiple_of(q * quad + f * rows + begin, 8), 8)
                own, other = keep_ref[place, :], got_ref[place, :]
                fields[f] = jnp.where(odd == 0, own, other)
                fields[4 + f] = jnp.where(odd == 0, other, own)
            for n, value in enumerate(rotation(fields)):
                if q == 0:
                    here[n, pl.ds(begin + lead, 8), :] = value
                else:
                    along[n, pl.ds(begin, 8), :] = value
        return 0

    lax.fori_loop(0, rows // 8, turn, 0, unroll=3)

    def update(d, i):
        begin = i * 8

        def matrix(read):
            value = [read(n) for n in range(18)]
            return [[(value[3 * r + c], value[9 + 3 * r + c]) for c in range(3)] for r in range(3)]

        if d == 0:

            def shifted(n):
                return along[n, pl.ds(begin, 8), :]

        elif d == 1:

            def shifted(n):
                return moved(here, n, 8 + begin, 8, side)

        else:
            at_end = (last_index(8, side) + begin * LANES) % side == side - 1

            def shifted(n):
                return jnp.where(
                    at_end,
                    moved(here, n, 8 + begin, 8, 1 - side),
                    moved(here, n, 8 + begin, 8, 1),
                )

        def own(r, c):
            return tuple(here[9 * part + 3 * r + c, pl.ds(begin + 8, 8), :] for part in range(2))

        links = matrix(lambda n: links_ref[d * 18 + n, pl.ds(begin, 8), :])
        ahead = matrix(shifted)
        moved_rows = []
        for r in range(2):
            left = [own(r, k) for k in range(3)]
            line = [add(*[times(left[k], links[k][c]) for k in range(3)]) for c in range(3)]
            moved_rows.append(
                [add(*[times_conj(line[k], ahead[c][k]) for k in range(3)]) for c in range(3)]
            )
        whole = tuple(turns_ref[d * 2 + part, pl.ds(begin, 8), :] for part in range(2))
        whole = times(whole, tuple(here[18 + part, pl.ds(begin + 8, 8), :] for part in range(2)))
        whole = times_conj(whole, (shifted(18), shifted(19)))
        moved_rows.append([times_conj(whole, cross(*moved_rows, c)) for c in range(3)])
        for r in range(3):
            for c in range(3):
                for part in range(2):
                    staged[d * 18 + part * 9 + r * 3 + c, pl.ds(begin, 8), :] = moved_rows[r][c][part]

    tiles = rows // 8
    copies = []

    def write(place, rows_place, n):
        copy = pltpu.make_async_copy(
            staged.at[place, rows_place], fixed_ref.at[place, rows_place], semaphores.at[n]
        )
        copy.start()
        copies.append(copy)

    for n in range(20):
        wrap(here, n, rows)
    for d in (1, 2, 0):
        chunks = 1 if d == 1 else 3
        for m in range(chunks):
            part = tiles // chunks

            for i in range(m * part, (m + 1) * part):
                update(d, i)
            write(pl.ds(d * 18, 18), pl.ds(m * part * 8, part * 8), len(copies))
    total = keep_ref[pl.ds(2 * quad, 8), :] + got_ref[pl.ds(2 * quad, 8), :]
    drift_ref[0] = jnp.sum(total) * (1.0 / (9.0 * plan.count_x * plan.cells))
    for copy in copies:
        copy.wait()


def cross(first, second, c):
    one = times(first[(c + 1) % 3], second[(c + 2) % 3])
    two = times(first[(c + 2) % 3], second[(c + 1) % 3])
    return (one[0] - two[0], one[1] - two[1])


def add(first, second, third):
    return (first[0] + second[0] + third[0], first[1] + second[1] + third[1])


def whole_spec():
    return pl.BlockSpec(memory_space=pltpu.VMEM)


def scalar_spec():
    return pl.BlockSpec(memory_space=pltpu.SMEM)


def shape_of(*shape):
    return jax.ShapeDtypeStruct(shape, jnp.float32)


def local(gauge_links):
    count_x = lax.axis_size("gx")
    plan = Plan(count_x, SIDE)
    rows, pairs = plan.rows, plan.pairs
    table = tables(plan)
    index = lax.axis_index("gx").astype(jnp.int32).reshape(1)
    links = gauge_links.reshape(54, rows, LANES)
    held = pltpu.with_memory_space_constraint(links, pltpu.HBM)
    quads = 8 * rows
    swap = [(i, i ^ 1) for i in range(count_x)]
    halo = [(2 * p, 2 * p - 1) for p in range(1, pairs)] + [(count_x - 1, 0)]
    same_core, same_core_back = [
        [[c + 2 * p for p in sorted(range(pairs), key=place.__getitem__)] for c in range(2)]
        for place in (plan.place, plan.back_place)
    ]

    keep, send, ahead = pl.pallas_call(
        functools.partial(divergence_kernel, plan),
        out_shape=(shape_of(quads, LANES),) * 3,
        in_specs=[scalar_spec(), pl.BlockSpec(memory_space=pltpu.HBM)],
        out_specs=(whole_spec(),) * 3,
        scratch_shapes=[
            pltpu.VMEM((54, rows, LANES), jnp.float32),
            pltpu.VMEM((8, rows + 16, LANES), jnp.float32),
            pltpu.VMEM((8, rows + 16, LANES), jnp.float32),
            pltpu.SemaphoreType.DMA((3, 3)),
        ],
        compiler_params=params(),
        name="divergence",
    )(index, held)
    got = lax.ppermute(send, "gx", swap)
    beside = lax.ppermute(ahead, "gx", halo)
    sent, odd_part, odd_drift = pl.pallas_call(
        functools.partial(forward_kernel, plan),
        out_shape=(
            shape_of(pairs, plan.sent, LANES),
            shape_of(SIDE, 4 * LANES),
            shape_of(8, LANES),
        ),
        in_specs=[scalar_spec()] + [whole_spec()] * 5,
        out_specs=(pl.BlockSpec(memory_space=pltpu.HBM), whole_spec(), whole_spec()),
        scratch_shapes=[
            pltpu.VMEM((pairs, plan.sent, LANES), jnp.float32),
            pltpu.SemaphoreType.DMA((2,)),
        ],
        compiler_params=params(),
        name="forward",
    )(index, keep, got, table["last"], table["second"], table["modes"])
    arrived = lax.all_to_all(
        sent, "gx", split_axis=0, concat_axis=0, tiled=True, axis_index_groups=same_core
    )
    drift_part, turns, own_modes = pl.pallas_call(
        functools.partial(drift_kernel, plan),
        out_shape=(shape_of(8, LANES), shape_of(6, rows, LANES), shape_of(plan.block, LANES)),
        in_specs=[scalar_spec()] + [whole_spec()] * 4 + [pl.BlockSpec(memory_space=pltpu.HBM)],
        out_specs=(whole_spec(),) * 3,
        scratch_shapes=[pltpu.VMEM((54, rows, LANES), jnp.float32), pltpu.SemaphoreType.DMA((3,))],
        compiler_params=params(),
        cost_estimate=pl.CostEstimate(flops=5 * 10**10, bytes_accessed=5 * 10**7, transcendentals=0),
        name="drift",
    )(index, odd_drift, beside, keep, send, held)
    back = pl.pallas_call(
        functools.partial(filter_kernel, plan),
        out_shape=shape_of(pairs, plan.returned, LANES),
        in_specs=[scalar_spec()] + [whole_spec()] * 3,
        out_specs=whole_spec(),
        compiler_params=params(),
        name="filter",
    )(index, arrived, drift_part, own_modes)
    returned = lax.all_to_all(
        back, "gx", split_axis=0, concat_axis=0, tiled=True, axis_index_groups=same_core_back
    )
    keep, send = pl.pallas_call(
        functools.partial(backward_kernel, plan),
        out_shape=(shape_of(quads + 8, LANES), shape_of(quads + 8, LANES)),
        in_specs=[scalar_spec()] + [whole_spec()] * 5,
        out_specs=(whole_spec(), whole_spec()),
        scratch_shapes=[
            pltpu.VMEM((2 * plan.tiles, SIDE, LANES), jnp.float32),
        ],
        compiler_params=params(),
        name="backward",
    )(index, returned, odd_part, table["last_back"], table["second"], table["modes"])
    got = lax.ppermute(send, "gx", swap)
    fixed, drift = pl.pallas_call(
        functools.partial(update_kernel, plan),
        out_shape=(shape_of(54, rows, LANES), shape_of(1)),
        in_specs=[scalar_spec()] + [whole_spec()] * 4,
        out_specs=(pl.BlockSpec(memory_space=pltpu.HBM), scalar_spec()),
        scratch_shapes=[
            pltpu.VMEM((20, rows + 16, LANES), jnp.float32),
            pltpu.VMEM((20, rows, LANES), jnp.float32),
            pltpu.VMEM((54, rows, LANES), jnp.float32),
            pltpu.SemaphoreType.DMA((7,)),
        ],
        compiler_params=params(),
        name="update",
    )(index, keep, got, links, turns)
    return fixed.reshape(gauge_links.shape), drift


def solution(mesh):
    in_specs = (P(None, None, None, None, ("ta", "gx"), None),)
    out_specs = (P(None, None, None, None, ("ta", "gx"), None), P("ta"))
    return jax.shard_map(local, mesh=mesh, in_specs=in_specs, out_specs=out_specs, check_vma=False)
```
